32 devices in a mesh: dp: 8 (over y, x, core), tensor: 4 (over z).
Axes of the slice: x: 2, y: 2, z: 4, core: 2. Of those that a mesh axis runs over, the one named last changes fastest.
Arguments:
- tokens: bfloat16 [16384, 768], P(('dp', 'tensor')), may hold values from -6 to 6
- w_query: bfloat16 [768, 768], P(('tensor', 'dp')), may hold values from -0.4375 to 0.4375
- w_key: bfloat16 [768, 768], P(('tensor', 'dp')), may hold values from -0.21875 to 0.21875
- w_value: bfloat16 [768, 768], P(('tensor', 'dp')), may hold values from -0.21875 to 0.21875
- w_out: bfloat16 [768, 768], P(('tensor', 'dp')), may hold values from -1.25 to 1.25
- qkv_bias: bfloat16 [3, 768], P(None, ('tensor', 'dp')), may hold values from -3 to 3
- w_ff_in: bfloat16 [3072, 768], P(('tensor', 'dp')), may hold values from -0.21875 to 0.21875
- w_ff_out: bfloat16 [3072, 768], P(('tensor', 'dp')), may hold values from -0.109375 to 0.109375
- ff_bias: bfloat16 [3072], P(('tensor', 'dp')), may hold values from -3 to 3
- rel_table: bfloat16 [256, 768], P('dp'), may hold values from -6 to 6
- gains: bfloat16 [2, 768], P(None, 'dp'), may hold values from 0.099609375 to 1.8984375
- shifts: bfloat16 [4, 768], P(None, 'dp'), may hold values from -3 to 3
- rel_bucket: int32 [4095], replicated, may hold values from 0 to 255
- lengths: int32 [8], P('dp'), may hold values from 1024 to 2048, as said below
- out_grad: bfloat16 [16384, 768], P(('dp', 'tensor')), may hold values from -6 to 6
Outputs:
- layer_result_rows: bfloat16 [16384, 768], P(('dp', 'tensor'))
- tokens_grad: float32 [16384, 768], P(('dp', 'tensor'))
- w_query_grad: float32 [768, 768], P(('tensor', 'dp'))
- w_key_grad: float32 [768, 768], P(('tensor', 'dp'))
- w_value_grad: float32 [768, 768], P(('tensor', 'dp'))
- w_out_grad: float32 [768, 768], P(('tensor', 'dp'))
- qkv_bias_grad: float32 [3, 768], P(None, ('tensor', 'dp'))
- w_ff_in_grad: float32 [3072, 768], P(('tensor', 'dp'))
- w_ff_out_grad: float32 [3072, 768], P(('tensor', 'dp'))
- ff_bias_grad: float32 [3072], P(('tensor', 'dp'))
- rel_table_grad: float32 [256, 768], P('dp')
- gains_grad: float32 [2, 768], P(None, 'dp')
- shifts_grad: float32 [4, 768], P(None, 'dp')
The draws below stay inside these ranges and needn't reach their ends.
Inputs may be any that keep to these rules, and one draw needn't show every extreme that they name: lengths[s] is the number of leading tokens of sequence s whose keys count.
All inputs are finite; a program needn't handle non-finite values.
Results may differ from the reference program's by a relative error of at most 0.02.
Values may be sent and summed in bfloat16 or wider, within the bound.
A program may use at most 320 MiB of HBM per device.

```python
import math
import jax
import jax.numpy as jnp
from jax import lax

D = 768
HEADS = 12
DH = 64
FF = 3072
NB = 256
SEQ = 2048
TOKENS = 16384
NSEQ = 8


def draw_lengths(key, part):
    drawn = jax.random.randint(key, (NSEQ,), SEQ // 2, SEQ + 1, dtype=jnp.int32)
    return drawn.at[0].set(SEQ)


def plant(values, stream_key, low, largest):
    shape = values.shape
    spot = [jax.random.randint(jax.random.fold_in(stream_key, axis), (), 0, shape[axis]) for axis in range(len(shape))]
    values = values.at[tuple(spot)].set(low)
    longest = shape.index(max(shape))
    spot[longest] = (spot[longest] + 1) % shape[longest]
    return values.at[tuple(spot)].set(largest)


def level_of(rng, extent, split, least, top_value):
    factor_of, own = 1.0, jax.random.fold_in(rng, 6)
    for dim, blocks in split:
        heights = jnp.exp(jax.random.uniform(jax.random.fold_in(own, dim), (blocks,), jnp.float32, least / len(split), top_value / len(split)))
        factor_of = factor_of * jnp.repeat(heights, extent[dim] // blocks).reshape([-1 if axis == dim else 1 for axis in range(len(extent))])
    return factor_of


def gaussian(rng, dims, scale, most, pieces=(), kind=jnp.bfloat16):
    values = scale * jax.random.normal(rng, dims, jnp.float32)
    if pieces:
        values = values * level_of(rng, dims, pieces, -0.22, 0.18)
    return jnp.clip(values, -most, most).astype(kind)


def setup_inputs(seed: int = 0) -> dict:
    splits = jax.random.split(jax.random.key(seed), 16)
    return {
        "tokens": gaussian(splits[0], (TOKENS, D), 1.0, 6.0, ((0, 32),)),
        "w_query": gaussian(splits[1], (D, D), (D // 4) ** -0.5, 0.4375, ((0, 32),)),
        "w_key": gaussian(splits[2], (D, D), D ** -0.5, 0.21875, ((0, 32),)),
        "w_value": gaussian(splits[3], (D, D), D ** -0.5, 0.21875, ((0, 32),)),
        "w_out": gaussian(splits[4], (D, D), (D // 32) ** -0.5, 1.25, ((0, 32),)),
        "qkv_bias": gaussian(splits[5], (3, D), 0.5, 3.0, ((1, 32),)),
        "w_ff_in": gaussian(splits[6], (FF, D), D ** -0.5, 0.21875, ((0, 32),)),
        "w_ff_out": gaussian(splits[7], (FF, D), FF ** -0.5, 0.109375, ((0, 32),)),
        "ff_bias": gaussian(splits[8], (FF,), 0.5, 3.0, ((0, 32),)),
        "rel_table": gaussian(splits[9], (NB, D), 1.0, 6.0, ((0, 8),)),
        "gains": jnp.clip(1.0 + 0.18 * jax.random.normal(splits[10], (2, D), jnp.float32), 0.099609375, 1.8984375).astype(jnp.bfloat16),
        "shifts": gaussian(splits[11], (4, D), 0.5, 3.0, ((1, 8),)),
        "rel_bucket": plant(jax.random.randint(splits[12], (2 * SEQ - 1,), 0, NB), jax.random.fold_in(splits[12], 1), 0, NB - 1).astype(jnp.int32),
        "lengths": draw_lengths(jax.random.fold_in(splits[15], 71), 0),
        "out_grad": gaussian(splits[14], (TOKENS, D), 1.0, 6.0, ((0, 32),)),
    }


@jax.custom_vjp
def low(v):
    return lax.optimization_barrier(v.astype(jnp.bfloat16)).astype(jnp.float32)

@jax.custom_vjp
def low_back(v):
    return v

def low_keep(v):
    return (low(v), None)

def low_pass(kept, grad):
    return (grad,)

def back_keep(v):
    return (v, None)

def back_low(kept, grad):
    return (low(grad),)
low.defvjp(low_keep, low_pass)
low_back.defvjp(back_keep, back_low)
norm_eps = 1e-06

def highest(left, right):
    return jnp.dot(left, right, precision=lax.Precision.HIGHEST, preferred_element_type=jnp.float32)

def dense(inputs, weights, bias):
    return jnp.einsum('td,fd->tf', inputs, weights, precision=lax.Precision.HIGHEST) + bias

def layer_norm(values, gain, shift):
    middle = lax.optimization_barrier(jnp.mean(values, axis=-1, keepdims=True))
    centered = values - middle
    spread = lax.optimization_barrier(jnp.mean(centered * centered, axis=-1, keepdims=True))
    return centered * lax.rsqrt(spread + norm_eps) * gain + shift

def attend(query, key, value, key_rel, query_rel, valid, rel_bucket):
    block = min(512, SEQ)
    factor = 1.0 / math.sqrt(3 * DH)
    positions = jnp.arange(SEQ, dtype=jnp.int32)
    query_heads = query.reshape(SEQ, HEADS, DH)
    key_heads = key.reshape(SEQ, HEADS, DH)
    value_heads = value.reshape(SEQ, HEADS, DH)
    key_rel_heads = key_rel.reshape(NB, HEADS, DH)
    query_rel_heads = query_rel.reshape(NB, HEADS, DH)
    key_to_bucket = jnp.einsum('jhd,bhd->hjb', key_heads, query_rel_heads, precision=lax.Precision.HIGHEST)

    def single_block(start):
        rows = start + jnp.arange(block, dtype=jnp.int32)
        query_tile_rows = lax.dynamic_slice_in_dim(query_heads, start, block, 0)
        content = jnp.einsum('rhd,jhd->hrj', query_tile_rows, key_heads, precision=lax.Precision.HIGHEST)
        to_buckets = jnp.einsum('rhd,bhd->hrb', query_tile_rows, key_rel_heads, precision=lax.Precision.HIGHEST)
        near = rel_bucket[rows[:, None] - positions[None, :] + SEQ - 1]
        far = rel_bucket[positions[None, :] - rows[:, None] + SEQ - 1]
        from_query = jnp.take_along_axis(to_buckets, jnp.broadcast_to(near[None], (HEADS, block, SEQ)), axis=2)
        from_key = key_to_bucket[:, positions[None, :], far]
        raw = low_back(content + from_query + from_key)
        scores = jnp.where(valid[None, None, :], raw * factor, -1000000000.0)
        peak = lax.optimization_barrier(jnp.max(scores, axis=-1, keepdims=True))
        powers = jnp.exp(scores - peak)
        weights = low(powers / lax.optimization_barrier(jnp.sum(powers, axis=-1, keepdims=True)))
        context = jnp.einsum('hrj,jhd->rhd', weights, value_heads, precision=lax.Precision.HIGHEST)
        return context.reshape(block, HEADS * DH)
    starts = jnp.arange(SEQ // block, dtype=jnp.int32) * block
    return lax.map(jax.checkpoint(single_block), starts).reshape(SEQ, HEADS * DH)

def reference(tokens, w_query, w_key, w_value, w_out, qkv_bias, w_ff_in, w_ff_out, ff_bias, rel_table, gains, shifts, rel_bucket, lengths, out_grad):
    floats = [array.astype(jnp.float32) for array in (tokens, w_query, w_key, w_value, w_out, qkv_bias, w_ff_in, w_ff_out, ff_bias, rel_table, gains, shifts)]

    def layer(tokens, w_query, w_key, w_value, w_out, qkv_bias, w_ff_in, w_ff_out, ff_bias, rel_table, gains, shifts):
        query = low(low_back(dense(tokens, w_query, qkv_bias[0])))
        key = low(low_back(dense(tokens, w_key, qkv_bias[1])))
        value = low(low_back(dense(tokens, w_value, qkv_bias[2])))
        key_rel = low(dense(rel_table, w_key, qkv_bias[1]))
        query_rel = low(dense(rel_table, w_query, qkv_bias[0]))
        count = tokens.shape[0] // SEQ
        positions = jnp.arange(SEQ, dtype=jnp.int32)

        def per_sequence(carry, items):
            valid = positions < items[3]
            return (carry, attend(items[0], items[1], items[2], key_rel, query_rel, valid, rel_bucket))
        carry, context = lax.scan(per_sequence, jnp.zeros((), jnp.float32), (query.reshape(count, SEQ, D), key.reshape(count, SEQ, D), value.reshape(count, SEQ, D), lengths))
        context = low(low_back(context.reshape(count * SEQ, D)))
        attended = low_back(highest(context, w_out))
        resid_one = tokens + attended + shifts[0]
        hidden_one = layer_norm(resid_one, gains[0], shifts[1])
        pre = low_back(dense(low(hidden_one), w_ff_in, ff_bias))
        gated = low(jax.nn.gelu(pre, approximate=False))
        feed_out = low_back(highest(gated, w_ff_out))
        resid_two = hidden_one + feed_out + shifts[2]
        return layer_norm(resid_two, gains[1], shifts[3])
    final_value, reverse_mapping = jax.vjp(layer, *floats)
    grads = reverse_mapping(out_grad.astype(jnp.float32))
    return (final_value.astype(jnp.bfloat16), grads[0], grads[1], grads[2], grads[3], grads[4], grads[5], grads[6], grads[7], grads[8], grads[9], grads[10], grads[11])
```

```python
import functools
import math

import jax
import jax.numpy as jnp
from jax import lax
from jax.experimental import pallas as pl
from jax.experimental.pallas import tpu as pltpu
from jax.sharding import PartitionSpec as P

bf=jnp.bfloat16; f32=jnp.float32
DH=64; NB=256
SCALE=1.0/math.sqrt(3*DH)
LOG2E=math.log2(math.e)

def dot_nt(a,b):
    return lax.dot_general(a,b,(((1,),(1,)),((),())),preferred_element_type=f32)
def dot_nn(a,b):
    return lax.dot_general(a,b,(((1,),(0,)),((),())),preferred_element_type=f32)
def dot_tn(a,b):
    return lax.dot_general(a,b,(((0,),(0,)),((),())),preferred_element_type=f32)

def flip_matrix(n):
    a=lax.broadcasted_iota(jnp.int32,(n,n),0); b=lax.broadcasted_iota(jnp.int32,(n,n),1)
    return jnp.where(a+b==n-1,1.0,0.0).astype(bf)

def flip_rows(x):
    n,w=x.shape
    idx=7-lax.broadcasted_iota(jnp.int32,(8,w),0)
    return jnp.concatenate([jnp.take_along_axis(x[n-8-8*g:n-8*g],idx,axis=0) for g in range(n//8)],axis=0)

def fwd_kernel(R,L,B,C,mask_ref,q_ref,k_ref,v_ref,kt_ref,qr_ref,ctx_ref,scale_ref,e_ref,yt_ref,acc_ref):
    hh=pl.program_id(1)
    W=L+R
    def lanes(n): return (lax.broadcasted_iota(jnp.int32,(n,128),1)//DH)==hh
    zero=jnp.zeros((),bf)
    def yblock(i,_):
        j0=pl.multiple_of(i*C,C)
        kb=jnp.where(lanes(C),k_ref[pl.ds(j0,C),:],zero)
        us=pl.multiple_of(L-C-j0,C)
        y=dot_nt(kb,qr_ref[pl.ds(us,R+C),:])
        y=pltpu.roll(y,R+1,1,stride=1,stride_axis=0)[:,:R]
        yt_ref[:,pl.ds(j0,C)]=y.T+mask_ref[:,pl.ds(j0,C)]
        return 0
    lax.fori_loop(0,L//C,yblock,0,unroll=2)
    v_one=jnp.where(lanes(L),v_ref[...],jnp.ones((),bf))
    def strip(i,_):
        r0=pl.multiple_of(i*B,B)
        q=jnp.where(lanes(B),q_ref[pl.ds(r0,B),:],zero)
        ws=pl.multiple_of(R-B-r0,B)
        x=dot_nt(q,kt_ref[pl.ds(ws,L+B),:])
        x=pltpu.roll(x,L+1,1,stride=1,stride_axis=0)[:,:L]
        raw=dot_nt(q,k_ref[...])+x+yt_ref[pl.ds(r0,B),:]
        peak=jnp.max(raw,axis=1,keepdims=True)
        e=jnp.exp2((raw-peak)*(SCALE*LOG2E))
        e=flip_rows(e).astype(bf)
        rr=pl.multiple_of(R-B-r0,B)
        e_ref[0,pl.ds(rr,B),:]=e
        acc_ref[pl.ds(rr,B),:]=dot_nn(e,v_one)
        return 0
    lax.fori_loop(0,R//B,strip,0,unroll=2)
    acc=acc_ref[...]
    inv=1.0/pltpu.roll(acc,DH,1)
    ctx=dot_nn(flip_matrix(R),(acc*inv).astype(bf)).astype(bf)
    mine=lanes(R)
    inv_hi=inv.astype(bf)
    J=flip_matrix(R)
    sc=dot_nn(J,inv_hi)+dot_nn(J,(inv-inv_hi.astype(f32)).astype(bf))
    sc=sc*SCALE
    @pl.when(hh==0)
    def _():
        ctx_ref[...]=ctx
        scale_ref[...]=sc
    @pl.when(hh==1)
    def _():
        ctx_ref[...]=jnp.where(mine,ctx,ctx_ref[...])
        scale_ref[...]=jnp.where(mine,sc,scale_ref[...])

def attention_forward(q,k,v,kt,qr,mask,B=128,C=256):
    R,F=q.shape; L=k.shape[0]; W=L+R; pairs=F//128
    col=lambda n: pl.BlockSpec((n,128),lambda p,h:(0,p))
    flops=2*pairs*2*R*L*128*4
    return pl.pallas_call(functools.partial(fwd_kernel,R,L,B,C),
        grid=(pairs,2),
        in_specs=[pl.BlockSpec((1,L),lambda p,h:(0,0)),col(R),col(L),col(L),col(W),col(W)],
        out_specs=[col(R),col(R),pl.BlockSpec((1,R,L),lambda p,h:(2*p+h,0,0))],
        out_shape=[jax.ShapeDtypeStruct((R,F),bf),jax.ShapeDtypeStruct((R,F),f32),jax.ShapeDtypeStruct((2*pairs,R,L),bf)],
        scratch_shapes=[pltpu.VMEM((R,L),f32),pltpu.VMEM((R,128),f32)],
        compiler_params=pltpu.CompilerParams(vmem_limit_bytes=48*1024*1024,dimension_semantics=("arbitrary","arbitrary")),
        cost_estimate=pl.CostEstimate(flops=flops,bytes_accessed=2*pairs*R*L*2+10*L*F,transcendentals=2*pairs*R*L),
        name="attend",
    )(mask,q,k,v,kt,qr)

def bwd_kernel(R,L,B,C,q_ref,k_ref,v_ref,do_ref,ctx_ref,e_ref,kr_ref,qrel_ref,ox_ref,oy_ref,
               dq_ref,dk_ref,dv_ref,dkr_ref,dqr_ref,ds_ref,dor_ref,qrev_ref,dqa_ref,dka_ref,dva_ref):
    hh=pl.program_id(1)
    def lanes(n): return (lax.broadcasted_iota(jnp.int32,(n,128),1)//DH)==hh
    zero=jnp.zeros((),bf)
    @pl.when(hh==0)
    def _():
        dqa_ref[...]=jnp.zeros_like(dqa_ref)
        dka_ref[...]=jnp.zeros_like(dka_ref)
        dva_ref[...]=jnp.zeros_like(dva_ref)
        dkr_ref[...]=jnp.zeros_like(dkr_ref)
        dqr_ref[...]=jnp.zeros_like(dqr_ref)
    J=flip_matrix(R)
    do=jnp.where(lanes(R),dot_nn(J,do_ref[...]).astype(bf),zero)
    ctx=dot_nn(J,ctx_ref[...])
    dor_ref[...]=do
    qrev_ref[...]=jnp.where(lanes(R),dot_nn(J,q_ref[...]).astype(bf),zero)
    delta_all=jnp.sum(do.astype(f32)*ctx,axis=1,keepdims=True)
    own=lanes(B)
    for i in range(R//B):
        r0=i*B
        do_s=dor_ref[r0:r0+B,:]
        dp=dot_nt(do_s,v_ref[...])
        ds=(e_ref[0,r0:r0+B,:].astype(f32)*(dp-delta_all[r0:r0+B])).astype(bf)
        ds_ref[r0:r0+B,:]=ds
        wide=jnp.concatenate([ds,jnp.zeros((B,B),bf)],axis=1)
        wide=pltpu.roll(wide,0,1,stride=1,stride_axis=0)
        db=dot_nn(wide,ox_ref[r0:r0+L+B,:]).astype(bf)
        dq=dot_nn(ds,k_ref[...])+dot_nn(db,kr_ref[...])
        dqa_ref[r0:r0+B,:]=jnp.where(own,dq,dqa_ref[r0:r0+B,:])
        dkr_ref[...]+=dot_tn(db,qrev_ref[r0:r0+B,:])
    ownk=lanes(C)
    qrel=jnp.where(lanes(NB),qrel_ref[...],zero)
    def jblock(i,_):
        j0=pl.multiple_of(i*C,C)
        dst=ds_ref[:,pl.ds(j0,C)].T
        et=e_ref[0,:,pl.ds(j0,C)].T
        wide=jnp.concatenate([dst,jnp.zeros((C,C),bf)],axis=1)
        wide=pltpu.roll(wide,0,1,stride=1,stride_axis=0)
        db=dot_nn(wide,oy_ref[pl.ds(j0,R+C),:]).astype(bf)
        dka_ref[pl.ds(j0,C),:]+=dot_nn(dst,qrev_ref[...])+dot_nn(db,qrel)
        dva_ref[pl.ds(j0,C),:]+=dot_nn(et,dor_ref[...])
        kb=jnp.where(ownk,k_ref[pl.ds(j0,C),:],zero)
        dqr_ref[...]+=dot_tn(db,kb)
        return 0
    lax.fori_loop(0,L//C,jblock,0,unroll=2)
    @pl.when(hh==1)
    def _():
        dq_ref[...]=dot_nn(J,dqa_ref[...].astype(bf)).astype(bf)
        dk_ref[...]=dka_ref[...].astype(bf)
        dv_ref[...]=(dva_ref[...]*(1.0/SCALE)).astype(bf)

def attention_backward(q,k,v,do,ctx,e,key_rel,query_rel,onehot_x,onehot_y,B=128,C=256):
    R,F=q.shape; L=k.shape[0]; W=L+R; pairs=F//128
    col=lambda n: pl.BlockSpec((n,128),lambda p,h:(0,p))
    full=pl.BlockSpec((W,NB),lambda p,h:(0,0))
    flops=2*pairs*2*R*L*128*8
    return pl.pallas_call(functools.partial(bwd_kernel,R,L,B,C),
        grid=(pairs,2),
        in_specs=[col(R),col(L),col(L),col(R),col(R),pl.BlockSpec((1,R,L),lambda p,h:(2*p+h,0,0)),col(NB),col(NB),full,full],
        out_specs=[col(R),col(L),col(L),col(NB),col(NB)],
        out_shape=[jax.ShapeDtypeStruct((R,F),bf),jax.ShapeDtypeStruct((L,F),bf),jax.ShapeDtypeStruct((L,F),bf),
                   jax.ShapeDtypeStruct((NB,F),f32),jax.ShapeDtypeStruct((NB,F),f32)],
        scratch_shapes=[pltpu.VMEM((R,L),bf),pltpu.VMEM((R,128),bf),pltpu.VMEM((R,128),bf),
                        pltpu.VMEM((R,128),f32),pltpu.VMEM((L,128),f32),pltpu.VMEM((L,128),f32)],
        compiler_params=pltpu.CompilerParams(vmem_limit_bytes=48*1024*1024,dimension_semantics=("arbitrary","arbitrary")),
        cost_estimate=pl.CostEstimate(flops=flops,bytes_accessed=2*pairs*R*L*2+20*L*F,transcendentals=0),
        name="attend_back",
    )(q,k,v,do,ctx,e,key_rel,query_rel,onehot_x,onehot_y)

EPS=1e-06
ALL=("tensor","dp")

def layer_norm(values, gain, shift):
    middle = jnp.mean(values, axis=-1, keepdims=True)
    centered = values - middle
    spread = jnp.mean(centered * centered, axis=-1, keepdims=True)
    return centered * lax.rsqrt(spread + EPS) * gain + shift

def exact_gelu(values):
    return jax.nn.gelu(values, approximate=False)

def project(inputs, weights, bias):
    return (jnp.einsum("td,fd->tf", inputs, weights, preferred_element_type=f32) + bias).astype(bf)

def local(tokens, w_query, w_key, w_value, w_out, qkv_bias, w_ff_in, w_ff_out, ff_bias, rel_table,
          gains, shifts, rel_bucket, lengths, out_grad):
    D = tokens.shape[1]
    n_t, n_dp = lax.axis_size("tensor"), lax.axis_size("dp")
    n_all = n_t * n_dp
    t = lax.axis_index("tensor")
    R = tokens.shape[0]
    L = (rel_bucket.shape[0] + 1) // 2
    W = L + R
    part = rel_table.shape[0] // n_t
    wide, inner, cols = qkv_bias.shape[1], ff_bias.shape[0], gains.shape[1]
    misc = jnp.concatenate([qkv_bias.reshape(-1), ff_bias, gains.reshape(-1), shifts.reshape(-1)])
    used = misc.shape[0]
    misc = jnp.pad(misc, (0, D - used))[None]
    rel_part = lax.dynamic_slice_in_dim(rel_table, t * part, part, 0)
    small = jnp.concatenate([misc, rel_part], axis=0)
    gather = lambda x: lax.all_gather(x, ALL, axis=0, tiled=True)
    small_all = lax.all_gather(small, ALL, axis=0, tiled=False)
    query_rows, key_rows, value_rows, out_rows = gather(w_query), gather(w_key), gather(w_value), gather(w_out)
    inner_rows, outer_rows = gather(w_ff_in), gather(w_ff_out)
    misc_all = small_all[:, 0]
    o1 = 3 * wide
    o2 = o1 + inner
    o3 = o2 + 2 * cols
    bias = misc_all[:, :o1].reshape(n_all, 3, wide).transpose(1, 0, 2).reshape(3, D).astype(f32)
    inner_bias = misc_all[:, o1:o2].reshape(-1).astype(f32)
    first = misc_all[:n_dp]
    gain = first[:, o2:o3].reshape(n_dp, 2, cols).transpose(1, 0, 2).reshape(2, D).astype(f32)
    shift = first[:, o3:used].reshape(n_dp, 4, cols).transpose(1, 0, 2).reshape(4, D).astype(f32)
    table = small_all[:, 1:].reshape(n_t, n_dp, part, D).transpose(1, 0, 2, 3).reshape(NB, D)

    gathered = lax.all_gather(tokens, "tensor", axis=0, tiled=True)
    query = project(tokens, query_rows, bias[0])
    key = project(gathered, key_rows, bias[1])
    value = project(gathered, value_rows, bias[2])
    key_rel = project(table, key_rows, bias[1])
    query_rel = project(table, query_rows, bias[0])

    none = jnp.full((1,), -1, jnp.int32)
    ahead = jnp.concatenate([rel_bucket, none])
    back = jnp.concatenate([rel_bucket[::-1], none])
    buckets = jnp.arange(NB, dtype=jnp.int32)[None, :]
    pick = lambda line, start: (lax.dynamic_slice_in_dim(line, start, W, 0)[:, None] == buckets).astype(bf)
    pick_x = pick(back, L - R - R * t)
    pick_y = pick(ahead, L - R - R * t)
    pick_u = pick(back, R * t)
    key_table = jnp.dot(pick_x, key_rel, preferred_element_type=f32).astype(bf)
    query_table = jnp.dot(pick_u, query_rel, preferred_element_type=f32).astype(bf)
    mask = jnp.where(jnp.arange(L, dtype=jnp.int32)[None, :] < lengths[0], 0.0, -1e9).astype(f32)

    context, scale, shares = attention_forward(query, key, value, key_table, query_table, mask)
    attended = jnp.dot(context, out_rows, preferred_element_type=f32)
    resid_one = tokens.astype(f32) + attended + shift[0]
    hidden_one, norm_one_back = jax.vjp(layer_norm, resid_one, gain[0], shift[1])
    hidden_low = hidden_one.astype(bf)
    pre = jnp.einsum("td,fd->tf", hidden_low, inner_rows, preferred_element_type=f32) + inner_bias
    activated, gelu_back = jax.vjp(exact_gelu, pre)
    gated = activated.astype(bf)
    feed_out = jnp.dot(gated, outer_rows, preferred_element_type=f32)
    resid_two = hidden_one + feed_out + shift[2]
    final_value, norm_two_back = jax.vjp(layer_norm, resid_two, gain[1], shift[3])
    layer_result_rows = final_value.astype(bf)
    d_resid_two, d_gain_two, d_shift_three = norm_two_back(out_grad.astype(f32))
    d_shift_two = jnp.sum(d_resid_two, axis=0)
    d_feed = d_resid_two.astype(bf)
    d_gated = jnp.einsum("td,fd->tf", d_feed, outer_rows, preferred_element_type=f32)
    grad_outer = jnp.einsum("tf,td->fd", gated, d_feed, preferred_element_type=f32)
    d_pre = gelu_back(d_gated)[0].astype(bf)
    grad_inner = jnp.einsum("tf,td->fd", d_pre, hidden_low, preferred_element_type=f32)
    grad_bias_inner = jnp.sum(d_pre.astype(f32), axis=0)
    d_hidden_one = d_resid_two + jnp.dot(d_pre, inner_rows, preferred_element_type=f32)
    d_resid_one, d_gain_one, d_shift_one = norm_one_back(d_hidden_one)
    d_shift_zero = jnp.sum(d_resid_one, axis=0)
    d_attended = d_resid_one.astype(bf)
    grad_out = jnp.einsum("tf,td->fd", context, d_attended, preferred_element_type=f32)
    d_context = jnp.einsum("td,fd->tf", d_attended, out_rows, preferred_element_type=f32)
    d_scaled = (d_context * scale).astype(bf)
    d_query, d_key, d_value, d_key_rel, d_query_rel = attention_backward(
        query, key, value, d_scaled, context, shares, key_rel, query_rel, pick_x, pick_y)

    scatter = lambda x: lax.psum_scatter(x, ALL, scatter_dimension=0, tiled=True)
    lowered = lambda x: scatter(x.astype(bf)).astype(f32)
    g_inner, g_outer, g_out = lowered(grad_inner), lowered(grad_outer), lowered(grad_out)
    dqr, dkr = d_query_rel.astype(bf), d_key_rel.astype(bf)
    grad_query = jnp.einsum("tf,td->fd", d_query, tokens, preferred_element_type=f32) + jnp.einsum(
        "tf,td->fd", dqr, table, preferred_element_type=f32)
    grad_key = jnp.einsum("tf,td->fd", d_key, gathered, preferred_element_type=f32) + jnp.einsum(
        "tf,td->fd", dkr, table, preferred_element_type=f32)
    grad_value = jnp.einsum("tf,td->fd", d_value, gathered, preferred_element_type=f32)
    bias_gradient = jnp.stack([
        jnp.sum(d_query.astype(f32), axis=0) + jnp.sum(d_query_rel, axis=0),
        jnp.sum(d_key.astype(f32), axis=0) + jnp.sum(d_key_rel, axis=0),
        jnp.sum(d_value.astype(f32), axis=0)])
    d_rel = jnp.dot(dqr, query_rows, preferred_element_type=f32) + jnp.dot(dkr, key_rows, preferred_element_type=f32)
    own = jnp.dot(d_query, query_rows, preferred_element_type=f32)
    spread = (jnp.dot(d_key, key_rows, preferred_element_type=f32)
              + jnp.dot(d_value, value_rows, preferred_element_type=f32)).astype(bf)
    back_sum = lax.psum_scatter(spread, "tensor", scatter_dimension=0, tiled=True)
    tokens_grad = d_resid_one + own + back_sum.astype(f32)
    g_query, g_key, g_value = lowered(grad_query), lowered(grad_key), lowered(grad_value)

    gain_grads = jnp.stack([d_gain_one, d_gain_two])
    shift_grads = jnp.stack([d_shift_zero, d_shift_one, d_shift_two, d_shift_three])
    shape_dp = lambda x, k: jnp.broadcast_to(
        x.reshape(k, n_dp, cols).transpose(1, 0, 2).reshape(1, n_dp, k * cols), (n_t, n_dp, k * cols)).reshape(n_all, k * cols)
    line = jnp.concatenate([
        bias_gradient.reshape(3, n_all, wide).transpose(1, 0, 2).reshape(n_all, o1),
        grad_bias_inner.reshape(n_all, inner),
        shape_dp(gain_grads, 2), shape_dp(shift_grads, 4)], axis=1)
    line = jnp.pad(line, ((0, 0), (0, D - used)))[:, None]
    rel_rows = rel_table.shape[0]
    d_rel_all = jnp.broadcast_to(d_rel.reshape(1, n_dp, rel_rows, D), (n_t, n_dp, rel_rows, D)).reshape(n_all, rel_rows, D)
    packed = jnp.concatenate([line, d_rel_all], axis=1)
    small_grad = lax.psum_scatter(packed, ALL, scatter_dimension=0, tiled=True)[0]
    row = small_grad[0]
    return (layer_result_rows, tokens_grad, g_query, g_key, g_value, g_out,
            row[:o1].reshape(3, wide), g_inner, g_outer, row[o1:o2], small_grad[1:],
            row[o2:o3].reshape(2, cols), row[o3:used].reshape(4, cols))

def solution(mesh):
    rows, params = P(("dp", "tensor"), None), P(ALL, None)
    return jax.shard_map(
        local, mesh=mesh,
        in_specs=(rows, params, params, params, params, P(None, ALL), params, params, P(ALL), P("dp", None),
                  P(None, "dp"), P(None, "dp"), P(), P("dp"), rows),
        out_specs=(rows, rows, params, params, params, params, P(None, ALL), params, params, P(ALL), P("dp", None),
                   P(None, "dp"), P(None, "dp")),
        check_vma=False)
```

```python
import functools
import math

import jax
import jax.numpy as jnp
from jax import lax
from jax.experimental import pallas as pl
from jax.experimental.pallas import tpu as pltpu
from jax.sharding import PartitionSpec as P

bf = jnp.bfloat16
f32 = jnp.float32
DH=64; NB=256
SCALE=1.0/math.sqrt(3*DH)
LOG2E=math.log2(math.e)

def dot_nt(a,b):
    return lax.dot_general(a,b,(((1,),(1,)),((),())),preferred_element_type=f32)
def dot_nn(a,b):
    return lax.dot_general(a,b,(((1,),(0,)),((),())),preferred_element_type=f32)
def dot_tn(a,b):
    return lax.dot_general(a,b,(((0,),(0,)),((),())),preferred_element_type=f32)

def flip_matrix(n):
    a=lax.broadcasted_iota(jnp.int32,(n,n),0); b=lax.broadcasted_iota(jnp.int32,(n,n),1)
    return jnp.where(a+b==n-1,1.0,0.0).astype(bf)

def flip_rows(x):
    n,w=x.shape
    idx=7-lax.broadcasted_iota(jnp.int32,(8,w),0)
    return jnp.concatenate([jnp.take_along_axis(x[n-8-8*g:n-8*g],idx,axis=0) for g in range(n//8)],axis=0)

def fwd_kernel(R,L,B,C,mask_ref,q_ref,k_ref,v_ref,kt_ref,qr_ref,ctx_ref,scale_ref,e_ref,yt_ref,acc_ref):
    hh=pl.program_id(1)
    W=L+R
    def lanes(n): return (lax.broadcasted_iota(jnp.int32,(n,128),1)//DH)==hh
    zero=jnp.zeros((),bf)
    def yblock(i,_):
        j0=pl.multiple_of(i*C,C)
        kb=jnp.where(lanes(C),k_ref[pl.ds(j0,C),:],zero)
        us=pl.multiple_of(L-C-j0,C)
        y=dot_nt(kb,qr_ref[pl.ds(us,R+C),:])
        y=pltpu.roll(y,R+1,1,stride=1,stride_axis=0)[:,:R]
        yt_ref[:,pl.ds(j0,C)]=y.T+mask_ref[:,pl.ds(j0,C)]
        return 0
    lax.fori_loop(0,L//C,yblock,0,unroll=2)
    v_one=jnp.where(lanes(L),v_ref[...],jnp.ones((),bf))
    def strip(i,_):
        r0=pl.multiple_of(i*B,B)
        q=jnp.where(lanes(B),q_ref[pl.ds(r0,B),:],zero)
        ws=pl.multiple_of(R-B-r0,B)
        x=dot_nt(q,kt_ref[pl.ds(ws,L+B),:])
        x=pltpu.roll(x,L+1,1,stride=1,stride_axis=0)[:,:L]
        raw=dot_nt(q,k_ref[...])+x+yt_ref[pl.ds(r0,B),:]
        peak=jnp.max(raw,axis=1,keepdims=True)
        e=jnp.exp2((raw-peak)*(SCALE*LOG2E))
        e=flip_rows(e).astype(bf)
        rr=pl.multiple_of(R-B-r0,B)
        e_ref[0,pl.ds(rr,B),:]=e
        acc_ref[pl.ds(rr,B),:]=dot_nn(e,v_one)
        return 0
    lax.fori_loop(0,R//B,strip,0,unroll=2)
    acc=acc_ref[...]
    inv=1.0/pltpu.roll(acc,DH,1)
    ctx=dot_nn(flip_matrix(R),(acc*inv).astype(bf)).astype(bf)
    mine=lanes(R)
    inv_hi=inv.astype(bf)
    J=flip_matrix(R)
    sc=dot_nn(J,inv_hi)+dot_nn(J,(inv-inv_hi.astype(f32)).astype(bf))
    sc=sc*SCALE
    @pl.when(hh==0)
    def _():
        ctx_ref[...]=ctx
        scale_ref[...]=sc
    @pl.when(hh==1)
    def _():
        ctx_ref[...]=jnp.where(mine,ctx,ctx_ref[...])
        scale_ref[...]=jnp.where(mine,sc,scale_ref[...])

def attention_forward(q,k,v,kt,qr,mask,B=128,C=256):
    R,F=q.shape; L=k.shape[0]; W=L+R; pairs=F//128
    col=lambda n: pl.BlockSpec((n,128),lambda p,h:(0,p))
    flops=2*pairs*2*R*L*128*4
    return pl.pallas_call(functools.partial(fwd_kernel,R,L,B,C),
        grid=(pairs,2),
        in_specs=[pl.BlockSpec((1,L),lambda p,h:(0,0)),col(R),col(L),col(L),col(W),col(W)],
        out_specs=[col(R),col(R),pl.BlockSpec((1,R,L),lambda p,h:(2*p+h,0,0))],
        out_shape=[jax.ShapeDtypeStruct((R,F),bf),jax.ShapeDtypeStruct((R,F),f32),jax.ShapeDtypeStruct((2*pairs,R,L),bf)],
        scratch_shapes=[pltpu.VMEM((R,L),f32),pltpu.VMEM((R,128),f32)],
        compiler_params=pltpu.CompilerParams(vmem_limit_bytes=48*1024*1024,dimension_semantics=("arbitrary","arbitrary")),
        cost_estimate=pl.CostEstimate(flops=flops,bytes_accessed=2*pairs*R*L*2+10*L*F,transcendentals=2*pairs*R*L),
        name="attend",
    )(mask,q,k,v,kt,qr)

def bwd_kernel(R,L,B,C,q_ref,k_ref,v_ref,do_ref,ctx_ref,e_ref,kr_ref,qrel_ref,ox_ref,oy_ref,
               dq_ref,dk_ref,dv_ref,dkr_ref,dqr_ref,ds_ref,dor_ref,qrev_ref,dqa_ref,dka_ref,dva_ref):
    hh=pl.program_id(1)
    def lanes(n): return (lax.broadcasted_iota(jnp.int32,(n,128),1)//DH)==hh
    zero=jnp.zeros((),bf)
    @pl.when(hh==0)
    def _():
        dqa_ref[...]=jnp.zeros_like(dqa_ref)
        dka_ref[...]=jnp.zeros_like(dka_ref)
        dva_ref[...]=jnp.zeros_like(dva_ref)
        dkr_ref[...]=jnp.zeros_like(dkr_ref)
        dqr_ref[...]=jnp.zeros_like(dqr_ref)
    J=flip_matrix(R)
    do=jnp.where(lanes(R),dot_nn(J,do_ref[...]).astype(bf),zero)
    ctx=dot_nn(J,ctx_ref[...])
    dor_ref[...]=do
    qrev_ref[...]=jnp.where(lanes(R),dot_nn(J,q_ref[...]).astype(bf),zero)
    delta_all=jnp.sum(do.astype(f32)*ctx,axis=1,keepdims=True)
    own=lanes(B)
    for i in range(R//B):
        r0=i*B
        do_s=dor_ref[r0:r0+B,:]
        dp=dot_nt(do_s,v_ref[...])
        ds=(e_ref[0,r0:r0+B,:].astype(f32)*(dp-delta_all[r0:r0+B])).astype(bf)
        ds_ref[r0:r0+B,:]=ds
        wide=jnp.concatenate([ds,jnp.zeros((B,B),bf)],axis=1)
        wide=pltpu.roll(wide,0,1,stride=1,stride_axis=0)
        db=dot_nn(wide,ox_ref[r0:r0+L+B,:]).astype(bf)
        dq=dot_nn(ds,k_ref[...])+dot_nn(db,kr_ref[...])
        dqa_ref[r0:r0+B,:]=jnp.where(own,dq,dqa_ref[r0:r0+B,:])
        dkr_ref[...]+=dot_tn(db,qrev_ref[r0:r0+B,:])
    ownk=lanes(C)
    qrel=jnp.where(lanes(NB),qrel_ref[...],zero)
    def jblock(i,_):
        j0=pl.multiple_of(i*C,C)
        dst=ds_ref[:,pl.ds(j0,C)].T
        et=e_ref[0,:,pl.ds(j0,C)].T
        wide=jnp.concatenate([dst,jnp.zeros((C,C),bf)],axis=1)
        wide=pltpu.roll(wide,0,1,stride=1,stride_axis=0)
        db=dot_nn(wide,oy_ref[pl.ds(j0,R+C),:]).astype(bf)
        dka_ref[pl.ds(j0,C),:]+=dot_nn(dst,qrev_ref[...])+dot_nn(db,qrel)
        dva_ref[pl.ds(j0,C),:]+=dot_nn(et,dor_ref[...])
        kb=jnp.where(ownk,k_ref[pl.ds(j0,C),:],zero)
        dqr_ref[...]+=dot_tn(db,kb)
        return 0
    lax.fori_loop(0,L//C,jblock,0,unroll=2)
    @pl.when(hh==1)
    def _():
        dq_ref[...]=dot_nn(J,dqa_ref[...].astype(bf)).astype(bf)
        dk_ref[...]=dka_ref[...].astype(bf)
        dv_ref[...]=(dva_ref[...]*(1.0/SCALE)).astype(bf)

def attention_backward(q,k,v,do,ctx,e,key_rel,query_rel,onehot_x,onehot_y,B=128,C=256):
    R,F=q.shape; L=k.shape[0]; W=L+R; pairs=F//128
    col=lambda n: pl.BlockSpec((n,128),lambda p,h:(0,p))
    full=pl.BlockSpec((W,NB),lambda p,h:(0,0))
    flops=2*pairs*2*R*L*128*8
    return pl.pallas_call(functools.partial(bwd_kernel,R,L,B,C),
        grid=(pairs,2),
        in_specs=[col(R),col(L),col(L),col(R),col(R),pl.BlockSpec((1,R,L),lambda p,h:(2*p+h,0,0)),col(NB),col(NB),full,full],
        out_specs=[col(R),col(L),col(L),col(NB),col(NB)],
        out_shape=[jax.ShapeDtypeStruct((R,F),bf),jax.ShapeDtypeStruct((L,F),bf),jax.ShapeDtypeStruct((L,F),bf),
                   jax.ShapeDtypeStruct((NB,F),f32),jax.ShapeDtypeStruct((NB,F),f32)],
        scratch_shapes=[pltpu.VMEM((R,L),bf),pltpu.VMEM((R,128),bf),pltpu.VMEM((R,128),bf),
                        pltpu.VMEM((R,128),f32),pltpu.VMEM((L,128),f32),pltpu.VMEM((L,128),f32)],
        compiler_params=pltpu.CompilerParams(vmem_limit_bytes=48*1024*1024,dimension_semantics=("arbitrary","arbitrary")),
        cost_estimate=pl.CostEstimate(flops=flops,bytes_accessed=2*pairs*R*L*2+20*L*F,transcendentals=0),
        name="attend_back",
    )(q,k,v,do,ctx,e,key_rel,query_rel,onehot_x,onehot_y)

MESH=pl.DeviceIdType.MESH

def places(n_t, n_dp):
    dp, t = lax.axis_index("dp"), lax.axis_index("tensor")
    high, core = dp // 2, dp % 2
    bits = (n_dp // 2).bit_length() - 1
    flips = [high + (1 - 2 * ((high // 2**i) % 2)) * 2**i for i in range(bits)]
    right, left = lax.rem(t + 1, n_t), lax.rem(t + n_t - 1, n_t)
    return dp, t, high, core, bits, flips, right, left

def meet(peers):
    barrier = pltpu.get_barrier_semaphore()
    for peer in peers:
        pl.semaphore_signal(barrier, inc=1, device_id=peer, device_id_type=MESH)
    pl.semaphore_wait(barrier, len(peers))

def remote(src, dst, send, recv, peer):
    return pltpu.make_async_remote_copy(src_ref=src, dst_ref=dst, send_sem=send, recv_sem=recv,
                                        device_id=peer, device_id_type=MESH)

def interleave(*lists):
    out = []
    for i in range(max(len(x) for x in lists)):
        out += [x[i] for x in lists if i < len(x)]
    return out

def gather_kernel(n_t, n_dp, tok_ref, pack_ref, toks_ref, packs_ref, own_sem, tok_send, tok_recv, pack_send, pack_recv):
    dp, t, high, core, bits, flips, right, left = places(n_t, n_dp)
    peers = [{"tensor": right}, {"tensor": left}, {"dp": high * 2 + 1 - core}] + [{"dp": f * 2 + core} for f in flips]
    meet(peers)
    own_tok = pltpu.make_async_copy(tok_ref, toks_ref.at[t], own_sem.at[0])
    own_pack = pltpu.make_async_copy(pack_ref, packs_ref.at[t, high, core], own_sem.at[1])
    own_tok.start()
    own_pack.start()
    rows = tok_ref.shape[0]
    half = rows // 2
    token = {}
    pack = {}

    def send_pack(s):
        b = lax.rem(t - s + n_t, n_t)
        src = pack_ref if s == 0 else packs_ref.at[b, high, core]
        pack[s] = remote(src, packs_ref.at[b, high, core], pack_send.at[s], pack_recv.at[s], {"tensor": right})
        pack[s].start()

    def send_token(s, j):
        b = lax.rem(t - s + n_t, n_t)
        src = (tok_ref if s == 0 else toks_ref.at[b]).at[pl.ds(j * half, half)]
        token[s, j] = remote(src, toks_ref.at[b, pl.ds(j * half, half)], tok_send.at[s, j], tok_recv.at[s, j], {"tensor": right})
        token[s, j].start()

    def swap(i):
        s = n_t - 1 + i
        if i < bits:
            base = (high // 2**i) * 2**i
            part = packs_ref.at[:, pl.ds(base, 2**i), core]
            peer = {"dp": flips[i] * 2 + core}
        else:
            part = packs_ref.at[:, :, core]
            peer = {"dp": high * 2 + 1 - core}
        pack[s] = remote(part, part, pack_send.at[s], pack_recv.at[s], peer)
        pack[s].start()

    send_pack(0)
    send_token(0, 0)
    send_token(0, 1)
    for s in range(1, n_t - 1):
        pack[s - 1].wait_recv()
        send_pack(s)
    pack[n_t - 2].wait_recv()
    own_pack.wait()
    swap(0)

    def token_step(s):
        def run():
            for j in range(2):
                token[s - 1, j].wait_recv()
                if s < n_t - 1:
                    send_token(s, j)
        return run

    def pack_step(i):
        def run():
            pack[n_t - 1 + i - 1].wait_recv()
            if i <= bits:
                swap(i)
        return run

    for step in interleave([token_step(s) for s in range(1, n_t)], [pack_step(i) for i in range(1, bits + 2)]):
        step()
    own_tok.wait()
    for copy in list(pack.values()) + list(token.values()):
        copy.wait_send()

def gather_start(tokens, pack, n_t, n_dp):
    rows, D = tokens.shape
    pr = pack.shape[0]
    bits = (n_dp // 2).bit_length() - 1
    n_pack = n_t + bits
    hbm = pl.BlockSpec(memory_space=pl.ANY)
    return pl.pallas_call(
        functools.partial(gather_kernel, n_t, n_dp),
        out_shape=[jax.ShapeDtypeStruct((n_t, rows, D), bf), jax.ShapeDtypeStruct((n_t, n_dp // 2, 2, pr, D), bf)],
        in_specs=[hbm, hbm], out_specs=[hbm, hbm],
        scratch_shapes=[pltpu.SemaphoreType.DMA((2,)), pltpu.SemaphoreType.DMA((n_t - 1, 2)), pltpu.SemaphoreType.DMA((n_t - 1, 2)),
                        pltpu.SemaphoreType.DMA((n_pack,)), pltpu.SemaphoreType.DMA((n_pack,))],
        compiler_params=pltpu.CompilerParams(collective_id=0, has_side_effects=True),
        name="gather_start",
    )(tokens, pack)

def reduce_kernel(n_t, n_dp, tok_ref, pack_ref, tok_out, pack_out, tok_got, tok_acc, first, acc, ring_got, ring_acc, *rest):
    dp, t, high, core, bits, flips, right, left = places(n_t, n_dp)
    halves, (tok_send, tok_recv, send, recv) = rest[:bits], rest[bits:]
    peers = [{"tensor": right}, {"tensor": left}, {"dp": high * 2 + 1 - core}] + [{"dp": f * 2 + core} for f in flips]
    meet(peers)
    n_hi = n_dp // 2
    pr = pack_ref.shape[3]
    rows = tok_ref.shape[1]
    piece = 64 if rows % 64 == 0 else rows
    copies = {}

    def block(s):
        return lax.rem(t - 1 - s + 2 * n_t, n_t)

    def send_token(s):
        src = tok_ref.at[block(0)] if s == 0 else tok_acc.at[s - 1]
        copies["t", s] = remote(src, tok_got.at[s], tok_send.at[s], tok_recv.at[s], {"tensor": right})
        copies["t", s].start()

    def token_step(s):
        def run():
            copies["t", s - 1].wait_recv()
            last = s == n_t - 1
            b = t if last else block(s)

            @pl.loop(0, rows // piece)
            def _(i):
                at = pl.ds(pl.multiple_of(i * piece, piece), piece)
                total = tok_got[s - 1, at].astype(f32) + tok_ref[b, at].astype(f32)
                if last:
                    tok_out[at] = total
                else:
                    tok_acc[s - 1, at] = total.astype(bf)
            if not last:
                send_token(s)
        return run

    def start(k, src, dst, peer):
        copies["p", k] = remote(src, dst, send.at[k], recv.at[k], peer)
        copies["p", k].start()

    def swap(k):
        if k == 0:
            start(0, pack_ref.at[:, :, 1 - core], first, {"dp": high * 2 + 1 - core})
        else:
            i = bits - k
            base = (high // 2**(i + 1)) * 2**(i + 1)
            other = base + (1 - (high // 2**i) % 2) * 2**i
            start(k, acc.at[:, pl.ds(other, 2**i)], halves[i], {"dp": flips[i] * 2 + core})

    def add_swap(k):
        copies["p", k].wait_recv()
        if k == 0:
            @pl.loop(0, n_t * n_hi)
            def _(m):
                a, b = m // n_hi, m % n_hi
                acc[a, b] = (pack_ref[a, b, core].astype(f32) + first[a, b].astype(f32)).astype(bf)
        else:
            i = bits - k
            keep = (high // 2**i) * 2**i

            @pl.loop(0, n_t * 2**i)
            def _(m):
                a, b = m // 2**i, m % 2**i
                acc[a, keep + b] = (acc[a, keep + b].astype(f32) + halves[i][a, b].astype(f32)).astype(bf)

    def ring(s):
        src = acc.at[block(0), high] if s == 0 else ring_acc.at[s - 1]
        start(bits + 1 + s, src, ring_got.at[s], {"tensor": right})

    def ring_add(s):
        copies["p", bits + s].wait_recv()
        last = s == n_t - 1
        b = t if last else block(s)
        total = ring_got[s - 1].astype(f32) + acc[b, high].astype(f32)
        if last:
            pack_out[...] = total
        else:
            ring_acc[s - 1] = total.astype(bf)

    swap(0)
    send_token(0)

    def pack_step(k):
        def run():
            if k <= bits:
                add_swap(k)
                if k < bits:
                    swap(k + 1)
                else:
                    ring(0)
            else:
                s = k - bits
                ring_add(s)
                if s < n_t - 1:
                    ring(s)
        return run

    for step in interleave([pack_step(k) for k in range(bits + n_t)], [lambda: None] + [token_step(s) for s in range(1, n_t)]):
        step()
    for copy in copies.values():
        copy.wait_send()

def reduce_end(spread, pack, n_t, n_dp):
    _, rows, D = spread.shape
    pr = pack.shape[3]
    n_hi = n_dp // 2
    bits = n_hi.bit_length() - 1
    n_pack = bits + n_t
    vm = pl.BlockSpec(memory_space=pltpu.VMEM)
    return pl.pallas_call(
        functools.partial(reduce_kernel, n_t, n_dp),
        out_shape=[jax.ShapeDtypeStruct((rows, D), f32), jax.ShapeDtypeStruct((pr, D), f32)],
        in_specs=[vm, vm], out_specs=[vm, vm],
        scratch_shapes=[pltpu.VMEM((n_t - 1, rows, D), bf), pltpu.VMEM((max(n_t - 2, 1), rows, D), bf),
                        pltpu.VMEM((n_t, n_hi, pr, D), bf), pltpu.VMEM((n_t, n_hi, pr, D), bf),
                        pltpu.VMEM((n_t - 1, pr, D), bf), pltpu.VMEM((max(n_t - 2, 1), pr, D), bf)]
                       + [pltpu.VMEM((n_t, 2**i, pr, D), bf) for i in range(bits)]
                       + [pltpu.SemaphoreType.DMA((n_t - 1,)), pltpu.SemaphoreType.DMA((n_t - 1,)),
                          pltpu.SemaphoreType.DMA((n_pack,)), pltpu.SemaphoreType.DMA((n_pack,))],
        compiler_params=pltpu.CompilerParams(collective_id=1, has_side_effects=True, vmem_limit_bytes=56 * 1024 * 1024),
        name="reduce_end",
    )(spread, pack)

EPS=1e-06
ALL=("tensor","dp")

def layer_norm(values, gain, shift):
    middle = jnp.mean(values, axis=-1, keepdims=True)
    centered = values - middle
    spread = jnp.mean(centered * centered, axis=-1, keepdims=True)
    return centered * lax.rsqrt(spread + EPS) * gain + shift

def exact_gelu(values):
    return jax.nn.gelu(values, approximate=False)

def project(inputs, weights, bias):
    return (jnp.einsum("td,fd->tf", inputs, weights, preferred_element_type=f32) + bias).astype(bf)

def local(tokens, w_query, w_key, w_value, w_out, qkv_bias, w_ff_in, w_ff_out, ff_bias, rel_table,
          gains, shifts, rel_bucket, lengths, out_grad):
    D = tokens.shape[1]
    n_t, n_dp = lax.axis_size("tensor"), lax.axis_size("dp")
    n_all = n_t * n_dp
    t = lax.axis_index("tensor")
    R = tokens.shape[0]
    L = (rel_bucket.shape[0] + 1) // 2
    W = L + R
    part = rel_table.shape[0] // n_t
    wide, inner, cols = qkv_bias.shape[1], ff_bias.shape[0], gains.shape[1]
    misc = jnp.concatenate([qkv_bias.reshape(-1), ff_bias, gains.reshape(-1), shifts.reshape(-1)])
    used = misc.shape[0]
    misc = jnp.pad(misc, (0, D - used))[None]
    rel_part = lax.dynamic_slice_in_dim(rel_table, t * part, part, 0)
    small = jnp.concatenate([misc, rel_part], axis=0)
    early = jnp.concatenate([w_query, w_key, w_value, small], axis=0)
    own_rows = w_query.shape[0]
    late_rows = w_ff_in.shape[0]
    early_rows = early.shape[0]
    early = jnp.pad(early, ((0, -early_rows % 16), (0, 0)))
    late = jnp.concatenate([w_ff_in, w_ff_out, w_out], axis=0)
    gathered, early_all = gather_start(tokens, early, n_t, n_dp)
    late_all = lax.all_gather(late, ALL, axis=0, tiled=False)
    gathered = gathered.reshape(L, D)
    early_all = early_all.reshape(n_all, early.shape[0], D)
    cut = lambda x, at, n: x[:, at:at + n].reshape(n_all * n, D)
    query_rows, key_rows, value_rows = [cut(early_all, i * own_rows, own_rows) for i in range(3)]
    small_all = early_all[:, 3 * own_rows:early_rows]
    inner_rows, outer_rows = cut(late_all, 0, late_rows), cut(late_all, late_rows, late_rows)
    out_rows = cut(late_all, 2 * late_rows, own_rows)
    misc_all = small_all[:, 0]
    o1 = 3 * wide
    o2 = o1 + inner
    o3 = o2 + 2 * cols
    bias = misc_all[:, :o1].reshape(n_all, 3, wide).transpose(1, 0, 2).reshape(3, D).astype(f32)
    inner_bias = misc_all[:, o1:o2].reshape(-1).astype(f32)
    first = misc_all[:n_dp]
    gain = first[:, o2:o3].reshape(n_dp, 2, cols).transpose(1, 0, 2).reshape(2, D).astype(f32)
    shift = first[:, o3:used].reshape(n_dp, 4, cols).transpose(1, 0, 2).reshape(4, D).astype(f32)
    table = small_all[:, 1:].reshape(n_t, n_dp, part, D).transpose(1, 0, 2, 3).reshape(NB, D)

    query = project(tokens, query_rows, bias[0])
    key = project(gathered, key_rows, bias[1])
    value = project(gathered, value_rows, bias[2])
    key_rel = project(table, key_rows, bias[1])
    query_rel = project(table, query_rows, bias[0])

    none = jnp.full((1,), -1, jnp.int32)
    ahead = jnp.concatenate([rel_bucket, none])
    back = jnp.concatenate([rel_bucket[::-1], none])
    buckets = jnp.arange(NB, dtype=jnp.int32)[None, :]
    pick = lambda line, start: (lax.dynamic_slice_in_dim(line, start, W, 0)[:, None] == buckets).astype(bf)
    pick_x = pick(back, L - R - R * t)
    pick_y = pick(ahead, L - R - R * t)
    pick_u = pick(back, R * t)
    key_table = jnp.dot(pick_x, key_rel, preferred_element_type=f32).astype(bf)
    query_table = jnp.dot(pick_u, query_rel, preferred_element_type=f32).astype(bf)
    mask = jnp.where(jnp.arange(L, dtype=jnp.int32)[None, :] < lengths[0], 0.0, -1e9).astype(f32)

    context, scale, shares = attention_forward(query, key, value, key_table, query_table, mask)
    attended = jnp.dot(context, out_rows, preferred_element_type=f32)
    resid_one = tokens.astype(f32) + attended + shift[0]
    hidden_one, norm_one_back = jax.vjp(layer_norm, resid_one, gain[0], shift[1])
    hidden_low = hidden_one.astype(bf)
    pre = jnp.einsum("td,fd->tf", hidden_low, inner_rows, preferred_element_type=f32) + inner_bias
    activated, gelu_back = jax.vjp(exact_gelu, pre)
    gated = activated.astype(bf)
    feed_out = jnp.dot(gated, outer_rows, preferred_element_type=f32)
    resid_two = hidden_one + feed_out + shift[2]
    final_value, norm_two_back = jax.vjp(layer_norm, resid_two, gain[1], shift[3])
    layer_result_rows = final_value.astype(bf)
    d_resid_two, d_gain_two, d_shift_three = norm_two_back(out_grad.astype(f32))
    d_shift_two = jnp.sum(d_resid_two, axis=0)
    d_feed = d_resid_two.astype(bf)
    d_gated = jnp.einsum("td,fd->tf", d_feed, outer_rows, preferred_element_type=f32)
    grad_outer = jnp.einsum("tf,td->fd", gated, d_feed, preferred_element_type=f32)
    d_pre = gelu_back(d_gated)[0].astype(bf)
    grad_inner = jnp.einsum("tf,td->fd", d_pre, hidden_low, preferred_element_type=f32)
    grad_bias_inner = jnp.sum(d_pre.astype(f32), axis=0)
    d_hidden_one = d_resid_two + jnp.dot(d_pre, inner_rows, preferred_element_type=f32)
    d_resid_one, d_gain_one, d_shift_one = norm_one_back(d_hidden_one)
    d_shift_zero = jnp.sum(d_resid_one, axis=0)
    d_attended = d_resid_one.astype(bf)
    grad_out = jnp.einsum("tf,td->fd", context, d_attended, preferred_element_type=f32)
    d_context = jnp.einsum("td,fd->tf", d_attended, out_rows, preferred_element_type=f32)
    d_scaled = (d_context * scale).astype(bf)
    d_query, d_key, d_value, d_key_rel, d_query_rel = attention_backward(
        query, key, value, d_scaled, context, shares, key_rel, query_rel, pick_x, pick_y)

    parted = lambda x: x.astype(bf).reshape(n_all, -1, D)
    late_grad = jnp.concatenate([parted(grad_inner), parted(grad_outer), parted(grad_out)], axis=1)
    late_sum = lax.psum_scatter(late_grad, ALL, scatter_dimension=0, tiled=True)[0].astype(f32)
    g_inner, g_outer, g_out = late_sum[:late_rows], late_sum[late_rows:2 * late_rows], late_sum[2 * late_rows:]
    dqr, dkr = d_query_rel.astype(bf), d_key_rel.astype(bf)
    grad_query = jnp.einsum("tf,td->fd", d_query, tokens, preferred_element_type=f32) + jnp.einsum(
        "tf,td->fd", dqr, table, preferred_element_type=f32)
    grad_key = jnp.einsum("tf,td->fd", d_key, gathered, preferred_element_type=f32) + jnp.einsum(
        "tf,td->fd", dkr, table, preferred_element_type=f32)
    grad_value = jnp.einsum("tf,td->fd", d_value, gathered, preferred_element_type=f32)
    bias_gradient = jnp.stack([
        jnp.sum(d_query.astype(f32), axis=0) + jnp.sum(d_query_rel, axis=0),
        jnp.sum(d_key.astype(f32), axis=0) + jnp.sum(d_key_rel, axis=0),
        jnp.sum(d_value.astype(f32), axis=0)])
    d_rel = jnp.dot(dqr, query_rows, preferred_element_type=f32) + jnp.dot(dkr, key_rows, preferred_element_type=f32)
    own = jnp.dot(d_query, query_rows, preferred_element_type=f32)
    spread = (jnp.dot(d_key, key_rows, preferred_element_type=f32)
              + jnp.dot(d_value, value_rows, preferred_element_type=f32)).astype(bf)
    gain_grads = jnp.stack([d_gain_one, d_gain_two])
    shift_grads = jnp.stack([d_shift_zero, d_shift_one, d_shift_two, d_shift_three])
    shape_dp = lambda x, k: jnp.broadcast_to(
        x.reshape(k, n_dp, cols).transpose(1, 0, 2).reshape(1, n_dp, k * cols), (n_t, n_dp, k * cols)).reshape(n_all, k * cols)
    line = jnp.concatenate([
        bias_gradient.reshape(3, n_all, wide).transpose(1, 0, 2).reshape(n_all, o1),
        grad_bias_inner.reshape(n_all, inner),
        shape_dp(gain_grads, 2), shape_dp(shift_grads, 4)], axis=1)
    line = jnp.pad(line, ((0, 0), (0, D - used)))[:, None]
    rel_rows = rel_table.shape[0]
    d_rel_all = jnp.broadcast_to(d_rel.reshape(1, n_dp, rel_rows, D), (n_t, n_dp, rel_rows, D)).reshape(n_all, rel_rows, D)
    early_grad = jnp.concatenate([parted(grad_query), parted(grad_key), parted(grad_value), line.astype(bf), d_rel_all.astype(bf)], axis=1)
    end_rows = early_grad.shape[1]
    early_grad = jnp.pad(early_grad, ((0, 0), (0, -end_rows % 16), (0, 0)))
    back_sum, early_sum = reduce_end(spread.reshape(n_t, R, D), early_grad.reshape(n_t, n_dp // 2, 2, -1, D), n_t, n_dp)
    tokens_grad = d_resid_one + own + back_sum
    g_query, g_key, g_value = [early_sum[i * own_rows:(i + 1) * own_rows] for i in range(3)]
    row = early_sum[3 * own_rows]
    g_rel = early_sum[3 * own_rows + 1:end_rows]
    return (layer_result_rows, tokens_grad, g_query, g_key, g_value, g_out,
            row[:o1].reshape(3, wide), g_inner, g_outer, row[o1:o2], g_rel,
            row[o2:o3].reshape(2, cols), row[o3:used].reshape(4, cols))

def solution(mesh):
    rows, params = P(("dp", "tensor"), None), P(ALL, None)
    return jax.shard_map(
        local, mesh=mesh,
        in_specs=(rows, params, params, params, params, P(None, ALL), params, params, P(ALL), P("dp", None),
                  P(None, "dp"), P(None, "dp"), P(), P("dp"), rows),
        out_specs=(rows, rows, params, params, params, params, P(None, ALL), params, params, P(ALL), P("dp", None),
                   P(None, "dp"), P(None, "dp")),
        check_vma=False)
```

```python
import functools
import math

import jax
import jax.numpy as jnp
from jax import lax
from jax.experimental import pallas as pl
from jax.experimental.pallas import tpu as pltpu
from jax.sharding import PartitionSpec as P

bf = jnp.bfloat16
f32 = jnp.float32
DH=64; NB=256
SCALE=1.0/math.sqrt(3*DH)
LOG2E=math.log2(math.e)

def dot_nt(a,b):
    return lax.dot_general(a,b,(((1,),(1,)),((),())),preferred_element_type=f32)
def dot_nn(a,b):
    return lax.dot_general(a,b,(((1,),(0,)),((),())),preferred_element_type=f32)
def dot_tn(a,b):
    return lax.dot_general(a,b,(((0,),(0,)),((),())),preferred_element_type=f32)

def flip_matrix(n):
    a=lax.broadcasted_iota(jnp.int32,(n,n),0); b=lax.broadcasted_iota(jnp.int32,(n,n),1)
    return jnp.where(a+b==n-1,1.0,0.0).astype(bf)

def flip_rows(x):
    n,w=x.shape
    idx=7-lax.broadcasted_iota(jnp.int32,(8,w),0)
    return jnp.concatenate([jnp.take_along_axis(x[n-8-8*g:n-8*g],idx,axis=0) for g in range(n//8)],axis=0)

def fwd_kernel(R,L,B,C,mask_ref,q_ref,k_ref,v_ref,kt_ref,qr_ref,ctx_ref,scale_ref,e_ref,yt_ref,acc_ref,km_ref,y_ref,s_ref,x_ref,p_ref):
    hh=pl.program_id(1)
    lane=lambda n: lax.broadcasted_iota(jnp.int32,(n,128),1)
    def lanes(n): return (lane(n)//DH)==hh
    zero,one=jnp.zeros((),bf),jnp.ones((),bf)
    spare=(1-hh)*DH
    for i in range(L//C):
        at=slice(i*C,i*C+C)
        km_ref[at,:]=jnp.where(lane(C)==spare,mask_ref[at,:],k_ref[at,:])
    def yblock(i):
        at=slice(i*C,i*C+C)
        us=L-C-i*C
        kb=jnp.where(lanes(C),k_ref[at,:],zero)
        y=y_ref.at[i%2]
        y[...]=dot_nt(kb,qr_ref[us:us+R+C,:])
        for g in range(C//16):
            rows=slice(16*g,16*g+16)
            part=y[rows,:].astype(bf)
            s_part=pltpu.roll(part,R+1+16*g,1,stride=1,stride_axis=0)[:,:R]
            yt_ref[i%2,rows,:]=s_part
        return yt_ref[i%2].T
    for i in range(L//C):
        acc_ref[:,i*C:i*C+C]=yblock(i)
    v_one=jnp.where(lanes(L),v_ref[...],one)
    own=lanes(B)
    sp=lane(B)==spare
    accs=[]
    for i in range(R//B):
        r0=i*B
        qm=q_ref[r0:r0+B,:]
        q=jnp.where(own,qm,zero)
        qs=jnp.where(sp,one,q)
        ws=R-B-r0
        x,s=x_ref.at[i%2],s_ref.at[i%2]
        x[...]=dot_nt(q,kt_ref[ws:ws+L+B,:])
        s[...]=dot_nt(qs,km_ref[...])
        rr=R-B-r0
        p=p_ref.at[i%2]
        for g in range(B//16):
            rows=slice(16*g,16*g+16)
            xr=pltpu.roll(x[rows,:],(L+1+16*g)%(L+B),1,stride=1,stride_axis=0)[:,:L]
            raw=s[rows,:]+xr+acc_ref[r0+16*g:r0+16*g+16,:].astype(f32)
            s[rows,:]=raw
            top=raw[:,:128]
            for j in range(1,L//128):
                top=jnp.maximum(top,raw[:,128*j:128*j+128])
            p[rows,:]=top
        p[...]=jnp.broadcast_to(jnp.max(p[...],axis=1,keepdims=True)*(SCALE*LOG2E),(B,128))
        for g in range(B//16):
            rows=slice(16*g,16*g+16)
            peak=jnp.concatenate([p[rows,:]]*(L//128),axis=1)
            e=jnp.exp2(s[rows,:]*(SCALE*LOG2E)-peak)
            e=flip_rows(e).astype(bf)
            to=rr+B-16-16*g
            e_ref[0,to:to+16,:]=e
        accs.append(dot_nn(e_ref[0,rr:rr+B,:],v_one))
    acc=jnp.concatenate(accs[::-1],axis=0)
    inv=1.0/pltpu.roll(acc,DH,1)
    J=flip_matrix(R)
    ctx=dot_nn(J,(acc*inv).astype(bf)).astype(bf)
    mine=lanes(R)
    inv_hi=inv.astype(bf)
    sc=dot_nn(J,inv_hi)+dot_nn(J,(inv-inv_hi.astype(f32)).astype(bf))
    sc=sc*SCALE
    @pl.when(hh==0)
    def _():
        ctx_ref[...]=ctx
        scale_ref[...]=sc
    @pl.when(hh==1)
    def _():
        ctx_ref[...]=jnp.where(mine,ctx,ctx_ref[...])
        scale_ref[...]=jnp.where(mine,sc,scale_ref[...])

def attention_forward(q,k,v,kt,qr,mask,B=128,C=256):
    R,F=q.shape; L=k.shape[0]; W=L+R; pairs=F//128
    B=min(B,R)
    col=lambda n: pl.BlockSpec((n,128),lambda p,h:(0,p))
    flops=2*pairs*2*R*L*128*4
    return pl.pallas_call(functools.partial(fwd_kernel,R,L,B,C),
        grid=(pairs,2),
        in_specs=[pl.BlockSpec((L,128),lambda p,h:(0,0)),col(R),col(L),col(L),col(W),col(W)],
        out_specs=[col(R),col(R),pl.BlockSpec((1,R,L),lambda p,h:(2*p+h,0,0))],
        out_shape=[jax.ShapeDtypeStruct((R,F),bf),jax.ShapeDtypeStruct((R,F),f32),jax.ShapeDtypeStruct((2*pairs,R,L),bf)],
        scratch_shapes=[pltpu.VMEM((2,C,R),bf),pltpu.VMEM((R,L),bf),pltpu.VMEM((L,128),bf),pltpu.VMEM((2,C,R+C),f32),
                        pltpu.VMEM((2,B,L),f32),pltpu.VMEM((2,B,L+B),f32),pltpu.VMEM((2,B,128),f32)],
        compiler_params=pltpu.CompilerParams(vmem_limit_bytes=48*1024*1024,dimension_semantics=("arbitrary","arbitrary")),
        cost_estimate=pl.CostEstimate(flops=flops,bytes_accessed=2*pairs*R*L*2+10*L*F,transcendentals=2*pairs*R*L),
        name="attend",
    )(mask,q,k,v,kt,qr)

def bwd_kernel(R,L,B,C,q_ref,k_ref,v_ref,do_ref,ctx_ref,e_ref,kr_ref,qrel_ref,ox_ref,oy_ref,
               dq_ref,dk_ref,dv_ref,dkr_ref,dqr_ref,ds_ref,dor_ref,qrev_ref,dqa_ref,dka_ref,dva_ref,
               delta_ref,dp_ref,wide_ref,dst_ref,wide2_ref):
    hh=pl.program_id(1)
    def lanes(n): return (lax.broadcasted_iota(jnp.int32,(n,128),1)//DH)==hh
    zero=jnp.zeros((),bf)
    @pl.when(hh==0)
    def _():
        dqa_ref[...]=jnp.zeros_like(dqa_ref)
        dka_ref[...]=jnp.zeros_like(dka_ref)
        dva_ref[...]=jnp.zeros_like(dva_ref)
        dkr_ref[...]=jnp.zeros_like(dkr_ref)
        dqr_ref[...]=jnp.zeros_like(dqr_ref)
    J=flip_matrix(R)
    do=jnp.where(lanes(R),dot_nn(J,do_ref[...]).astype(bf),zero)
    ctx=dot_nn(J,ctx_ref[...])
    dor_ref[...]=do
    qrev_ref[...]=jnp.where(lanes(R),dot_nn(J,q_ref[...]).astype(bf),zero)
    delta_ref[...]=jnp.broadcast_to(jnp.sum(do.astype(f32)*ctx,axis=1,keepdims=True),(R,128))
    own=lanes(B)
    for i in range(R//B):
        r0=i*B
        dp,wide=dp_ref.at[i%2],wide_ref.at[i%2]
        dp[...]=dot_nt(dor_ref[r0:r0+B,:],v_ref[...])
        for g in range(B//16):
            rows=slice(16*g,16*g+16)
            at=slice(r0+16*g,r0+16*g+16)
            delta=jnp.concatenate([delta_ref[at,:]]*(L//128),axis=1)
            ds=(e_ref[0,at,:].astype(f32)*(dp[rows,:]-delta)).astype(bf)
            ds_ref[at,:]=ds
            part=jnp.concatenate([ds,jnp.zeros((16,B),bf)],axis=1)
            wide[rows,:]=pltpu.roll(part,16*g,1,stride=1,stride_axis=0)
        db=dot_nn(wide[...],ox_ref[r0:r0+L+B,:]).astype(bf)
        dq=dot_nn(ds_ref[r0:r0+B,:],k_ref[...])+dot_nn(db,kr_ref[...])
        dqa_ref[r0:r0+B,:]=jnp.where(own,dq,dqa_ref[r0:r0+B,:])
        dkr_ref[...]+=dot_tn(db,qrev_ref[r0:r0+B,:])
    ownk=lanes(C)
    qrel=jnp.where(lanes(NB),qrel_ref[...],zero)
    for i in range(L//C):
        at=slice(i*C,i*C+C)
        dst,wide=dst_ref.at[i%2],wide2_ref.at[i%2]
        dst[...]=ds_ref[:,at].T
        for g in range(C//16):
            rows=slice(16*g,16*g+16)
            part=jnp.concatenate([dst[rows,:],jnp.zeros((16,C),bf)],axis=1)
            wide[rows,:]=pltpu.roll(part,16*g,1,stride=1,stride_axis=0)
        db=dot_nn(wide[...],oy_ref[i*C:i*C+R+C,:]).astype(bf)
        dka_ref[at,:]+=dot_nn(dst[...],qrev_ref[...])+dot_nn(db,qrel)
        dva_ref[at,:]+=dot_tn(e_ref[0,:,at],dor_ref[...])
        kb=jnp.where(ownk,k_ref[at,:],zero)
        dqr_ref[...]+=dot_tn(db,kb)
    @pl.when(hh==1)
    def _():
        dq_ref[...]=dot_nn(J,dqa_ref[...].astype(bf)).astype(bf)
        dk_ref[...]=dka_ref[...].astype(bf)
        dv_ref[...]=(dva_ref[...]*(1.0/SCALE)).astype(bf)

def attention_backward(q,k,v,do,ctx,e,key_rel,query_rel,onehot_x,onehot_y,B=128,C=128):
    R,F=q.shape; L=k.shape[0]; W=L+R; pairs=F//128
    col=lambda n: pl.BlockSpec((n,128),lambda p,h:(0,p))
    full=pl.BlockSpec((W,NB),lambda p,h:(0,0))
    flops=2*pairs*2*R*L*128*8
    return pl.pallas_call(functools.partial(bwd_kernel,R,L,B,C),
        grid=(pairs,2),
        in_specs=[col(R),col(L),col(L),col(R),col(R),pl.BlockSpec((1,R,L),lambda p,h:(2*p+h,0,0)),col(NB),col(NB),full,full],
        out_specs=[col(R),col(L),col(L),col(NB),col(NB)],
        out_shape=[jax.ShapeDtypeStruct((R,F),bf),jax.ShapeDtypeStruct((L,F),bf),jax.ShapeDtypeStruct((L,F),bf),
                   jax.ShapeDtypeStruct((NB,F),f32),jax.ShapeDtypeStruct((NB,F),f32)],
        scratch_shapes=[pltpu.VMEM((R,L),bf),pltpu.VMEM((R,128),bf),pltpu.VMEM((R,128),bf),
                        pltpu.VMEM((R,128),f32),pltpu.VMEM((L,128),f32),pltpu.VMEM((L,128),f32),
                        pltpu.VMEM((R,128),f32),pltpu.VMEM((2,B,L),f32),pltpu.VMEM((2,B,L+B),bf),pltpu.VMEM((2,C,R),bf),pltpu.VMEM((2,C,R+C),bf)],
        compiler_params=pltpu.CompilerParams(vmem_limit_bytes=48*1024*1024,dimension_semantics=("arbitrary","arbitrary")),
        cost_estimate=pl.CostEstimate(flops=flops,bytes_accessed=2*pairs*R*L*2+20*L*F,transcendentals=0),
        name="attend_back",
    )(q,k,v,do,ctx,e,key_rel,query_rel,onehot_x,onehot_y)

EPS=1e-6

def gelu_parts(v):
    a=jnp.abs(v)
    t=1.0/(1.0+(0.3275911/math.sqrt(2.0))*a)
    bell=jnp.exp(-0.5*v*v)
    poly=t*(0.127414796+t*(-0.142248368+t*(0.7107068705+t*(-0.7265760135+t*0.5307027145))))
    tail=poly*bell
    phi=jnp.where(v>0,1.0-tail,tail)
    return v*phi, phi+v*bell*(1.0/math.sqrt(2.0*math.pi))

def feed_kernel(R,D,tiles,per,rows_in,own_rows,ctx_ref,tok_ref,og_ref,scale_ref,wo_ref,late_ref,bias_ref,gain_ref,shift_ref,
                res_ref,dres_ref,do_ref,sums_ref,bsum_ref,grad_ref,
                u1_ref,r1_ref,low_ref,acc_ref,pre_ref,gated_ref,gp_ref,dfeed_ref,stage_ref,tail_ref,datt_ref,sem):
    step=pl.program_id(0)
    width=per*rows_in
    CH=64
    def chunks(f):
        def body(i,c):
            f(pl.ds(pl.multiple_of(i*CH,CH),CH))
            return c
        lax.fori_loop(0,R//CH,body,0)
    mean=lambda x: jnp.mean(x,axis=1,keepdims=True)
    gain=lambda i: gain_ref[i:i+1,:]
    shift=lambda i: shift_ref[i:i+1,:]
    def add_sum(i,x):
        sums_ref[i:i+1,:]+=jnp.sum(x,axis=0,keepdims=True)
    @pl.when(step==0)
    def _():
        sums_ref[...]=jnp.zeros_like(sums_ref)
        acc_ref[...]=dot_nn(ctx_ref[...],wo_ref[...])
        def norm(at):
            v=tok_ref[at,:].astype(f32)+acc_ref[at,:]+shift(0)
            c=v-mean(v)
            r=lax.rsqrt(mean(c*c)+EPS)
            u=c*r
            u1_ref[at,:]=u
            r1_ref[at,:]=jnp.broadcast_to(r,(CH,128))
            h=u*gain(0)+shift(1)
            low_ref[at,:]=h.astype(bf)
            acc_ref[at,:]=h+shift(2)
        chunks(norm)
    w_in=late_ref[:,0:rows_in,:].reshape(width,D)
    w_outer=late_ref[:,rows_in:2*rows_in,:].reshape(width,D)
    @pl.when(step<tiles)
    def _():
        pre_ref[...]=dot_nt(low_ref[...],w_in)
        def act(at):
            g,gp=gelu_parts(pre_ref[at,:]+bias_ref[0])
            gated_ref[step,at,:]=g.astype(bf)
            gp_ref[step,at,:]=gp.astype(bf)
        chunks(act)
        acc_ref[...]+=dot_nn(gated_ref[step],w_outer)
    @pl.when(step==tiles-1)
    def _():
        def norm(at):
            v=acc_ref[at,:]
            c=v-mean(v)
            r=lax.rsqrt(mean(c*c)+EPS)
            u=c*r
            res_ref[at,:]=(u*gain(1)+shift(3)).astype(bf)
            top=og_ref[at,:].astype(f32)
            add_sum(1,top*u)
            add_sum(5,top)
            e=top*gain(1)
            d=(e-mean(e)-u*mean(e*u))*r
            add_sum(4,d)
            dfeed_ref[at,:]=d.astype(bf)
            acc_ref[at,:]=d
        chunks(norm)
    @pl.when(step>=tiles)
    def _():
        k=step-tiles
        slot=lax.rem(k,2)
        pre_ref[...]=dot_nt(dfeed_ref[...],w_outer)
        def act(at):
            d=(pre_ref[at,:]*gp_ref[k,at,:].astype(f32)).astype(bf)
            gp_ref[k,at,:]=d
        chunks(act)
        bsum_ref[0]=jnp.sum(gp_ref[k].astype(f32),axis=0,keepdims=True)
        def out(kk,s):
            return pltpu.make_async_copy(stage_ref.at[s],grad_ref.at[pl.ds(kk*per,per),pl.ds(0,2*rows_in)],sem.at[s])
        @pl.when(k>=2)
        def _():
            out(k-2,slot).wait()
        stage_ref[slot,:,0:rows_in,:]=dot_tn(gp_ref[k],low_ref[...]).astype(bf).reshape(per,rows_in,D)
        stage_ref[slot,:,rows_in:2*rows_in,:]=dot_tn(gated_ref[k],dfeed_ref[...]).astype(bf).reshape(per,rows_in,D)
        out(k,slot).start()
        acc_ref[...]+=dot_nn(gp_ref[k],w_in)
        @pl.when(k==tiles-1)
        def _():
            def norm(at):
                d=acc_ref[at,:]
                u=u1_ref[at,:]
                r=r1_ref[at,0:1]
                add_sum(0,d*u)
                add_sum(3,d)
                e=d*gain(0)
                g=(e-mean(e)-u*mean(e*u))*r
                add_sum(2,g)
                dres_ref[at,:]=g
                datt_ref[at,:]=g.astype(bf)
            chunks(norm)
            do_ref[...]=(dot_nt(datt_ref[...],wo_ref[...])*scale_ref[...]).astype(bf)
            outer=dot_tn(ctx_ref[...],datt_ref[...])
            n=D//own_rows
            gap=tail_ref.shape[1]-own_rows
            for p in range(n):
                piece=outer[p*own_rows:p*own_rows+own_rows,:]
                if gap:
                    piece=jnp.concatenate([piece,jnp.zeros((gap,D),f32)],axis=0)
                tail_ref[p]=piece.astype(bf)
            last=pltpu.make_async_copy(tail_ref,grad_ref.at[:,pl.ds(2*rows_in,tail_ref.shape[1])],sem.at[2])
            last.start()
            if tiles>1:
                out(k-1,1-slot).wait()
            out(k,slot).wait()
            last.wait()

def feed(ctx,tokens,out_grad,scale,out_rows,late,bias,gain,shift,rows_in,own_rows,tiles=4):
    R,D=ctx.shape
    n,rows_late,_=late.shape
    per=n//tiles
    width=per*rows_in
    tail=rows_late-2*rows_in
    vm=lambda s: pl.BlockSpec(s,lambda i: (0,)*len(s))
    return pl.pallas_call(functools.partial(feed_kernel,R,D,tiles,per,rows_in,own_rows),
        grid=(2*tiles,),
        in_specs=[vm((R,D)),vm((R,D)),vm((R,D)),vm((R,D)),vm((D,D)),
                  pl.BlockSpec((per,rows_late,D),lambda i:(lax.rem(i,tiles),0,0)),
                  pl.BlockSpec((1,1,width),lambda i:(lax.rem(i,tiles),0,0)),vm((2,D)),vm((4,D))],
        out_specs=[vm((R,D)),vm((R,D)),vm((R,D)),vm((8,D)),pl.BlockSpec((1,1,width),lambda i:(jnp.maximum(i-tiles,0),0,0)),
                   pl.BlockSpec(memory_space=pl.ANY)],
        out_shape=[jax.ShapeDtypeStruct((R,D),bf),jax.ShapeDtypeStruct((R,D),f32),jax.ShapeDtypeStruct((R,D),bf),
                   jax.ShapeDtypeStruct((8,D),f32),jax.ShapeDtypeStruct((tiles,1,width),f32),
                   jax.ShapeDtypeStruct((n,rows_late,D),bf)],
        scratch_shapes=[pltpu.VMEM((R,D),f32),pltpu.VMEM((R,128),f32),pltpu.VMEM((R,D),bf),pltpu.VMEM((R,D),f32),
                        pltpu.VMEM((R,width),f32),pltpu.VMEM((tiles,R,width),bf),pltpu.VMEM((tiles,R,width),bf),
                        pltpu.VMEM((R,D),bf),pltpu.VMEM((2,per,2*rows_in,D),bf),pltpu.VMEM((n,tail,D),bf),pltpu.VMEM((R,D),bf),
                        pltpu.SemaphoreType.DMA((3,))],
        compiler_params=pltpu.CompilerParams(vmem_limit_bytes=58*1024*1024,dimension_semantics=("arbitrary",)),
        cost_estimate=pl.CostEstimate(flops=2*R*D*n*rows_in*6+6*R*D*D,bytes_accessed=4*n*rows_late*D+20*R*D,transcendentals=2*R*n*rows_in),
        name="feed",
    )(ctx,tokens,out_grad,scale,out_rows,late,bias,gain,shift)

MESH=pl.DeviceIdType.MESH

def places(n_t, n_dp):
    dp, t = lax.axis_index("dp"), lax.axis_index("tensor")
    high, core = dp // 2, dp % 2
    bits = (n_dp // 2).bit_length() - 1
    flips = [high + (1 - 2 * ((high // 2**i) % 2)) * 2**i for i in range(bits)]
    right, left = lax.rem(t + 1, n_t), lax.rem(t + n_t - 1, n_t)
    return dp, t, high, core, bits, flips, right, left

def meet(peers):
    barrier = pltpu.get_barrier_semaphore()
    for peer in peers:
        pl.semaphore_signal(barrier, inc=1, device_id=peer, device_id_type=MESH)
    pl.semaphore_wait(barrier, len(peers))

def remote(src, dst, send, recv, peer):
    return pltpu.make_async_remote_copy(src_ref=src, dst_ref=dst, send_sem=send, recv_sem=recv,
                                        device_id=peer, device_id_type=MESH)

def interleave(*lists):
    out = []
    for i in range(max(len(x) for x in lists)):
        out += [x[i] for x in lists if i < len(x)]
    return out

def gather_kernel(n_t, n_dp, tok_ref, pack_ref, toks_ref, packs_ref, own_sem, tok_send, tok_recv, pack_send, pack_recv):
    dp, t, high, core, bits, flips, right, left = places(n_t, n_dp)
    peers = [{"tensor": right}, {"tensor": left}, {"dp": high * 2 + 1 - core}] + [{"dp": f * 2 + core} for f in flips]
    meet(peers)
    own_tok = pltpu.make_async_copy(tok_ref, toks_ref.at[t], own_sem.at[0])
    own_pack = pltpu.make_async_copy(pack_ref, packs_ref.at[t, high, core], own_sem.at[1])
    own_tok.start()
    own_pack.start()
    rows = tok_ref.shape[0]
    half = rows // 2
    token = {}
    pack = {}

    def send_pack(s):
        b = lax.rem(t - s + n_t, n_t)
        src = pack_ref if s == 0 else packs_ref.at[b, high, core]
        pack[s] = remote(src, packs_ref.at[b, high, core], pack_send.at[s], pack_recv.at[s], {"tensor": right})
        pack[s].start()

    def send_token(s, j):
        b = lax.rem(t - s + n_t, n_t)
        src = (tok_ref if s == 0 else toks_ref.at[b]).at[pl.ds(j * half, half)]
        token[s, j] = remote(src, toks_ref.at[b, pl.ds(j * half, half)], tok_send.at[s, j], tok_recv.at[s, j], {"tensor": right})
        token[s, j].start()

    def swap(i):
        s = n_t - 1 + i
        if i < bits:
            base = (high // 2**i) * 2**i
            part = packs_ref.at[:, pl.ds(base, 2**i), core]
            peer = {"dp": flips[i] * 2 + core}
        else:
            part = packs_ref.at[:, :, core]
            peer = {"dp": high * 2 + 1 - core}
        pack[s] = remote(part, part, pack_send.at[s], pack_recv.at[s], peer)
        pack[s].start()

    send_pack(0)
    send_token(0, 0)
    send_token(0, 1)
    for s in range(1, n_t - 1):
        pack[s - 1].wait_recv()
        send_pack(s)
    pack[n_t - 2].wait_recv()
    own_pack.wait()
    swap(0)

    def token_step(s):
        def run():
            for j in range(2):
                token[s - 1, j].wait_recv()
                if s < n_t - 1:
                    send_token(s, j)
        return run

    def pack_step(i):
        def run():
            pack[n_t - 1 + i - 1].wait_recv()
            if i <= bits:
                swap(i)
        return run

    for step in interleave([token_step(s) for s in range(1, n_t)], [pack_step(i) for i in range(1, bits + 2)]):
        step()
    own_tok.wait()
    for copy in list(pack.values()) + list(token.values()):
        copy.wait_send()

def gather_start(tokens, pack, n_t, n_dp):
    rows, D = tokens.shape
    pr = pack.shape[0]
    bits = (n_dp // 2).bit_length() - 1
    n_pack = n_t + bits
    hbm = pl.BlockSpec(memory_space=pl.ANY)
    return pl.pallas_call(
        functools.partial(gather_kernel, n_t, n_dp),
        out_shape=[jax.ShapeDtypeStruct((n_t, rows, D), bf), jax.ShapeDtypeStruct((n_t, n_dp // 2, 2, pr, D), bf)],
        in_specs=[hbm, hbm], out_specs=[hbm, hbm],
        scratch_shapes=[pltpu.SemaphoreType.DMA((2,)), pltpu.SemaphoreType.DMA((n_t - 1, 2)), pltpu.SemaphoreType.DMA((n_t - 1, 2)),
                        pltpu.SemaphoreType.DMA((n_pack,)), pltpu.SemaphoreType.DMA((n_pack,))],
        compiler_params=pltpu.CompilerParams(collective_id=0, has_side_effects=True),
        name="gather_start",
    )(tokens, pack)

def reduce_kernel(n_t, n_dp, tok_ref, pack_ref, tok_out, pack_out, tok_got, tok_acc, first, acc, ring_got, ring_acc, *rest):
    dp, t, high, core, bits, flips, right, left = places(n_t, n_dp)
    halves, (tok_send, tok_recv, send, recv) = rest[:bits], rest[bits:]
    peers = [{"tensor": right}, {"tensor": left}, {"dp": high * 2 + 1 - core}] + [{"dp": f * 2 + core} for f in flips]
    meet(peers)
    n_hi = n_dp // 2
    pr = pack_ref.shape[3]
    rows = tok_ref.shape[1]
    piece = 64 if rows % 64 == 0 else rows
    copies = {}

    def block(s):
        return lax.rem(t - 1 - s + 2 * n_t, n_t)

    def send_token(s):
        src = tok_ref.at[block(0)] if s == 0 else tok_acc.at[s - 1]
        copies["t", s] = remote(src, tok_got.at[s], tok_send.at[s], tok_recv.at[s], {"tensor": right})
        copies["t", s].start()

    def token_step(s):
        def run():
            copies["t", s - 1].wait_recv()
            last = s == n_t - 1
            b = t if last else block(s)

            @pl.loop(0, rows // piece)
            def _(i):
                at = pl.ds(pl.multiple_of(i * piece, piece), piece)
                total = tok_got[s - 1, at].astype(f32) + tok_ref[b, at].astype(f32)
                if last:
                    tok_out[at] = total
                else:
                    tok_acc[s - 1, at] = total.astype(bf)
            if not last:
                send_token(s)
        return run

    def start(k, src, dst, peer):
        copies["p", k] = remote(src, dst, send.at[k], recv.at[k], peer)
        copies["p", k].start()

    def swap(k):
        if k == 0:
            start(0, pack_ref.at[:, :, 1 - core], first, {"dp": high * 2 + 1 - core})
        else:
            i = bits - k
            base = (high // 2**(i + 1)) * 2**(i + 1)
            other = base + (1 - (high // 2**i) % 2) * 2**i
            start(k, acc.at[:, pl.ds(other, 2**i)], halves[i], {"dp": flips[i] * 2 + core})

    def add_swap(k):
        copies["p", k].wait_recv()
        if k == 0:
            @pl.loop(0, n_t * n_hi)
            def _(m):
                a, b = m // n_hi, m % n_hi
                acc[a, b] = (pack_ref[a, b, core].astype(f32) + first[a, b].astype(f32)).astype(bf)
        else:
            i = bits - k
            keep = (high // 2**i) * 2**i

            @pl.loop(0, n_t * 2**i)
            def _(m):
                a, b = m // 2**i, m % 2**i
                acc[a, keep + b] = (acc[a, keep + b].astype(f32) + halves[i][a, b].astype(f32)).astype(bf)

    def ring(s):
        src = acc.at[block(0), high] if s == 0 else ring_acc.at[s - 1]
        start(bits + 1 + s, src, ring_got.at[s], {"tensor": right})

    def ring_add(s):
        copies["p", bits + s].wait_recv()
        last = s == n_t - 1
        b = t if last else block(s)
        total = ring_got[s - 1].astype(f32) + acc[b, high].astype(f32)
        if last:
            pack_out[...] = total
        else:
            ring_acc[s - 1] = total.astype(bf)

    swap(0)
    send_token(0)

    def pack_step(k):
        def run():
            if k <= bits:
                add_swap(k)
                if k < bits:
                    swap(k + 1)
                else:
                    ring(0)
            else:
                s = k - bits
                ring_add(s)
                if s < n_t - 1:
                    ring(s)
        return run

    for step in interleave([pack_step(k) for k in range(bits + n_t)], [lambda: None] + [token_step(s) for s in range(1, n_t)]):
        step()
    for copy in copies.values():
        copy.wait_send()

def reduce_end(spread, pack, n_t, n_dp):
    _, rows, D = spread.shape
    pr = pack.shape[3]
    n_hi = n_dp // 2
    bits = n_hi.bit_length() - 1
    n_pack = bits + n_t
    vm = pl.BlockSpec(memory_space=pltpu.VMEM)
    return pl.pallas_call(
        functools.partial(reduce_kernel, n_t, n_dp),
        out_shape=[jax.ShapeDtypeStruct((rows, D), f32), jax.ShapeDtypeStruct((pr, D), f32)],
        in_specs=[vm, vm], out_specs=[vm, vm],
        scratch_shapes=[pltpu.VMEM((n_t - 1, rows, D), bf), pltpu.VMEM((max(n_t - 2, 1), rows, D), bf),
                        pltpu.VMEM((n_t, n_hi, pr, D), bf), pltpu.VMEM((n_t, n_hi, pr, D), bf),
                        pltpu.VMEM((n_t - 1, pr, D), bf), pltpu.VMEM((max(n_t - 2, 1), pr, D), bf)]
                       + [pltpu.VMEM((n_t, 2**i, pr, D), bf) for i in range(bits)]
                       + [pltpu.SemaphoreType.DMA((n_t - 1,)), pltpu.SemaphoreType.DMA((n_t - 1,)),
                          pltpu.SemaphoreType.DMA((n_pack,)), pltpu.SemaphoreType.DMA((n_pack,))],
        compiler_params=pltpu.CompilerParams(collective_id=1, has_side_effects=True, vmem_limit_bytes=56 * 1024 * 1024),
        name="reduce_end",
    )(spread, pack)

GROUPS, TILES = 32, 4
ALL=("tensor","dp")

def project(inputs, weights, bias):
    return (jnp.einsum("td,fd->tf", inputs, weights, preferred_element_type=f32) + bias).astype(bf)

def local(tokens, w_query, w_key, w_value, w_out, qkv_bias, w_ff_in, w_ff_out, ff_bias, rel_table,
          gains, shifts, rel_bucket, lengths, out_grad):
    D = tokens.shape[1]
    n_t, n_dp = lax.axis_size("tensor"), lax.axis_size("dp")
    n_all = n_t * n_dp
    t = lax.axis_index("tensor")
    R = tokens.shape[0]
    L = (rel_bucket.shape[0] + 1) // 2
    W = L + R
    part = rel_table.shape[0] // n_t
    wide, inner, cols = qkv_bias.shape[1], ff_bias.shape[0], gains.shape[1]
    misc = jnp.concatenate([qkv_bias.reshape(-1), ff_bias, gains.reshape(-1), shifts.reshape(-1)])
    used = misc.shape[0]
    misc = jnp.pad(misc, (0, D - used))[None]
    rel_part = lax.dynamic_slice_in_dim(rel_table, t * part, part, 0)
    small = jnp.concatenate([rel_part, misc], axis=0)
    early = jnp.concatenate([w_query, w_key, w_value, small], axis=0)
    own_rows = w_query.shape[0]
    late_rows = w_ff_in.shape[0]
    early_rows = early.shape[0]
    early = jnp.pad(early, ((0, -early_rows % 16), (0, 0)))
    even = late_rows % 16 == 0 and own_rows % 8 == 0
    late = jnp.concatenate([w_ff_in, w_ff_out, w_out], axis=0)
    late_own = late.shape[0]
    late = jnp.pad(late, ((0, -late_own % 16), (0, 0)))
    gathered, early_all = gather_start(tokens, early, n_t, n_dp)
    late_all = lax.all_gather(late, ALL, axis=0, tiled=False)
    gathered = gathered.reshape(L, D)
    early_all = early_all.reshape(n_all, early.shape[0], D)
    cut = lambda x, at, n: x[:, at:at + n].reshape(n_all * n, D)
    query_rows, key_rows, value_rows = [cut(early_all, i * own_rows, own_rows) for i in range(3)]
    small_all = early_all[:, 3 * own_rows:early_rows]
    out_rows = cut(late_all, 2 * late_rows, own_rows)
    groups = n_all if even else GROUPS
    group_rows, group_own = n_all * late_rows // groups, D // groups
    if not even:
        sections = [cut(late_all, 0, late_rows), cut(late_all, late_rows, late_rows)]
        late_all = jnp.concatenate([x.reshape(groups, group_rows, D) for x in sections]
                                   + [jnp.zeros((groups, -(-group_own // 16) * 16, D), bf)], axis=1)
    misc_all = small_all[:, part]
    o1 = 3 * wide
    o2 = o1 + inner
    o3 = o2 + 2 * cols
    bias = misc_all[:, :o1].reshape(n_all, 3, wide).transpose(1, 0, 2).reshape(3, D).astype(f32)
    inner_bias = misc_all[:, o1:o2].reshape(-1).astype(f32)
    first = misc_all[:n_dp]
    gain = first[:, o2:o3].reshape(n_dp, 2, cols).transpose(1, 0, 2).reshape(2, D).astype(f32)
    shift = first[:, o3:used].reshape(n_dp, 4, cols).transpose(1, 0, 2).reshape(4, D).astype(f32)
    table = small_all[:, :part].reshape(n_t, n_dp, part, D).transpose(1, 0, 2, 3).reshape(NB, D)

    query = project(tokens, query_rows, bias[0])
    key = project(gathered, key_rows, bias[1])
    value = project(gathered, value_rows, bias[2])
    key_rel = project(table, key_rows, bias[1])
    query_rel = project(table, query_rows, bias[0])

    none = jnp.full((1,), -1, jnp.int32)
    ahead = jnp.concatenate([rel_bucket, none])
    back = jnp.concatenate([rel_bucket[::-1], none])
    buckets = jnp.arange(NB, dtype=jnp.int32)[None, :]
    pick = lambda line, start: (lax.dynamic_slice_in_dim(line, start, W, 0)[:, None] == buckets).astype(bf)
    pick_x = pick(back, L - R - R * t)
    pick_y = pick(ahead, L - R - R * t)
    pick_u = pick(back, R * t)
    key_table = jnp.dot(pick_x, key_rel, preferred_element_type=f32).astype(bf)
    query_table = jnp.dot(pick_u, query_rel, preferred_element_type=f32).astype(bf)
    mask = jnp.where(jnp.arange(L, dtype=jnp.int32) < lengths[0], 0.0, -1e9).astype(bf)
    mask = jnp.broadcast_to(mask[:, None], (L, 128))

    context, scale, shares = attention_forward(query, key, value, key_table, query_table, mask)
    layer_result_rows, d_resid_one, d_scaled, sums, bias_sums, late_grad = feed(
        context, tokens, out_grad, scale, out_rows, late_all, inner_bias.reshape(TILES, 1, -1), gain, shift, group_rows, group_own)
    d_query, d_key, d_value, d_key_rel, d_query_rel = attention_backward(
        query, key, value, d_scaled, context, shares, key_rel, query_rel, pick_x, pick_y)

    parted = lambda x: x.astype(bf).reshape(n_all, -1, D)
    if not even:
        late_grad = jnp.concatenate([
            parted(late_grad[:, :group_rows]), parted(late_grad[:, group_rows:2 * group_rows]),
            parted(late_grad[:, 2 * group_rows:2 * group_rows + group_own]),
            jnp.zeros((n_all, late.shape[0] - late_own, D), bf)], axis=1)
    late_sum = lax.psum_scatter(late_grad, ALL, scatter_dimension=0, tiled=True)[0].astype(f32)
    g_inner, g_outer, g_out = late_sum[:late_rows], late_sum[late_rows:2 * late_rows], late_sum[2 * late_rows:late_own]
    dqr, dkr = d_query_rel.astype(bf), d_key_rel.astype(bf)
    grad_query = jnp.einsum("tf,td->fd", d_query, tokens, preferred_element_type=f32) + jnp.einsum(
        "tf,td->fd", dqr, table, preferred_element_type=f32)
    grad_key = jnp.einsum("tf,td->fd", d_key, gathered, preferred_element_type=f32) + jnp.einsum(
        "tf,td->fd", dkr, table, preferred_element_type=f32)
    grad_value = jnp.einsum("tf,td->fd", d_value, gathered, preferred_element_type=f32)
    bias_gradient = jnp.stack([
        jnp.sum(d_query.astype(f32), axis=0) + jnp.sum(d_query_rel, axis=0),
        jnp.sum(d_key.astype(f32), axis=0) + jnp.sum(d_key_rel, axis=0),
        jnp.sum(d_value.astype(f32), axis=0)])
    d_rel = jnp.dot(dqr, query_rows, preferred_element_type=f32) + jnp.dot(dkr, key_rows, preferred_element_type=f32)
    own = jnp.dot(d_query, query_rows, preferred_element_type=f32)
    spread = (jnp.dot(d_key, key_rows, preferred_element_type=f32)
              + jnp.dot(d_value, value_rows, preferred_element_type=f32)).astype(bf)
    shape_dp = lambda x, k: jnp.broadcast_to(
        x.reshape(k, n_dp, cols).transpose(1, 0, 2).reshape(1, n_dp, k * cols), (n_t, n_dp, k * cols)).reshape(n_all, k * cols)
    line = jnp.concatenate([
        bias_gradient.reshape(3, n_all, wide).transpose(1, 0, 2).reshape(n_all, o1),
        bias_sums.reshape(n_all, inner),
        shape_dp(sums[:2], 2), shape_dp(sums[2:6], 4)], axis=1)
    line = jnp.pad(line[:, None], ((0, 0), (0, 7), (0, D - used)))
    rel_rows = rel_table.shape[0]
    d_rel_all = jnp.broadcast_to(d_rel.reshape(1, n_dp, rel_rows, D), (n_t, n_dp, rel_rows, D)).reshape(n_all, rel_rows, D)
    early_grad = jnp.concatenate([parted(grad_query), parted(grad_key), parted(grad_value), line.astype(bf), d_rel_all.astype(bf)], axis=1)
    end_rows = early_grad.shape[1]
    early_grad = jnp.pad(early_grad, ((0, 0), (0, -end_rows % 16), (0, 0)))
    back_sum, early_sum = reduce_end(spread.reshape(n_t, R, D), early_grad.reshape(n_t, n_dp // 2, 2, -1, D), n_t, n_dp)
    tokens_grad = d_resid_one + own + back_sum
    g_query, g_key, g_value = [early_sum[i * own_rows:(i + 1) * own_rows] for i in range(3)]
    row = early_sum[3 * own_rows]
    g_rel = early_sum[3 * own_rows + 8:end_rows]
    return (layer_result_rows, tokens_grad, g_query, g_key, g_value, g_out,
            row[:o1].reshape(3, wide), g_inner, g_outer, row[o1:o2], g_rel,
            row[o2:o3].reshape(2, cols), row[o3:used].reshape(4, cols))

def solution(mesh):
    rows, params = P(("dp", "tensor"), None), P(ALL, None)
    return jax.shard_map(
        local, mesh=mesh,
        in_specs=(rows, params, params, params, params, P(None, ALL), params, params, P(ALL), P("dp", None),
                  P(None, "dp"), P(None, "dp"), P(), P("dp"), rows),
        out_specs=(rows, rows, params, params, params, params, P(None, ALL), params, params, P(ALL), P("dp", None),
                   P(None, "dp"), P(None, "dp")),
        check_vma=False)
```

```python
import functools
import math

import jax
import jax.numpy as jnp
from jax import lax
from jax.experimental import pallas as pl
from jax.experimental.pallas import tpu as pltpu
from jax.sharding import PartitionSpec as P

bf = jnp.bfloat16
f32 = jnp.float32
DH=64; NB=256
SCALE=1.0/math.sqrt(3*DH)
LOG2E=math.log2(math.e)

def dot_nt(a,b):
    return lax.dot_general(a,b,(((1,),(1,)),((),())),preferred_element_type=f32)
def dot_nn(a,b):
    return lax.dot_general(a,b,(((1,),(0,)),((),())),preferred_element_type=f32)
def dot_tn(a,b):
    return lax.dot_general(a,b,(((0,),(0,)),((),())),preferred_element_type=f32)

def flip_matrix(n):
    a=lax.broadcasted_iota(jnp.int32,(n,n),0); b=lax.broadcasted_iota(jnp.int32,(n,n),1)
    return jnp.where(a+b==n-1,1.0,0.0).astype(bf)

def flip_rows(x):
    n,w=x.shape
    idx=7-lax.broadcasted_iota(jnp.int32,(8,w),0)
    return jnp.concatenate([jnp.take_along_axis(x[n-8-8*g:n-8*g],idx,axis=0) for g in range(n//8)],axis=0)

def fwd_kernel(R,L,B,C,mask_ref,q_ref,k_ref,v_ref,kt_ref,qr_ref,ctx_ref,scale_ref,e_ref,yt_ref,acc_ref,km_ref,y_ref,s_ref,x_ref,p_ref):
    hh=pl.program_id(1)
    lane=lambda n: lax.broadcasted_iota(jnp.int32,(n,128),1)
    def lanes(n): return (lane(n)//DH)==hh
    zero,one=jnp.zeros((),bf),jnp.ones((),bf)
    spare=(1-hh)*DH
    for i in range(L//C):
        at=slice(i*C,i*C+C)
        km_ref[at,:]=jnp.where(lane(C)==spare,mask_ref[at,:],k_ref[at,:])
    def yblock(i):
        at=slice(i*C,i*C+C)
        us=L-C-i*C
        kb=jnp.where(lanes(C),k_ref[at,:],zero)
        y=y_ref.at[i%2]
        y[...]=dot_nt(kb,qr_ref[us:us+R+C,:])
        for g in range(C//16):
            rows=slice(16*g,16*g+16)
            part=y[rows,:].astype(bf)
            s_part=pltpu.roll(part,R+1+16*g,1,stride=1,stride_axis=0)[:,:R]
            yt_ref[i%2,rows,:]=s_part
        return yt_ref[i%2].T
    for i in range(L//C):
        acc_ref[:,i*C:i*C+C]=yblock(i)
    v_one=jnp.where(lanes(L),v_ref[...],one)
    own=lanes(B)
    sp=lane(B)==spare
    accs=[]
    for i in range(R//B):
        r0=i*B
        qm=q_ref[r0:r0+B,:]
        q=jnp.where(own,qm,zero)
        qs=jnp.where(sp,one,q)
        ws=R-B-r0
        x,s=x_ref.at[i%2],s_ref.at[i%2]
        x[...]=dot_nt(q,kt_ref[ws:ws+L+B,:])
        s[...]=dot_nt(qs,km_ref[...])
        rr=R-B-r0
        p=p_ref.at[i%2]
        for g in range(B//16):
            rows=slice(16*g,16*g+16)
            xr=pltpu.roll(x[rows,:],(L+1+16*g)%(L+B),1,stride=1,stride_axis=0)[:,:L]
            raw=s[rows,:]+xr+acc_ref[r0+16*g:r0+16*g+16,:].astype(f32)
            s[rows,:]=raw
            top=raw[:,:128]
            for j in range(1,L//128):
                top=jnp.maximum(top,raw[:,128*j:128*j+128])
            p[rows,:]=top
        p[...]=jnp.broadcast_to(jnp.max(p[...],axis=1,keepdims=True)*(SCALE*LOG2E),(B,128))
        for g in range(B//16):
            rows=slice(16*g,16*g+16)
            peak=jnp.concatenate([p[rows,:]]*(L//128),axis=1)
            e=jnp.exp2(s[rows,:]*(SCALE*LOG2E)-peak)
            e=flip_rows(e).astype(bf)
            to=rr+B-16-16*g
            e_ref[0,to:to+16,:]=e
        accs.append(dot_nn(e_ref[0,rr:rr+B,:],v_one))
    acc=jnp.concatenate(accs[::-1],axis=0)
    inv=1.0/pltpu.roll(acc,DH,1)
    J=flip_matrix(R)
    ctx=dot_nn(J,(acc*inv).astype(bf)).astype(bf)
    mine=lanes(R)
    inv_hi=inv.astype(bf)
    sc=dot_nn(J,inv_hi)+dot_nn(J,(inv-inv_hi.astype(f32)).astype(bf))
    sc=sc*SCALE
    @pl.when(hh==0)
    def _():
        ctx_ref[...]=ctx
        scale_ref[...]=sc
    @pl.when(hh==1)
    def _():
        ctx_ref[...]=jnp.where(mine,ctx,ctx_ref[...])
        scale_ref[...]=jnp.where(mine,sc,scale_ref[...])

def attention_forward(q,k,v,kt,qr,mask,B=128,C=256):
    R,F=q.shape; L=k.shape[0]; W=L+R; pairs=F//128
    B=min(B,R)
    col=lambda n: pl.BlockSpec((n,128),lambda p,h:(0,p))
    flops=2*pairs*2*R*L*128*4
    return pl.pallas_call(functools.partial(fwd_kernel,R,L,B,C),
        grid=(pairs,2),
        in_specs=[pl.BlockSpec((L,128),lambda p,h:(0,0)),col(R),col(L),col(L),col(W),col(W)],
        out_specs=[col(R),col(R),pl.BlockSpec((1,R,L),lambda p,h:(2*p+h,0,0))],
        out_shape=[jax.ShapeDtypeStruct((R,F),bf),jax.ShapeDtypeStruct((R,F),f32),jax.ShapeDtypeStruct((2*pairs,R,L),bf)],
        scratch_shapes=[pltpu.VMEM((2,C,R),bf),pltpu.VMEM((R,L),bf),pltpu.VMEM((L,128),bf),pltpu.VMEM((2,C,R+C),f32),
                        pltpu.VMEM((2,B,L),f32),pltpu.VMEM((2,B,L+B),f32),pltpu.VMEM((2,B,128),f32)],
        compiler_params=pltpu.CompilerParams(vmem_limit_bytes=48*1024*1024,dimension_semantics=("arbitrary","arbitrary")),
        cost_estimate=pl.CostEstimate(flops=flops,bytes_accessed=2*pairs*R*L*2+10*L*F,transcendentals=2*pairs*R*L),
        name="attend",
    )(mask,q,k,v,kt,qr)

def bwd_kernel(R,L,B,C,q_ref,k_ref,v_ref,do_ref,ctx_ref,e_ref,kr_ref,qrel_ref,ox_ref,oy_ref,
               dq_ref,dk_ref,dv_ref,dkr_ref,dqr_ref,ds_ref,dor_ref,qrev_ref,dqa_ref,dka_ref,dva_ref,
               delta_ref,dp_ref,wide_ref,dst_ref,wide2_ref):
    hh=pl.program_id(1)
    def lanes(n): return (lax.broadcasted_iota(jnp.int32,(n,128),1)//DH)==hh
    zero=jnp.zeros((),bf)
    @pl.when(hh==0)
    def _():
        dqa_ref[...]=jnp.zeros_like(dqa_ref)
        dka_ref[...]=jnp.zeros_like(dka_ref)
        dva_ref[...]=jnp.zeros_like(dva_ref)
        dkr_ref[...]=jnp.zeros_like(dkr_ref)
        dqr_ref[...]=jnp.zeros_like(dqr_ref)
    J=flip_matrix(R)
    do=jnp.where(lanes(R),dot_nn(J,do_ref[...]).astype(bf),zero)
    ctx=dot_nn(J,ctx_ref[...])
    dor_ref[...]=do
    qrev_ref[...]=jnp.where(lanes(R),dot_nn(J,q_ref[...]).astype(bf),zero)
    delta_ref[...]=jnp.broadcast_to(jnp.sum(do.astype(f32)*ctx,axis=1,keepdims=True),(R,128))
    own=lanes(B)
    for i in range(R//B):
        r0=i*B
        dp,wide=dp_ref.at[i%2],wide_ref.at[i%2]
        dp[...]=dot_nt(dor_ref[r0:r0+B,:],v_ref[...])
        for g in range(B//16):
            rows=slice(16*g,16*g+16)
            at=slice(r0+16*g,r0+16*g+16)
            delta=jnp.concatenate([delta_ref[at,:]]*(L//128),axis=1)
            ds=(e_ref[0,at,:].astype(f32)*(dp[rows,:]-delta)).astype(bf)
            ds_ref[at,:]=ds
            part=jnp.concatenate([ds,jnp.zeros((16,B),bf)],axis=1)
            wide[rows,:]=pltpu.roll(part,16*g,1,stride=1,stride_axis=0)
        db=dot_nt(wide[...],ox_ref[:,r0:r0+L+B]).astype(bf)
        dq=dot_nn(ds_ref[r0:r0+B,:],k_ref[...])+dot_nn(db,kr_ref[...])
        dqa_ref[r0:r0+B,:]=jnp.where(own,dq,dqa_ref[r0:r0+B,:])
        dkr_ref[...]+=dot_tn(db,qrev_ref[r0:r0+B,:])
    ownk=lanes(C)
    qrel=jnp.where(lanes(NB),qrel_ref[...],zero)
    for i in range(L//C):
        at=slice(i*C,i*C+C)
        dst,wide=dst_ref.at[i%2],wide2_ref.at[i%2]
        dst[...]=ds_ref[:,at].T
        for g in range(C//16):
            rows=slice(16*g,16*g+16)
            part=jnp.concatenate([dst[rows,:],jnp.zeros((16,C),bf)],axis=1)
            wide[rows,:]=pltpu.roll(part,16*g,1,stride=1,stride_axis=0)
        db=dot_nt(wide[...],oy_ref[:,i*C:i*C+R+C]).astype(bf)
        dka_ref[at,:]+=dot_nn(dst[...],qrev_ref[...])+dot_nn(db,qrel)
        dva_ref[at,:]+=dot_tn(e_ref[0,:,at],dor_ref[...])
        kb=jnp.where(ownk,k_ref[at,:],zero)
        dqr_ref[...]+=dot_tn(db,kb)
    @pl.when(hh==1)
    def _():
        dq_ref[...]=dot_nn(J,dqa_ref[...].astype(bf)).astype(bf)
        dk_ref[...]=dka_ref[...].astype(bf)
        dv_ref[...]=(dva_ref[...]*(1.0/SCALE)).astype(bf)

def attention_backward(q,k,v,do,ctx,e,key_rel,query_rel,onehot_x,onehot_y,B=128,C=128):
    R,F=q.shape; L=k.shape[0]; W=L+R; pairs=F//128
    col=lambda n: pl.BlockSpec((n,128),lambda p,h:(0,p))
    full=pl.BlockSpec((NB,W),lambda p,h:(0,0))
    flops=2*pairs*2*R*L*128*8
    return pl.pallas_call(functools.partial(bwd_kernel,R,L,B,C),
        grid=(pairs,2),
        in_specs=[col(R),col(L),col(L),col(R),col(R),pl.BlockSpec((1,R,L),lambda p,h:(2*p+h,0,0)),col(NB),col(NB),full,full],
        out_specs=[col(R),col(L),col(L),col(NB),col(NB)],
        out_shape=[jax.ShapeDtypeStruct((R,F),bf),jax.ShapeDtypeStruct((L,F),bf),jax.ShapeDtypeStruct((L,F),bf),
                   jax.ShapeDtypeStruct((NB,F),f32),jax.ShapeDtypeStruct((NB,F),f32)],
        scratch_shapes=[pltpu.VMEM((R,L),bf),pltpu.VMEM((R,128),bf),pltpu.VMEM((R,128),bf),
                        pltpu.VMEM((R,128),f32),pltpu.VMEM((L,128),f32),pltpu.VMEM((L,128),f32),
                        pltpu.VMEM((R,128),f32),pltpu.VMEM((2,B,L),f32),pltpu.VMEM((2,B,L+B),bf),pltpu.VMEM((2,C,R),bf),pltpu.VMEM((2,C,R+C),bf)],
        compiler_params=pltpu.CompilerParams(vmem_limit_bytes=48*1024*1024,dimension_semantics=("arbitrary","arbitrary")),
        cost_estimate=pl.CostEstimate(flops=flops,bytes_accessed=2*pairs*R*L*2+20*L*F,transcendentals=0),
        name="attend_back",
    )(q,k,v,do,ctx,e,key_rel,query_rel,onehot_x,onehot_y)

EPS=1e-6

def gelu_parts(v):
    a=jnp.abs(v)
    t=1.0/(1.0+(0.3275911/math.sqrt(2.0))*a)
    bell=jnp.exp(-0.5*v*v)
    poly=t*(0.127414796+t*(-0.142248368+t*(0.7107068705+t*(-0.7265760135+t*0.5307027145))))
    tail=poly*bell
    phi=jnp.where(v>0,1.0-tail,tail)
    return v*phi, phi+v*bell*(1.0/math.sqrt(2.0*math.pi))

def feed_kernel(R,D,tiles,per,rows_in,own_rows,ctx_ref,tok_ref,og_ref,scale_ref,wo_ref,late_ref,bias_ref,gain_ref,shift_ref,
                res_ref,dres_ref,do_ref,sums_ref,bsum_ref,grad_ref,
                u1_ref,r1_ref,low_ref,acc_ref,pre_ref,gated_ref,gp_ref,dfeed_ref,stage_ref,tail_ref,datt_ref,sem):
    step=pl.program_id(0)
    width=per*rows_in
    CH=64
    def chunks(f):
        def body(i,c):
            f(pl.ds(pl.multiple_of(i*CH,CH),CH))
            return c
        lax.fori_loop(0,R//CH,body,0)
    mean=lambda x: jnp.mean(x,axis=1,keepdims=True)
    gain=lambda i: gain_ref[i:i+1,:]
    shift=lambda i: shift_ref[i:i+1,:]
    def add_sum(i,x):
        sums_ref[i:i+1,:]+=jnp.sum(x,axis=0,keepdims=True)
    @pl.when(step==0)
    def _():
        sums_ref[...]=jnp.zeros_like(sums_ref)
        acc_ref[...]=dot_nn(ctx_ref[...],wo_ref[...])
        def norm(at):
            v=tok_ref[at,:].astype(f32)+acc_ref[at,:]+shift(0)
            c=v-mean(v)
            r=lax.rsqrt(mean(c*c)+EPS)
            u=c*r
            u1_ref[at,:]=u
            r1_ref[at,:]=jnp.broadcast_to(r,(CH,128))
            h=u*gain(0)+shift(1)
            low_ref[at,:]=h.astype(bf)
            acc_ref[at,:]=h+shift(2)
        chunks(norm)
    w_in=late_ref[:,0:rows_in,:].reshape(width,D)
    w_outer=late_ref[:,rows_in:2*rows_in,:].reshape(width,D)
    @pl.when(step<tiles)
    def _():
        pre_ref[...]=dot_nt(low_ref[...],w_in)
        def act(at):
            g,gp=gelu_parts(pre_ref[at,:]+bias_ref[0])
            gated_ref[step,at,:]=g.astype(bf)
            gp_ref[step,at,:]=gp.astype(bf)
        chunks(act)
        acc_ref[...]+=dot_nn(gated_ref[step],w_outer)
    @pl.when(step==tiles-1)
    def _():
        def norm(at):
            v=acc_ref[at,:]
            c=v-mean(v)
            r=lax.rsqrt(mean(c*c)+EPS)
            u=c*r
            res_ref[at,:]=(u*gain(1)+shift(3)).astype(bf)
            top=og_ref[at,:].astype(f32)
            add_sum(1,top*u)
            add_sum(5,top)
            e=top*gain(1)
            d=(e-mean(e)-u*mean(e*u))*r
            add_sum(4,d)
            dfeed_ref[at,:]=d.astype(bf)
            acc_ref[at,:]=d
        chunks(norm)
    @pl.when(step>=tiles)
    def _():
        k=step-tiles
        slot=lax.rem(k,2)
        pre_ref[...]=dot_nt(dfeed_ref[...],w_outer)
        def act(at):
            d=(pre_ref[at,:]*gp_ref[k,at,:].astype(f32)).astype(bf)
            gp_ref[k,at,:]=d
        chunks(act)
        bsum_ref[0]=jnp.sum(gp_ref[k].astype(f32),axis=0,keepdims=True)
        def out(kk,s):
            return pltpu.make_async_copy(stage_ref.at[s],grad_ref.at[pl.ds(kk*per,per),pl.ds(0,2*rows_in)],sem.at[s])
        @pl.when(k>=2)
        def _():
            out(k-2,slot).wait()
        stage_ref[slot,:,0:rows_in,:]=dot_tn(gp_ref[k],low_ref[...]).astype(bf).reshape(per,rows_in,D)
        stage_ref[slot,:,rows_in:2*rows_in,:]=dot_tn(gated_ref[k],dfeed_ref[...]).astype(bf).reshape(per,rows_in,D)
        out(k,slot).start()
        acc_ref[...]+=dot_nn(gp_ref[k],w_in)
        @pl.when(k==tiles-1)
        def _():
            def norm(at):
                d=acc_ref[at,:]
                u=u1_ref[at,:]
                r=r1_ref[at,0:1]
                add_sum(0,d*u)
                add_sum(3,d)
                e=d*gain(0)
                g=(e-mean(e)-u*mean(e*u))*r
                add_sum(2,g)
                dres_ref[at,:]=g
                datt_ref[at,:]=g.astype(bf)
            chunks(norm)
            do_ref[...]=(dot_nt(datt_ref[...],wo_ref[...])*scale_ref[...]).astype(bf)
            outer=dot_tn(ctx_ref[...],datt_ref[...])
            n=D//own_rows
            gap=tail_ref.shape[1]-own_rows
            for p in range(n):
                piece=outer[p*own_rows:p*own_rows+own_rows,:]
                if gap:
                    piece=jnp.concatenate([piece,jnp.zeros((gap,D),f32)],axis=0)
                tail_ref[p]=piece.astype(bf)
            last=pltpu.make_async_copy(tail_ref,grad_ref.at[:,pl.ds(2*rows_in,tail_ref.shape[1])],sem.at[2])
            last.start()
            if tiles>1:
                out(k-1,1-slot).wait()
            out(k,slot).wait()
            last.wait()

def feed(ctx,tokens,out_grad,scale,out_rows,late,bias,gain,shift,rows_in,own_rows,tiles=4):
    R,D=ctx.shape
    n,rows_late,_=late.shape
    per=n//tiles
    width=per*rows_in
    tail=rows_late-2*rows_in
    vm=lambda s: pl.BlockSpec(s,lambda i: (0,)*len(s))
    return pl.pallas_call(functools.partial(feed_kernel,R,D,tiles,per,rows_in,own_rows),
        grid=(2*tiles,),
        in_specs=[vm((R,D)),vm((R,D)),vm((R,D)),vm((R,D)),vm((D,D)),
                  pl.BlockSpec((per,rows_late,D),lambda i:(lax.rem(i,tiles),0,0)),
                  pl.BlockSpec((1,1,width),lambda i:(lax.rem(i,tiles),0,0)),vm((2,D)),vm((4,D))],
        out_specs=[vm((R,D)),vm((R,D)),vm((R,D)),vm((8,D)),pl.BlockSpec((1,1,width),lambda i:(jnp.maximum(i-tiles,0),0,0)),
                   pl.BlockSpec(memory_space=pl.ANY)],
        out_shape=[jax.ShapeDtypeStruct((R,D),bf),jax.ShapeDtypeStruct((R,D),f32),jax.ShapeDtypeStruct((R,D),bf),
                   jax.ShapeDtypeStruct((8,D),f32),jax.ShapeDtypeStruct((tiles,1,width),f32),
                   jax.ShapeDtypeStruct((n,rows_late,D),bf)],
        scratch_shapes=[pltpu.VMEM((R,D),f32),pltpu.VMEM((R,128),f32),pltpu.VMEM((R,D),bf),pltpu.VMEM((R,D),f32),
                        pltpu.VMEM((R,width),f32),pltpu.VMEM((tiles,R,width),bf),pltpu.VMEM((tiles,R,width),bf),
                        pltpu.VMEM((R,D),bf),pltpu.VMEM((2,per,2*rows_in,D),bf),pltpu.VMEM((n,tail,D),bf),pltpu.VMEM((R,D),bf),
                        pltpu.SemaphoreType.DMA((3,))],
        compiler_params=pltpu.CompilerParams(vmem_limit_bytes=58*1024*1024,dimension_semantics=("arbitrary",)),
        cost_estimate=pl.CostEstimate(flops=2*R*D*n*rows_in*6+6*R*D*D,bytes_accessed=4*n*rows_late*D+20*R*D,transcendentals=2*R*n*rows_in),
        name="feed",
    )(ctx,tokens,out_grad,scale,out_rows,late,bias,gain,shift)

MESH = pl.DeviceIdType.MESH
ANY = pl.BlockSpec(memory_space=pl.ANY)
VM = pl.BlockSpec(memory_space=pltpu.VMEM)

def remote(src, dst, send, recv, peer):
    return pltpu.make_async_remote_copy(src_ref=src, dst_ref=dst, send_sem=send, recv_sem=recv,
                                        device_id=peer, device_id_type=MESH)

def meet(peers):
    barrier = pltpu.get_barrier_semaphore()
    for peer in peers:
        pl.semaphore_signal(barrier, inc=1, device_id=peer, device_id_type=MESH)
    pl.semaphore_wait(barrier, len(peers))

class Place:
    def __init__(self, n_t, n_dp):
        self.n_t, self.n_dp = n_t, n_dp
        bits = (n_dp // 2).bit_length() - 1
        self.low = bits // 2
        self.high = bits - self.low
        dp, self.t = lax.axis_index("dp"), lax.axis_index("tensor")
        self.core = dp % 2
        self.down = (dp // 2) % 2**self.low
        self.up = dp // 2 // 2**self.low
        self.others = [lax.rem(self.t + 1 + i, n_t) for i in range(n_t - 1)]
        self.twin = {"dp": dp - self.core + 1 - self.core}
        self.steps = [("down", i) for i in range(self.low)] + [("up", i) for i in range(self.high)]

    def bit(self, step):
        kind, i = step
        return (getattr(self, kind) // 2**i) % 2

    def peer(self, step):
        kind, i = step
        turn = (1 - 2 * self.bit(step)) * 2**i
        down = self.down + turn if kind == "down" else self.down
        up = self.up + turn if kind == "up" else self.up
        return {"dp": (up * 2**self.low + down) * 2 + self.core}

    def peers(self):
        return [{"tensor": o} for o in self.others] + [self.twin] + [self.peer(s) for s in self.steps]

    def orders(self):
        down = [s for s in self.steps if s[0] == "down"]
        up = [s for s in self.steps if s[0] == "up"]
        return [down + up, up + down]

    def spans(self, done):
        out = []
        for kind in ("up", "down"):
            n = sum(1 for s in done if s[0] == kind)
            here = getattr(self, kind)
            out.append(pl.ds((here // 2**n) * 2**n, 2**n))
        return out

    def parts(self):
        half = self.n_t // 2
        return [pl.ds(0, half), pl.ds(half, half)] if half else [pl.ds(0, 1)]

def lanes_of(count, width, shape, tall):
    wide_axis = 0 if tall else 1
    f = lax.broadcasted_iota(jnp.int32, shape, wide_axis)
    r = lax.broadcasted_iota(jnp.int32, shape, 1 - wide_axis)
    return jnp.where(f % count == r, 1.0, 0.0).astype(bf)

def spread_row(table, count, width, first):
    n = table.shape[0]
    full = dot_nn(table.astype(bf), lanes_of(count, width, (128, width), False))
    p = lax.broadcasted_iota(jnp.int32, (n, width), 0)
    f = lax.broadcasted_iota(jnp.int32, (n, width), 1)
    return jnp.sum(jnp.where(first + f // count == p, full, 0.0), axis=0, keepdims=True)

def fold_row(row, count, n, first):
    width = row.shape[1]
    p = lax.broadcasted_iota(jnp.int32, (n, width), 0)
    f = lax.broadcasted_iota(jnp.int32, (n, width), 1)
    full = jnp.where(first + f // count == p, jnp.broadcast_to(row, (n, width)), 0.0)
    return dot_nn(full.astype(bf), lanes_of(count, width, (width, 128), True))

def eight(n):
    return -(-n // 8) * 8

def begin_kernel(n_t, n_dp, own, part, cols, inner, tiles, L,
                 tok_ref, wq_ref, wk_ref, wv_ref, rel_ref, qkvb_ref, ffb_ref, gains_ref, shifts_ref, ahead_ref, back_ref,
                 q_out, k_out, v_out, krel_out, qrel_out, kt_out, qr_out, toks_out, w_out, ox_out, oy_out, table_out,
                 ibias_ref, gain_ref, shift_ref,
                 toks, packs, pack, packf, wf, w, kb, vb, qb, krel, qrel, kt, qr, table, tableb, miscf, ox, oy,
                 tok_send, tok_recv, z_send, z_recv, x_send, x_recv, out_sem):
    at = Place(n_t, n_dp)
    t = at.t
    R, D = tok_ref.shape
    W = L + R
    n_all = n_t * n_dp
    S, S2 = eight(own), eight(part)
    misc = 3 * S + S2
    right = {"tensor": lax.rem(t + 1, n_t)}

    packf[...] = jnp.zeros_like(packf)
    for i, ref in enumerate((wq_ref, wk_ref, wv_ref)):
        packf[i * S:i * S + own, :] = ref[...].astype(f32)
    for i in range(n_t):
        @pl.when(t == i)
        def _():
            packf[3 * S:3 * S + part, :] = rel_ref[...].astype(f32)[i * part:(i + 1) * part]
    for i in range(3):
        packf[misc:misc + 1, 128 * i:128 * i + own] = qkvb_ref[i:i + 1, :].astype(f32)
    packf[misc:misc + 1, 384:384 + inner] = ffb_ref[...].astype(f32)
    for i in range(2):
        packf[misc + 1:misc + 2, 128 * i:128 * i + cols] = gains_ref[i:i + 1, :].astype(f32)
    for i in range(4):
        packf[misc + 1:misc + 2, 256 + 128 * i:256 + 128 * i + cols] = shifts_ref[i:i + 1, :].astype(f32)
    pack[...] = packf[...].astype(bf)

    meet(at.peers())
    copies = []

    def go(copy):
        copy.start()
        copies.append(copy)
        return copy

    here = packs.at[t, at.up, at.down, at.core]
    ring = [go(remote(pack, here, z_send.at[i], z_recv.at[i], {"tensor": o})) for i, o in enumerate(at.others)]
    half = R // 2
    token = {}

    def send_token(s):
        b = lax.rem(t - s + n_t, n_t)
        src = tok_ref if s == 0 else toks.at[b]
        for j in range(2):
            if s:
                token[s - 1, j].wait_recv()
            rows = pl.ds(j * half, half)
            token[s, j] = go(remote(src.at[rows], toks.at[b, rows], tok_send.at[s, j], tok_recv.at[s, j], right))

    send_token(0)
    own_pack = pltpu.make_async_copy(pack, here, out_sem.at[0])
    own_pack.start()
    outs = []

    def put(src, dst):
        copy = pltpu.make_async_copy(src, dst, out_sem.at[1 + len(outs)])
        copy.start()
        outs.append(copy)

    def pick(line, start):
        rows = line[:, pl.ds(pl.multiple_of(start, 128), W)]
        ids = lax.broadcasted_iota(jnp.int32, (NB, W), 0)
        return jnp.where(ids == rows, 1.0, 0.0).astype(bf)

    ox[...] = pick(back_ref, L - R - R * t)
    oy[...] = pick(ahead_ref, L - R - R * t)
    put(ox, ox_out)
    put(oy, oy_out)

    for copy in ring:
        copy.wait_recv()
    own_pack.wait()
    parts, orders = at.parts(), at.orders()
    n_steps = len(at.steps)
    swaps = {}

    def swap(h, k):
        if k:
            swaps[h, k - 1].wait_recv()
        up, down = at.spans(orders[h][:k])
        if k < n_steps:
            piece, peer = packs.at[parts[h], up, down, at.core], at.peer(orders[h][k])
        else:
            piece, peer = packs.at[parts[h], :, :, at.core], at.twin
        swaps[h, k] = go(remote(piece, piece, x_send.at[h, k], x_recv.at[h, k], peer))

    hs = range(len(parts))
    sent = 1
    for k in range(n_steps + 1):
        for h in hs:
            swap(h, k)
        if k and sent < n_t - 1:
            send_token(sent)
            sent += 1
    for h in hs:
        swaps[h, n_steps].wait_recv()

    slots = [(a, u, d, c) for a in range(n_t) for u in range(2**at.high) for d in range(2**at.low) for c in range(2)]
    for i in range(3):
        for p, s in enumerate(slots):
            wf[p * own:p * own + own, :] = packs[s[0], s[1], s[2], s[3], i * S:i * S + own, :].astype(f32)
        w[i] = wf[...].astype(bf)
    put(w, w_out)
    for p, s in enumerate(slots):
        rows = packs[s[0], s[1], s[2], s[3], misc:misc + 8, :].astype(f32)
        miscf[0, p:p + 1, :] = rows[0:1]
        miscf[1, p:p + 1, :] = rows[1:2]
        a, dp = p // n_dp, p % n_dp
        to = dp * n_t * part + a * part
        table[to:to + part, :] = packs[s[0], s[1], s[2], s[3], 3 * S:3 * S + part, :].astype(f32)
    bias = [spread_row(miscf[0, :, 128 * i:128 * i + 128], own, D, 0) for i in range(3)]
    rel = table[...].astype(bf)
    tableb[...] = rel
    put(tableb, table_out)
    krel[...] = (dot_nt(rel, w[1]) + bias[1]).astype(bf)
    qrel[...] = (dot_nt(rel, w[0]) + bias[0]).astype(bf)
    put(krel, krel_out)
    put(qrel, qrel_out)
    kt[...] = dot_tn(ox[...], krel[...]).astype(bf)
    put(kt, kt_out)
    qr[...] = dot_tn(pick(back_ref, R * t), qrel[...]).astype(bf)
    put(qr, qr_out)
    while sent < n_t - 1:
        send_token(sent)
        sent += 1

    def project(tokens, i):
        return (dot_nt(tokens, w[i]) + bias[i]).astype(bf)

    qb[...] = project(tok_ref[...], 0)
    put(qb, q_out)
    width = n_all * inner // tiles
    for i in range(tiles):
        ibias_ref[i] = spread_row(miscf[0, :, 384:512], inner, width, i * (n_all // tiles))
    for i in range(2):
        gain_ref[i:i + 1, :] = spread_row(miscf[1, 0:n_dp, 128 * i:128 * i + 128], cols, D, 0)
    for i in range(4):
        shift_ref[i:i + 1, :] = spread_row(miscf[1, 0:n_dp, 256 + 128 * i:384 + 128 * i], cols, D, 0)

    for s in range(n_t):
        b = lax.rem(t - s + n_t, n_t)
        rows = pl.ds(pl.multiple_of(b * R, R), R)
        if s == n_t - 1:
            for j in range(2):
                token[s - 1, j].wait_recv()
        src = tok_ref if s == 0 else toks.at[b]
        put(src, toks_out.at[b])
        kb[s] = project(src[...], 1)
        put(kb.at[s], k_out.at[rows])
        vb[s] = project(src[...], 2)
        put(vb.at[s], v_out.at[rows])
    for copy in outs:
        copy.wait()
    for copy in copies:
        copy.wait_send()

def begin(tokens, w_query, w_key, w_value, rel_table, qkv_bias, ff_bias, gains, shifts, ahead, back, n_t, n_dp, tiles):
    R, D = tokens.shape
    L = ahead.shape[1] // 2
    W = L + R
    own, inner, cols = w_query.shape[0], ff_bias.shape[1], gains.shape[1]
    part = rel_table.shape[0] // n_t
    n_all = n_t * n_dp
    width = n_all * inner // tiles
    PR = -(-(3 * eight(own) + eight(part) + 8) // 16) * 16
    bits = (n_dp // 2).bit_length() - 1
    low = bits // 2
    S = jax.ShapeDtypeStruct
    big = [(R, D), (L, D), (L, D), (NB, D), (NB, D), (W, D), (W, D), (n_t, R, D), (3, D, D), (NB, W), (NB, W), (NB, D)]
    v = lambda s, t=bf: pltpu.VMEM(s, t)
    dma = lambda *s: pltpu.SemaphoreType.DMA(s)
    return pl.pallas_call(
        functools.partial(begin_kernel, n_t, n_dp, own, part, cols, inner, tiles, L),
        out_shape=[S(s, bf) for s in big] + [S((tiles, 1, width), f32), S((2, D), f32), S((4, D), f32)],
        in_specs=[VM] * 11, out_specs=[ANY] * len(big) + [VM] * 3,
        scratch_shapes=[v((n_t, R, D)), v((n_t, 2**(bits - low), 2**low, 2, PR, D)), v((PR, D)), v((PR, D), f32), v((D, D), f32),
                        v((3, D, D)), v((n_t, R, D)), v((n_t, R, D)), v((R, D)), v((NB, D)), v((NB, D)), v((W, D)), v((W, D)),
                        v((NB, D), f32), v((NB, D)), v((2, n_all, D), f32), v((NB, W)), v((NB, W)),
                        dma(n_t - 1, 2), dma(n_t - 1, 2), dma(n_t - 1), dma(n_t - 1), dma(2, bits + 1), dma(2, bits + 1),
                        dma(10 + 3 * n_t)],
        compiler_params=pltpu.CompilerParams(collective_id=0, has_side_effects=True, vmem_limit_bytes=58 * 1024 * 1024),
        name="begin",
    )(tokens, w_query, w_key, w_value, rel_table, qkv_bias, ff_bias, gains, shifts, ahead, back)

def finish_kernel(n_t, n_dp, own, rel_rows, cols, inner, tiles,
                  dq_in, dk_in, dv_in, tok_in, toks_in, w_in, table_in, dqr_in, dkr_in, dres_in, sums_ref, bsum_ref,
                  tg_ref, gq_ref, gk_ref, gv_ref, rel_ref, qkvb_ref, ffb_ref, gains_ref, shifts_ref,
                  dq, dk, dv, tok, toks, w, table, dqr, dkr, dres, g, relf, m0, m1, miscs, pack, first, acc, got, total,
                  tok_got, tok_acc, tok_own, base, *rest):
    at = Place(n_t, n_dp)
    t = at.t
    n_steps = len(at.steps)
    bufs, (in_sem, tok_send, tok_recv, x_send, x_recv, z_send, z_recv) = rest[:2 * n_steps], rest[2 * n_steps:]
    R, D = tok.shape
    L = n_t * R
    n_all = n_t * n_dp
    S, S3 = eight(own), eight(rel_rows)
    misc = 3 * S
    PR = pack.shape[4]
    right = {"tensor": lax.rem(t + 1, n_t)}
    loads = []

    def load(src, dst):
        copy = pltpu.make_async_copy(src, dst, in_sem.at[len(loads)])
        copy.start()
        loads.append(copy)
        return copy

    def block(s):
        return lax.rem(t - 1 - s + 2 * n_t, n_t)

    l_w = load(w_in, w)
    l_kv = []
    for s in range(n_t):
        b = block(s)
        l_kv.append((load(dk_in.at[b], dk.at[b]), load(dv_in.at[b], dv.at[b])))
    l_toks = load(toks_in, toks)
    l_rest = [load(tok_in, tok), load(dq_in, dq), load(table_in, table), load(dqr_in, dqr), load(dkr_in, dkr), load(dres_in, dres)]
    meet(at.peers())
    copies = []

    def go(copy):
        copy.start()
        copies.append(copy)
        return copy

    half = R // 2
    token = {}

    def partial(s):
        for copy in l_kv[s]:
            copy.wait()
        b = block(s)
        return dot_nn(dk[b], w[1]) + dot_nn(dv[b], w[2])

    def send_token(s):
        for j in range(2):
            rows = pl.ds(j * half, half)
            if s:
                token[s - 1, j].wait_recv()
                tok_acc[s, rows] = (tok_own[rows].astype(f32) + tok_got[s - 1, rows].astype(f32)).astype(bf)
            token[s, j] = go(remote(tok_acc.at[s, rows], tok_got.at[s, rows], tok_send.at[s, j], tok_recv.at[s, j], right))

    l_w.wait()
    tok_acc[0] = partial(0).astype(bf)
    send_token(0)
    blocks = [None] * n_t
    tok_own[...] = partial(1).astype(bf)

    for s in range(2, n_t):
        for copy in l_kv[s]:
            copy.wait()
    l_kv = [()] * n_t
    l_toks.wait()
    for copy in l_rest:
        copy.wait()
    dqb, dkb = dqr[...].astype(bf), dkr[...].astype(bf)
    rel_table = table[...]
    g[0] = dot_tn(dq[...], tok[...]) + dot_tn(dqb, rel_table)
    g[1] = dot_tn(dk[...].reshape(L, D), toks[...].reshape(L, D)) + dot_tn(dkb, rel_table)
    g[2] = dot_tn(dv[...].reshape(L, D), toks[...].reshape(L, D))
    relf[...] = dot_nn(dqb, w[0]) + dot_nn(dkb, w[1])
    ones = lambda n: jnp.ones((8, n), bf)
    columns = [dot_nn(ones(R), dq[...])[0:1] + jnp.sum(dqr[...], axis=0, keepdims=True),
               dot_nn(ones(L), dk[...].reshape(L, D))[0:1] + jnp.sum(dkr[...], axis=0, keepdims=True),
               dot_nn(ones(L), dv[...].reshape(L, D))[0:1]]
    for i in range(3):
        m0[:, 128 * i:128 * i + 128] = fold_row(columns[i], own, n_all, 0)
    units = jnp.zeros((n_all, 128), f32)
    for i in range(tiles):
        units += fold_row(bsum_ref[i], inner, n_all, i * (n_all // tiles))
    m0[:, 384:512] = units
    for i in range(6):
        m1[:, 128 * i:128 * i + 128] = fold_row(sums_ref[i:i + 1, :], cols, n_dp, 0)
    miscs[...] = jnp.zeros_like(miscs)
    slots = [(a, u, d, c) for a in range(n_t) for u in range(2**at.high) for d in range(2**at.low) for c in range(2)]

    def padded(x, n):
        return jnp.concatenate([x, jnp.zeros((n - x.shape[0], D), f32)], axis=0) if n > x.shape[0] else x

    for p, s in enumerate(slots):
        dp = p % n_dp
        miscs[8 * p:8 * p + 1, 0:512] = m0[p:p + 1, :]
        miscs[8 * p + 1:8 * p + 2, :] = m1[dp:dp + 1, :]
        pieces = [padded(g[i, p * own:p * own + own, :], S) for i in range(3)]
        pieces += [miscs[8 * p:8 * p + 8, :], padded(relf[dp * rel_rows:dp * rel_rows + rel_rows, :], S3)]
        whole = padded(jnp.concatenate(pieces, axis=0), PR)
        pack[s[0], s[1], s[2], s[3]] = whole.astype(bf)

    parts = at.parts()
    hs = range(len(parts))
    per = n_t // len(parts)
    orders = [list(reversed(o)) for o in at.orders()][:len(parts)]
    swaps = {}
    left = {h: {"up": at.high, "down": at.low} for h in hs}

    def region(h, cut=None):
        out = []
        for kind in ("up", "down"):
            n = left[h][kind]
            here = getattr(at, kind)
            if cut is not None and cut[0] == kind:
                start = (here // 2**n) * 2**n + (1 - at.bit(cut)) * 2**(n - 1)
                out.append((start, 2**(n - 1)))
            else:
                out.append(((here // 2**n) * 2**n, 2**n))
        return out

    def start(h, k):
        if k == 0:
            src, dst, peer = pack.at[parts[h], :, :, 1 - at.core], first.at[parts[h]], at.twin
        else:
            cut = orders[h][k - 1]
            up, down = [pl.ds(*x) for x in region(h, cut)]
            src, dst, peer = acc.at[parts[h], up, down], bufs[h * n_steps + k - 1], at.peer(cut)
        swaps[h, k] = go(remote(src, dst, x_send.at[h, k], x_recv.at[h, k], peer))

    def absorb(h, k):
        swaps[h, k].wait_recv()
        if k:
            left[h][orders[h][k - 1][0]] -= 1
        (u0, nu), (d0, nd) = region(h)
        buf = first if k == 0 else bufs[h * n_steps + k - 1]

        @pl.loop(0, per * nu * nd)
        def _(m):
            a, u, d = m // (nu * nd), m // nd % nu, m % nd
            if k == 0:
                x, y = pack[h * per + a, u, d, at.core], buf[h * per + a, u, d]
            else:
                x, y = acc[h * per + a, u0 + u, d0 + d], buf[a, u, d]
            acc[h * per + a, u0 + u, d0 + d] = (x.astype(f32) + y.astype(f32)).astype(bf)

    for h in hs:
        start(h, 0)
    sent = 1
    if n_t > 2:
        send_token(1)
        sent = 2
        tok_own[...] = partial(2).astype(bf)
    base[...] = partial(n_t - 1) + dres[...] + dot_nn(dq[...], w[0])
    for k in range(n_steps + 1):
        for h in hs:
            absorb(h, k)
            if k < n_steps:
                start(h, k + 1)
        if k == n_steps:
            ring = [go(remote(acc.at[o, at.up, at.down], got.at[i], z_send.at[i], z_recv.at[i], {"tensor": o}))
                    for i, o in enumerate(at.others)]
        if k and sent < n_t - 1:
            send_token(sent)
            sent += 1
            if sent < n_t - 1:
                tok_own[...] = partial(sent).astype(bf)
    for copy in ring:
        copy.wait_recv()
    total[...] = acc[t, at.up, at.down].astype(f32)
    for i in range(n_t - 1):
        total[...] += got[i].astype(f32)
    for i, ref in enumerate((gq_ref, gk_ref, gv_ref)):
        ref[...] = total[i * S:i * S + own, :]
    rel_ref[...] = total[misc + 8:misc + 8 + rel_rows, :]
    for i in range(3):
        qkvb_ref[i:i + 1, :] = total[misc:misc + 1, 128 * i:128 * i + own]
    ffb_ref[...] = total[misc:misc + 1, 384:384 + inner]
    for i in range(2):
        gains_ref[i:i + 1, :] = total[misc + 1:misc + 2, 128 * i:128 * i + cols]
    for i in range(4):
        shifts_ref[i:i + 1, :] = total[misc + 1:misc + 2, 256 + 128 * i:256 + 128 * i + cols]
    while sent < n_t - 1:
        send_token(sent)
        sent += 1
        if sent < n_t - 1:
            tok_own[...] = partial(sent).astype(bf)
    for j in range(2):
        rows = pl.ds(j * half, half)
        token[n_t - 2, j].wait_recv()
        tg_ref[rows, :] = base[rows, :] + tok_got[n_t - 2, rows].astype(f32)
    for copy in copies:
        copy.wait_send()

def finish(dq, dk, dv, tok, toks, w, table, dqr, dkr, dres, sums, bsum, own, rel_rows, cols, inner, n_t, n_dp):
    R, D = tok.shape
    L = n_t * R
    n_all = n_t * n_dp
    tiles = bsum.shape[0]
    S3 = eight(rel_rows)
    PR = -(-(3 * eight(own) + 8 + S3) // 16) * 16
    bits = (n_dp // 2).bit_length() - 1
    low = bits // 2
    high = bits - low
    per = n_t // 2
    v = lambda s, x=bf: pltpu.VMEM(s, x)
    dma = lambda *s: pltpu.SemaphoreType.DMA(s)
    bufs = []
    for order in ([("up", high), ("down", low)], [("down", low), ("up", high)]):
        left = {"up": high, "down": low}
        for kind, n in order:
            for _ in range(n):
                left[kind] -= 1
                bufs.append(v((per, 2**left["up"], 2**left["down"], PR, D)))
    S = jax.ShapeDtypeStruct
    outs = [(R, D), (own, D), (own, D), (own, D), (rel_rows, D), (3, own), (1, inner), (2, cols), (4, cols)]
    blocks = lambda x: x.reshape(n_t, R, D)
    return pl.pallas_call(
        functools.partial(finish_kernel, n_t, n_dp, own, rel_rows, cols, inner, tiles),
        out_shape=[S(s, f32) for s in outs],
        in_specs=[ANY] * 10 + [VM] * 2, out_specs=[VM] * len(outs),
        scratch_shapes=[v((R, D)), v((n_t, R, D)), v((n_t, R, D)), v((R, D)), v((n_t, R, D)), v((3, D, D)), v((NB, D)),
                        v((NB, D), f32), v((NB, D), f32), v((R, D), f32), v((3, D, D), f32), v((NB, D), f32),
                        v((n_all, 512), f32), v((n_dp, D), f32), v((8 * n_all, D), f32),
                        v((n_t, 2**high, 2**low, 2, PR, D)), v((n_t, 2**high, 2**low, PR, D)), v((n_t, 2**high, 2**low, PR, D)),
                        v((n_t - 1, PR, D)), v((PR, D), f32),
                        v((n_t - 1, R, D)), v((n_t - 1, R, D)), v((R, D)), v((R, D), f32)] + bufs
                       + [dma(2 * n_t + 8), dma(n_t - 1, 2), dma(n_t - 1, 2), dma(2, bits + 1), dma(2, bits + 1), dma(n_t - 1), dma(n_t - 1)],
        compiler_params=pltpu.CompilerParams(collective_id=1, has_side_effects=True, vmem_limit_bytes=60 * 1024 * 1024),
        name="finish",
    )(dq, blocks(dk), blocks(dv), tok, blocks(toks), w, table, dqr, dkr, dres, sums, bsum)

GROUPS, TILES = 32, 4
ALL=("tensor","dp")

def finish_plain(dq, dk, dv, tok, toks, w, table, dqr, dkr, dres, sums, bsum, own, rel_rows, cols, inner, n_t, n_dp):
    times = lambda s, a, b: jnp.einsum(s, a.astype(bf), b.astype(bf), preferred_element_type=f32)
    scatter = lambda x: lax.psum_scatter(x, ALL, scatter_dimension=0, tiled=True)
    grads = [times("tf,td->fd", dq, tok) + times("tf,td->fd", dqr, table),
             times("tf,td->fd", dk, toks) + times("tf,td->fd", dkr, table), times("tf,td->fd", dv, toks)]
    rel = times("bf,fd->bd", dqr, w[0]) + times("bf,fd->bd", dkr, w[1])
    spread = (times("tf,fd->td", dk, w[1]) + times("tf,fd->td", dv, w[2])).astype(bf)
    back_sum = lax.psum_scatter(spread, "tensor", scatter_dimension=0, tiled=True).astype(f32)
    tokens_grad = dres + times("tf,fd->td", dq, w[0]) + back_sum
    column = lambda x: jnp.sum(x.astype(f32), axis=0)
    bias = jnp.stack([column(dq) + column(dqr), column(dk) + column(dkr), column(dv)])
    every = lambda x: lax.psum(x, ALL)
    dp = lax.axis_index("dp")
    place = lax.axis_index("tensor") * n_dp + dp
    cut = lambda x, i, n: lax.dynamic_slice_in_dim(x, i * n, n, 1)
    rel = lax.dynamic_slice_in_dim(every(rel), dp * rel_rows, rel_rows, 0)
    return [tokens_grad] + [scatter(x) for x in grads] + [rel, cut(every(bias), place, own), cut(every(bsum.reshape(1, -1)), place, inner),
            cut(every(sums[:2]), dp, cols), cut(every(sums[2:6]), dp, cols)]

def local(tokens, w_query, w_key, w_value, w_out, qkv_bias, w_ff_in, w_ff_out, ff_bias, rel_table,
          gains, shifts, rel_bucket, lengths, out_grad):
    D = tokens.shape[1]
    n_t, n_dp = lax.axis_size("tensor"), lax.axis_size("dp")
    n_all = n_t * n_dp
    t = lax.axis_index("tensor")
    R = tokens.shape[0]
    L = (rel_bucket.shape[0] + 1) // 2
    W = L + R
    own_rows, cols, inner = w_query.shape[0], gains.shape[1], ff_bias.shape[0]
    none = jnp.full((1,), -1, jnp.int32)
    ahead = jnp.concatenate([rel_bucket, none])[None]
    back = jnp.concatenate([rel_bucket[::-1], none])[None]
    (query, key, value, key_rel, query_rel, key_table, query_table, gathered, weights, pick_x, pick_y, table,
     inner_bias, gain, shift) = begin(tokens, w_query, w_key, w_value, rel_table, qkv_bias, ff_bias.reshape(1, -1), gains, shifts,
                                      ahead, back, n_t, n_dp, TILES)
    gathered = gathered.reshape(L, D)
    late_rows = w_ff_in.shape[0]
    even = late_rows % 16 == 0 and own_rows % 8 == 0
    late = jnp.concatenate([w_ff_in, w_ff_out, w_out], axis=0)
    late_own = late.shape[0]
    late = jnp.pad(late, ((0, -late_own % 16), (0, 0)))
    late_all = lax.all_gather(late, ALL, axis=0, tiled=False)
    cut = lambda x, at, n: x[:, at:at + n].reshape(n_all * n, D)
    out_rows = cut(late_all, 2 * late_rows, own_rows)
    groups = n_all if even else GROUPS
    group_rows, group_own = n_all * late_rows // groups, D // groups
    if not even:
        sections = [cut(late_all, 0, late_rows), cut(late_all, late_rows, late_rows)]
        late_all = jnp.concatenate([x.reshape(groups, group_rows, D) for x in sections]
                                   + [jnp.zeros((groups, -(-group_own // 16) * 16, D), bf)], axis=1)
    mask = jnp.where(jnp.arange(L, dtype=jnp.int32) < lengths[0], 0.0, -1e9).astype(bf)
    mask = jnp.broadcast_to(mask[:, None], (L, 128))

    context, scale, shares = attention_forward(query, key, value, key_table, query_table, mask)
    layer_result_rows, d_resid_one, d_scaled, sums, bias_sums, late_grad = feed(
        context, tokens, out_grad, scale, out_rows, late_all, inner_bias, gain, shift, group_rows, group_own)
    d_query, d_key, d_value, d_key_rel, d_query_rel = attention_backward(
        query, key, value, d_scaled, context, shares, key_rel, query_rel, pick_x, pick_y)

    parted = lambda x: x.astype(bf).reshape(n_all, -1, D)
    if not even:
        late_grad = jnp.concatenate([
            parted(late_grad[:, :group_rows]), parted(late_grad[:, group_rows:2 * group_rows]),
            parted(late_grad[:, 2 * group_rows:2 * group_rows + group_own]),
            jnp.zeros((n_all, late.shape[0] - late_own, D), bf)], axis=1)
    late_sum = lax.psum_scatter(late_grad, ALL, scatter_dimension=0, tiled=True)[0].astype(f32)
    g_inner, g_outer, g_out = late_sum[:late_rows], late_sum[late_rows:2 * late_rows], late_sum[2 * late_rows:late_own]
    ends = (d_query, d_key, d_value, tokens, gathered, weights, table, d_query_rel, d_key_rel, d_resid_one, sums, bias_sums)
    rel_rows = rel_table.shape[0]
    finished = (finish if even else finish_plain)(*ends, own_rows, rel_rows, cols, inner, n_t, n_dp)
    tokens_grad, g_query, g_key, g_value, g_rel, g_qkv_bias, g_ff_bias, g_gains, g_shifts = finished
    return (layer_result_rows, tokens_grad, g_query, g_key, g_value, g_out,
            g_qkv_bias, g_inner, g_outer, g_ff_bias.reshape(inner), g_rel, g_gains, g_shifts)

def solution(mesh):
    rows, params = P(("dp", "tensor"), None), P(ALL, None)
    return jax.shard_map(
        local, mesh=mesh,
        in_specs=(rows, params, params, params, params, P(None, ALL), params, params, P(ALL), P("dp", None),
                  P(None, "dp"), P(None, "dp"), P(), P("dp"), rows),
        out_specs=(rows, rows, params, params, params, params, P(None, ALL), params, params, P(ALL), P("dp", None),
                   P(None, "dp"), P(None, "dp")),
        check_vma=False)
```

```python
import functools
import math

import jax
import jax.numpy as jnp
from jax import lax
from jax.experimental import pallas as pl
from jax.experimental.pallas import tpu as pltpu
from jax.sharding import PartitionSpec as P

bf = jnp.bfloat16
f32 = jnp.float32
DH=64; NB=256
SCALE=1.0/math.sqrt(3*DH)
LOG2E=math.log2(math.e)

def dot_nt(a,b):
    return lax.dot_general(a,b,(((1,),(1,)),((),())),preferred_element_type=f32)
def dot_nn(a,b):
    return lax.dot_general(a,b,(((1,),(0,)),((),())),preferred_element_type=f32)
def dot_tn(a,b):
    return lax.dot_general(a,b,(((0,),(0,)),((),())),preferred_element_type=f32)

def flip_matrix(n):
    a=lax.broadcasted_iota(jnp.int32,(n,n),0); b=lax.broadcasted_iota(jnp.int32,(n,n),1)
    return jnp.where(a+b==n-1,1.0,0.0).astype(bf)

def flip_rows(x):
    n,w=x.shape
    idx=7-lax.broadcasted_iota(jnp.int32,(8,w),0)
    return jnp.concatenate([jnp.take_along_axis(x[n-8-8*g:n-8*g],idx,axis=0) for g in range(n//8)],axis=0)

def fwd_kernel(R,L,B,C,mask_ref,q_ref,k_ref,v_ref,kt_ref,qr_ref,ctx_ref,scale_ref,e_ref,yt_ref,acc_ref,km_ref,y_ref,s_ref,x_ref,p_ref):
    hh=pl.program_id(1)
    lane=lambda n: lax.broadcasted_iota(jnp.int32,(n,128),1)
    def lanes(n): return (lane(n)//DH)==hh
    zero,one=jnp.zeros((),bf),jnp.ones((),bf)
    spare=(1-hh)*DH
    for i in range(L//C):
        at=slice(i*C,i*C+C)
        km_ref[at,:]=jnp.where(lane(C)==spare,mask_ref[at,:],k_ref[at,:])
    def yblock(i):
        at=slice(i*C,i*C+C)
        us=L-C-i*C
        kb=jnp.where(lanes(C),k_ref[at,:],zero)
        y=y_ref.at[i%2]
        y[...]=dot_nt(kb,qr_ref[us:us+R+C,:])
        for g in range(C//16):
            rows=slice(16*g,16*g+16)
            part=y[rows,:].astype(bf)
            s_part=pltpu.roll(part,R+1+16*g,1,stride=1,stride_axis=0)[:,:R]
            yt_ref[i%2,rows,:]=s_part
        return yt_ref[i%2].T
    for i in range(L//C):
        acc_ref[:,i*C:i*C+C]=yblock(i)
    v_one=jnp.where(lanes(L),v_ref[...],one)
    own=lanes(B)
    sp=lane(B)==spare
    accs=[]
    for i in range(R//B):
        r0=i*B
        qm=q_ref[r0:r0+B,:]
        q=jnp.where(own,qm,zero)
        qs=jnp.where(sp,one,q)
        ws=R-B-r0
        x,s=x_ref.at[i%2],s_ref.at[i%2]
        x[...]=dot_nt(q,kt_ref[ws:ws+L+B,:])
        s[...]=dot_nt(qs,km_ref[...])
        rr=R-B-r0
        p=p_ref.at[i%2]
        for g in range(B//16):
            rows=slice(16*g,16*g+16)
            xr=pltpu.roll(x[rows,:],(L+1+16*g)%(L+B),1,stride=1,stride_axis=0)[:,:L]
            raw=s[rows,:]+xr+acc_ref[r0+16*g:r0+16*g+16,:].astype(f32)
            s[rows,:]=raw
            top=raw[:,:128]
            for j in range(1,L//128):
                top=jnp.maximum(top,raw[:,128*j:128*j+128])
            p[rows,:]=top
        p[...]=jnp.broadcast_to(jnp.max(p[...],axis=1,keepdims=True)*(SCALE*LOG2E),(B,128))
        for g in range(B//16):
            rows=slice(16*g,16*g+16)
            peak=jnp.concatenate([p[rows,:]]*(L//128),axis=1)
            e=jnp.exp2(s[rows,:]*(SCALE*LOG2E)-peak)
            e=flip_rows(e).astype(bf)
            to=rr+B-16-16*g
            e_ref[0,to:to+16,:]=e
        accs.append(dot_nn(e_ref[0,rr:rr+B,:],v_one))
    acc=jnp.concatenate(accs[::-1],axis=0)
    inv=1.0/pltpu.roll(acc,DH,1)
    J=flip_matrix(R)
    ctx=dot_nn(J,(acc*inv).astype(bf)).astype(bf)
    mine=lanes(R)
    inv_hi=inv.astype(bf)
    sc=dot_nn(J,inv_hi)+dot_nn(J,(inv-inv_hi.astype(f32)).astype(bf))
    sc=sc*SCALE
    @pl.when(hh==0)
    def _():
        ctx_ref[...]=ctx
        scale_ref[...]=sc
    @pl.when(hh==1)
    def _():
        ctx_ref[...]=jnp.where(mine,ctx,ctx_ref[...])
        scale_ref[...]=jnp.where(mine,sc,scale_ref[...])

def attention_forward(q,k,v,kt,qr,mask,B=128,C=256):
    R,F=q.shape; L=k.shape[0]; W=L+R; pairs=F//128
    B=min(B,R)
    col=lambda n: pl.BlockSpec((n,128),lambda p,h:(0,p))
    flops=2*pairs*2*R*L*128*4
    return pl.pallas_call(functools.partial(fwd_kernel,R,L,B,C),
        grid=(pairs,2),
        in_specs=[pl.BlockSpec((L,128),lambda p,h:(0,0)),col(R),col(L),col(L),col(W),col(W)],
        out_specs=[col(R),col(R),pl.BlockSpec((1,R,L),lambda p,h:(2*p+h,0,0))],
        out_shape=[jax.ShapeDtypeStruct((R,F),bf),jax.ShapeDtypeStruct((R,F),f32),jax.ShapeDtypeStruct((2*pairs,R,L),bf)],
        scratch_shapes=[pltpu.VMEM((2,C,R),bf),pltpu.VMEM((R,L),bf),pltpu.VMEM((L,128),bf),pltpu.VMEM((2,C,R+C),f32),
                        pltpu.VMEM((2,B,L),f32),pltpu.VMEM((2,B,L+B),f32),pltpu.VMEM((2,B,128),f32)],
        compiler_params=pltpu.CompilerParams(vmem_limit_bytes=48*1024*1024,dimension_semantics=("arbitrary","arbitrary")),
        cost_estimate=pl.CostEstimate(flops=flops,bytes_accessed=2*pairs*R*L*2+10*L*F,transcendentals=2*pairs*R*L),
        name="attend",
    )(mask,q,k,v,kt,qr)

def bwd_kernel(R,L,B,C,q_ref,k_ref,v_ref,do_ref,ctx_ref,e_ref,kr_ref,qrel_ref,ox_ref,oy_ref,
               dq_ref,dk_ref,dv_ref,dkr_ref,dqr_ref,ds_ref,dor_ref,qrev_ref,dqa_ref,dka_ref,dva_ref,
               delta_ref,dp_ref,wide_ref,dst_ref,wide2_ref):
    hh=pl.program_id(1)
    def lanes(n): return (lax.broadcasted_iota(jnp.int32,(n,128),1)//DH)==hh
    zero=jnp.zeros((),bf)
    @pl.when(hh==0)
    def _():
        dqa_ref[...]=jnp.zeros_like(dqa_ref)
        dka_ref[...]=jnp.zeros_like(dka_ref)
        dva_ref[...]=jnp.zeros_like(dva_ref)
        dkr_ref[...]=jnp.zeros_like(dkr_ref)
        dqr_ref[...]=jnp.zeros_like(dqr_ref)
    J=flip_matrix(R)
    do=jnp.where(lanes(R),dot_nn(J,do_ref[...]).astype(bf),zero)
    ctx=dot_nn(J,ctx_ref[...])
    dor_ref[...]=do
    qrev_ref[...]=jnp.where(lanes(R),dot_nn(J,q_ref[...]).astype(bf),zero)
    delta_ref[...]=jnp.broadcast_to(jnp.sum(do.astype(f32)*ctx,axis=1,keepdims=True),(R,128))
    own=lanes(B)
    for i in range(R//B):
        r0=i*B
        dp,wide=dp_ref.at[i%2],wide_ref.at[i%2]
        dp[...]=dot_nt(dor_ref[r0:r0+B,:],v_ref[...])
        for g in range(B//16):
            rows=slice(16*g,16*g+16)
            at=slice(r0+16*g,r0+16*g+16)
            delta=jnp.concatenate([delta_ref[at,:]]*(L//128),axis=1)
            ds=(e_ref[0,at,:].astype(f32)*(dp[rows,:]-delta)).astype(bf)
            ds_ref[at,:]=ds
            part=jnp.concatenate([ds,jnp.zeros((16,B),bf)],axis=1)
            wide[rows,:]=pltpu.roll(part,16*g,1,stride=1,stride_axis=0)
        db=dot_nn(wide[...],ox_ref[r0:r0+L+B,:]).astype(bf)
        dq=dot_nn(ds_ref[r0:r0+B,:],k_ref[...])+dot_nn(db,kr_ref[...])
        dqa_ref[r0:r0+B,:]=jnp.where(own,dq,dqa_ref[r0:r0+B,:])
        dkr_ref[...]+=dot_tn(db,qrev_ref[r0:r0+B,:])
    ownk=lanes(C)
    qrel=jnp.where(lanes(NB),qrel_ref[...],zero)
    for i in range(L//C):
        at=slice(i*C,i*C+C)
        dst,wide=dst_ref.at[i%2],wide2_ref.at[i%2]
        dst[...]=ds_ref[:,at].T
        for g in range(C//16):
            rows=slice(16*g,16*g+16)
            part=jnp.concatenate([dst[rows,:],jnp.zeros((16,C),bf)],axis=1)
            wide[rows,:]=pltpu.roll(part,16*g,1,stride=1,stride_axis=0)
        db=dot_nn(wide[...],oy_ref[i*C:i*C+R+C,:]).astype(bf)
        dka_ref[at,:]+=dot_nn(dst[...],qrev_ref[...])+dot_nn(db,qrel)
        dva_ref[at,:]+=dot_tn(e_ref[0,:,at],dor_ref[...])
        kb=jnp.where(ownk,k_ref[at,:],zero)
        dqr_ref[...]+=dot_tn(db,kb)
    @pl.when(hh==1)
    def _():
        dq_ref[...]=dot_nn(J,dqa_ref[...].astype(bf)).astype(bf)
        dk_ref[...]=dka_ref[...].astype(bf)
        dv_ref[...]=(dva_ref[...]*(1.0/SCALE)).astype(bf)

def attention_backward(q,k,v,do,ctx,e,key_rel,query_rel,onehot_x,onehot_y,p0=0,count=None,before=None,after=None,through=None,B=128,C=128):
    R,F=q.shape; L=k.shape[0]; W=L+R; pairs=F//128
    count=pairs if count is None else count
    B=min(B,R)
    col=lambda n: pl.BlockSpec((n,128),lambda p,h:(0,p0+p))
    full=pl.BlockSpec((W,NB),lambda p,h:(0,0))
    flops=2*count*2*R*L*128*8
    args=[q,k,v,do,ctx,e,key_rel,query_rel,onehot_x,onehot_y]
    specs=[col(R),col(L),col(L),col(R),col(R),pl.BlockSpec((1,R,L),lambda p,h:(2*(p0+p)+h,0,0)),col(NB),col(NB),full,full]
    n_in=len(args)
    through=list(through or [])
    extra=list(before or [])+through+list(after or [])
    n_before=len(before or [])
    body=functools.partial(bwd_kernel,R,L,B,C)
    def kernel(*refs):
        rest=refs[n_in+len(extra):]
        body(*refs[:n_in],*rest[:5],*rest[5+len(through):])
    return pl.pallas_call(kernel,
        grid=(count,2),
        in_specs=specs+[pl.BlockSpec(memory_space=pl.ANY)]*len(extra),
        out_specs=[col(R),col(L),col(L),col(NB),col(NB)]+[pl.BlockSpec(memory_space=pl.ANY)]*len(through),
        out_shape=[jax.ShapeDtypeStruct((R,F),bf),jax.ShapeDtypeStruct((L,F),bf),jax.ShapeDtypeStruct((L,F),bf),
                   jax.ShapeDtypeStruct((NB,F),f32),jax.ShapeDtypeStruct((NB,F),f32)]+[jax.ShapeDtypeStruct(x.shape,x.dtype) for x in through],
        input_output_aliases={**({n_in+i:i for i in range(5)} if before else {}),**{n_in+n_before+i:5+i for i in range(len(through))}},
        scratch_shapes=[pltpu.VMEM((R,L),bf),pltpu.VMEM((R,128),bf),pltpu.VMEM((R,128),bf),
                        pltpu.VMEM((R,128),f32),pltpu.VMEM((L,128),f32),pltpu.VMEM((L,128),f32),
                        pltpu.VMEM((R,128),f32),pltpu.VMEM((2,B,L),f32),pltpu.VMEM((2,B,L+B),bf),pltpu.VMEM((2,C,R),bf),pltpu.VMEM((2,C,R+C),bf)],
        compiler_params=pltpu.CompilerParams(vmem_limit_bytes=48*1024*1024,dimension_semantics=("arbitrary","arbitrary")),
        cost_estimate=pl.CostEstimate(flops=flops,bytes_accessed=2*count*R*L*2+20*L*128*count,transcendentals=0),
        name="attend_back",
    )(*args,*extra)

EPS=1e-6

def gelu_parts(v):
    a=jnp.abs(v)
    t=1.0/(1.0+(0.3275911/math.sqrt(2.0))*a)
    bell=jnp.exp(-0.5*v*v)
    poly=t*(0.127414796+t*(-0.142248368+t*(0.7107068705+t*(-0.7265760135+t*0.5307027145))))
    tail=poly*bell
    phi=jnp.where(v>0,1.0-tail,tail)
    return v*phi, phi+v*bell*(1.0/math.sqrt(2.0*math.pi))

class Both:
    def __init__(self,*copies):
        self.copies=copies

    def start(self):
        for copy in self.copies:
            copy.start()

    def wait(self):
        for copy in self.copies:
            copy.wait()

def feed_kernel(R,D,tiles,per,rows_in,own_rows,ctx_ref,tok_ref,og_ref,scale_ref,wo_ref,late_ref,bias_ref,gain_ref,shift_ref,
                res_ref,dres_ref,do_ref,sums_ref,bsum_ref,keep_ref,give_ref,
                u1_ref,r1_ref,low_ref,acc_ref,pre_ref,gated_ref,gp_ref,dfeed_ref,stage_ref,tail_ref,datt_ref,sem):
    step=pl.program_id(0)
    core=lax.axis_index("dp")%2
    pairs=per//2
    width=per*rows_in
    CH=64
    def chunks(f):
        def body(i,c):
            f(pl.ds(pl.multiple_of(i*CH,CH),CH))
            return c
        lax.fori_loop(0,R//CH,body,0)
    mean=lambda x: jnp.mean(x,axis=1,keepdims=True)
    gain=lambda i: gain_ref[i:i+1,:]
    shift=lambda i: shift_ref[i:i+1,:]
    def add_sum(i,x):
        sums_ref[i:i+1,:]+=jnp.sum(x,axis=0,keepdims=True)
    @pl.when(step==0)
    def _():
        sums_ref[...]=jnp.zeros_like(sums_ref)
        acc_ref[...]=dot_nn(ctx_ref[...],wo_ref[...])
        def norm(at):
            v=tok_ref[at,:].astype(f32)+acc_ref[at,:]+shift(0)
            c=v-mean(v)
            r=lax.rsqrt(mean(c*c)+EPS)
            u=c*r
            u1_ref[at,:]=u
            r1_ref[at,:]=jnp.broadcast_to(r,(CH,128))
            h=u*gain(0)+shift(1)
            low_ref[at,:]=h.astype(bf)
            acc_ref[at,:]=h+shift(2)
        chunks(norm)
    w_in=late_ref[:,0:rows_in,:].reshape(width,D)
    w_outer=late_ref[:,rows_in:2*rows_in,:].reshape(width,D)
    @pl.when(step<tiles)
    def _():
        pre_ref[...]=dot_nt(low_ref[...],w_in)
        def act(at):
            g,gp=gelu_parts(pre_ref[at,:]+bias_ref[0])
            gated_ref[step,at,:]=g.astype(bf)
            gp_ref[step,at,:]=gp.astype(bf)
        chunks(act)
        acc_ref[...]+=dot_nn(gated_ref[step],w_outer)
    @pl.when(step==tiles-1)
    def _():
        def norm(at):
            v=acc_ref[at,:]
            c=v-mean(v)
            r=lax.rsqrt(mean(c*c)+EPS)
            u=c*r
            res_ref[at,:]=(u*gain(1)+shift(3)).astype(bf)
            top=og_ref[at,:].astype(f32)
            add_sum(1,top*u)
            add_sum(5,top)
            e=top*gain(1)
            d=(e-mean(e)-u*mean(e*u))*r
            add_sum(4,d)
            dfeed_ref[at,:]=d.astype(bf)
            acc_ref[at,:]=d
        chunks(norm)
    @pl.when(step>=tiles)
    def _():
        k=step-tiles
        slot=lax.rem(k,2)
        pre_ref[...]=dot_nt(dfeed_ref[...],w_outer)
        def act(at):
            d=(pre_ref[at,:]*gp_ref[k,at,:].astype(f32)).astype(bf)
            gp_ref[k,at,:]=d
        chunks(act)
        bsum_ref[0]=jnp.sum(gp_ref[k].astype(f32),axis=0,keepdims=True)
        def out(kk,s):
            to=(pl.ds(kk*pairs,pairs),pl.ds(0,2*rows_in))
            return Both(pltpu.make_async_copy(stage_ref.at[s,:,core],keep_ref.at[to],sem.at[s,0]),
                        pltpu.make_async_copy(stage_ref.at[s,:,1-core],give_ref.at[to],sem.at[s,1]))
        @pl.when(k>=2)
        def _():
            out(k-2,slot).wait()
        stage_ref[slot,:,:,0:rows_in,:]=dot_tn(gp_ref[k],low_ref[...]).astype(bf).reshape(pairs,2,rows_in,D)
        stage_ref[slot,:,:,rows_in:2*rows_in,:]=dot_tn(gated_ref[k],dfeed_ref[...]).astype(bf).reshape(pairs,2,rows_in,D)
        out(k,slot).start()
        acc_ref[...]+=dot_nn(gp_ref[k],w_in)
        @pl.when(k==tiles-1)
        def _():
            def norm(at):
                d=acc_ref[at,:]
                u=u1_ref[at,:]
                r=r1_ref[at,0:1]
                add_sum(0,d*u)
                add_sum(3,d)
                e=d*gain(0)
                g=(e-mean(e)-u*mean(e*u))*r
                add_sum(2,g)
                dres_ref[at,:]=g
                datt_ref[at,:]=g.astype(bf)
            chunks(norm)
            do_ref[...]=(dot_nt(datt_ref[...],wo_ref[...])*scale_ref[...]).astype(bf)
            outer=dot_tn(ctx_ref[...],datt_ref[...])
            n=D//own_rows
            gap=tail_ref.shape[2]-own_rows
            for p in range(n):
                piece=outer[p*own_rows:p*own_rows+own_rows,:]
                if gap:
                    piece=jnp.concatenate([piece,jnp.zeros((gap,D),f32)],axis=0)
                tail_ref[p//2,p%2]=piece.astype(bf)
            to=(slice(None),pl.ds(2*rows_in,tail_ref.shape[2]))
            last=Both(pltpu.make_async_copy(tail_ref.at[:,core],keep_ref.at[to],sem.at[2,0]),
                      pltpu.make_async_copy(tail_ref.at[:,1-core],give_ref.at[to],sem.at[2,1]))
            last.start()
            if tiles>1:
                out(k-1,1-slot).wait()
            out(k,slot).wait()
            last.wait()

def feed(ctx,tokens,out_grad,scale,out_rows,late,bias,gain,shift,rows_in,own_rows,tiles=4):
    R,D=ctx.shape
    n,rows_late,_=late.shape
    per=n//tiles
    width=per*rows_in
    tail=rows_late-2*rows_in
    vm=lambda s: pl.BlockSpec(s,lambda i: (0,)*len(s))
    return pl.pallas_call(functools.partial(feed_kernel,R,D,tiles,per,rows_in,own_rows),
        grid=(2*tiles,),
        in_specs=[vm((R,D)),vm((R,D)),vm((R,D)),vm((R,D)),vm((D,D)),
                  pl.BlockSpec((per,rows_late,D),lambda i:(lax.rem(i,tiles),0,0)),
                  pl.BlockSpec((1,1,width),lambda i:(lax.rem(i,tiles),0,0)),vm((2,D)),vm((4,D))],
        out_specs=[vm((R,D)),vm((R,D)),vm((R,D)),vm((8,D)),pl.BlockSpec((1,1,width),lambda i:(jnp.maximum(i-tiles,0),0,0)),
                   pl.BlockSpec(memory_space=pl.ANY),pl.BlockSpec(memory_space=pl.ANY)],
        out_shape=[jax.ShapeDtypeStruct((R,D),bf),jax.ShapeDtypeStruct((R,D),f32),jax.ShapeDtypeStruct((R,D),bf),
                   jax.ShapeDtypeStruct((8,D),f32),jax.ShapeDtypeStruct((tiles,1,width),f32),
                   jax.ShapeDtypeStruct((n//2,rows_late,D),bf),jax.ShapeDtypeStruct((n//2,rows_late,D),bf)],
        scratch_shapes=[pltpu.VMEM((R,D),f32),pltpu.VMEM((R,128),f32),pltpu.VMEM((R,D),bf),pltpu.VMEM((R,D),f32),
                        pltpu.VMEM((R,width),f32),pltpu.VMEM((tiles,R,width),bf),pltpu.VMEM((tiles,R,width),bf),
                        pltpu.VMEM((R,D),bf),pltpu.VMEM((2,per//2,2,2*rows_in,D),bf),pltpu.VMEM((n//2,2,tail,D),bf),pltpu.VMEM((R,D),bf),
                        pltpu.SemaphoreType.DMA((3,2))],
        compiler_params=pltpu.CompilerParams(vmem_limit_bytes=58*1024*1024,dimension_semantics=("arbitrary",)),
        cost_estimate=pl.CostEstimate(flops=2*R*D*n*rows_in*6+6*R*D*D,bytes_accessed=4*n*rows_late*D+20*R*D,transcendentals=2*R*n*rows_in),
        name="feed",
    )(ctx,tokens,out_grad,scale,out_rows,late,bias,gain,shift)

MESH = pl.DeviceIdType.MESH
ANY = pl.BlockSpec(memory_space=pl.ANY)
VM = pl.BlockSpec(memory_space=pltpu.VMEM)

def remote(src, dst, send, recv, peer):
    return pltpu.make_async_remote_copy(src_ref=src, dst_ref=dst, send_sem=send, recv_sem=recv,
                                        device_id=peer, device_id_type=MESH)

def meet(peers):
    barrier = pltpu.get_barrier_semaphore()
    for peer in peers:
        pl.semaphore_signal(barrier, inc=1, device_id=peer, device_id_type=MESH)
    pl.semaphore_wait(barrier, len(peers))

class Place:
    def __init__(self, n_t, n_dp):
        self.n_t, self.n_dp = n_t, n_dp
        bits = (n_dp // 2).bit_length() - 1
        self.low = bits // 2
        self.high = bits - self.low
        dp, self.t = lax.axis_index("dp"), lax.axis_index("tensor")
        self.core = dp % 2
        self.down = (dp // 2) % 2**self.low
        self.up = dp // 2 // 2**self.low
        self.others = [lax.rem(self.t + 1 + i, n_t) for i in range(n_t - 1)]
        self.twin = {"dp": dp - self.core + 1 - self.core}
        self.steps = [("down", i) for i in range(self.low)] + [("up", i) for i in range(self.high)]

    def bit(self, step):
        kind, i = step
        return (getattr(self, kind) // 2**i) % 2

    def peer(self, step):
        kind, i = step
        turn = (1 - 2 * self.bit(step)) * 2**i
        down = self.down + turn if kind == "down" else self.down
        up = self.up + turn if kind == "up" else self.up
        return {"dp": (up * 2**self.low + down) * 2 + self.core}

    def peers(self):
        return [{"tensor": o} for o in self.others] + [self.twin] + [self.peer(s) for s in self.steps]

    def orders(self):
        down = [s for s in self.steps if s[0] == "down"]
        up = [s for s in self.steps if s[0] == "up"]
        return [down + up, up + down]

    def spans(self, done):
        out = []
        for kind in ("up", "down"):
            n = sum(1 for s in done if s[0] == kind)
            here = getattr(self, kind)
            out.append(pl.ds((here // 2**n) * 2**n, 2**n))
        return out

    def parts(self):
        half = self.n_t // 2
        return [pl.ds(0, half), pl.ds(half, half)] if half else [pl.ds(0, 1)]

class Line:
    def __init__(self, t, n, own, slot, rows, pieces, send, recv):
        self.t, self.n, self.own, self.slot = t, n, own, slot
        self.rows, self.pieces, self.send, self.recv = rows, pieces, send, recv

    def piece(self, ref, j):
        size = self.rows // self.pieces
        return ref.at[pl.ds(j * size, size)]

    def copy(self, d, s, j, b, own):
        at = self.piece(self.slot(b), j)
        src = self.piece(self.own, j) if own else at
        peer = {"tensor": self.t + 1 - 2 * d}
        return remote(src, at, self.send.at[d, s, j], self.recv.at[d, s, j], peer)

    def post(self, s, j):
        for d in range(2):
            b = self.t - s + 2 * d * s
            go_on = (b >= 0) & (self.t + 1 < self.n) if d == 0 else (b < self.n) & (self.t > 0)

            @pl.when(go_on)
            def _():
                self.copy(d, s, j, b, s == 0).start()

    def take(self, s, j):
        for d in range(2):
            b = self.t - 1 - s if d == 0 else self.t + 1 + s

            @pl.when(b >= 0 if d == 0 else b < self.n)
            def _():
                self.copy(d, s, j, b, False).wait_recv()

    def step(self, s):
        for j in range(self.pieces):
            self.take(s, j)
            if s + 1 < self.n - 1:
                self.post(s + 1, j)

    def drain(self):
        for s in range(self.n - 1):
            for j in range(self.pieces):
                for d in range(2):
                    b = self.t - s + 2 * d * s

                    @pl.when((b >= 0) & (self.t + 1 < self.n) if d == 0 else (b < self.n) & (self.t > 0))
                    def _():
                        self.copy(d, s, j, b, s == 0).wait_send()

def lanes_of(count, width, shape, tall):
    wide_axis = 0 if tall else 1
    f = lax.broadcasted_iota(jnp.int32, shape, wide_axis)
    r = lax.broadcasted_iota(jnp.int32, shape, 1 - wide_axis)
    return jnp.where(f % count == r, 1.0, 0.0).astype(bf)

def spread_row(table, count, width, first):
    n = table.shape[0]
    full = dot_nn(table.astype(bf), lanes_of(count, width, (128, width), False))
    p = lax.broadcasted_iota(jnp.int32, (n, width), 0)
    f = lax.broadcasted_iota(jnp.int32, (n, width), 1)
    return jnp.sum(jnp.where(first + f // count == p, full, 0.0), axis=0, keepdims=True)

def fold_row(row, count, n, first):
    width = row.shape[1]
    p = lax.broadcasted_iota(jnp.int32, (n, width), 0)
    f = lax.broadcasted_iota(jnp.int32, (n, width), 1)
    full = jnp.where(first + f // count == p, jnp.broadcast_to(row, (n, width)), 0.0)
    return dot_nn(full.astype(bf), lanes_of(count, width, (width, 128), True))

def eight(n):
    return -(-n // 8) * 8

def begin_kernel(n_t, n_dp, own, part, cols, inner, tiles, L,
                 tok_ref, wq_ref, wk_ref, wv_ref, rel_ref, qkvb_ref, ffb_ref, gains_ref, shifts_ref, ahead_ref, back_ref,
                 q_out, k_out, v_out, krel_out, qrel_out, kt_out, qr_out, toks_out, w_out, ox_out, oy_out, table_out,
                 ibias_ref, gain_ref, shift_ref,
                 toks, packs, pack, packf, wf, w, kb, vb, qb, krel, qrel, kt, qr, table, tableb, miscf, ox, ox_tall, oy_tall,
                 tok_send, tok_recv, z_send, z_recv, x_send, x_recv, out_sem):
    at = Place(n_t, n_dp)
    t = at.t
    R, D = tok_ref.shape
    W = L + R
    n_all = n_t * n_dp
    S, S2 = eight(own), eight(part)
    misc = 3 * S + S2

    packf[...] = jnp.zeros_like(packf)
    for i, ref in enumerate((wq_ref, wk_ref, wv_ref)):
        packf[i * S:i * S + own, :] = ref[...].astype(f32)
    for i in range(n_t):
        @pl.when(t == i)
        def _():
            packf[3 * S:3 * S + part, :] = rel_ref[...].astype(f32)[i * part:(i + 1) * part]
    for i in range(3):
        packf[misc:misc + 1, 128 * i:128 * i + own] = qkvb_ref[i:i + 1, :].astype(f32)
    packf[misc:misc + 1, 384:384 + inner] = ffb_ref[...].astype(f32)
    for i in range(2):
        packf[misc + 1:misc + 2, 128 * i:128 * i + cols] = gains_ref[i:i + 1, :].astype(f32)
    for i in range(4):
        packf[misc + 1:misc + 2, 256 + 128 * i:256 + 128 * i + cols] = shifts_ref[i:i + 1, :].astype(f32)
    pack[...] = packf[...].astype(bf)

    meet(at.peers())
    copies = []

    def go(copy):
        copy.start()
        copies.append(copy)
        return copy

    here = packs.at[t, at.up, at.down, at.core]
    column = Line(t, n_t, pack, lambda i: packs.at[i, at.up, at.down, at.core], pack.shape[0], 1, z_send, z_recv)
    tokens = Line(t, n_t, tok_ref, lambda i: toks.at[i], R, 2, tok_send, tok_recv)
    column.post(0, 0)
    for j in range(2):
        tokens.post(0, j)
    own_pack = pltpu.make_async_copy(pack, here, out_sem.at[0])
    own_pack.start()
    outs = []

    def put(src, dst):
        copy = pltpu.make_async_copy(src, dst, out_sem.at[1 + len(outs)])
        copy.start()
        outs.append(copy)

    def pick(line, start):
        rows = line[:, pl.ds(pl.multiple_of(start, 128), W)]
        ids = lax.broadcasted_iota(jnp.int32, (NB, W), 0)
        return jnp.where(ids == rows, 1.0, 0.0).astype(bf)

    ox[...] = pick(back_ref, L - R - R * t)
    ox_tall[...] = ox[...].T
    oy_tall[...] = pick(ahead_ref, L - R - R * t).T
    put(ox_tall, ox_out)
    put(oy_tall, oy_out)

    for s in range(n_t - 1):
        column.step(s)
    own_pack.wait()
    parts, orders = at.parts(), at.orders()
    n_steps = len(at.steps)
    swaps = {}

    def swap(h, k):
        if k:
            swaps[h, k - 1].wait_recv()
        up, down = at.spans(orders[h][:k])
        if k < n_steps:
            piece, peer = packs.at[parts[h], up, down, at.core], at.peer(orders[h][k])
        else:
            piece, peer = packs.at[parts[h], :, :, at.core], at.twin
        swaps[h, k] = go(remote(piece, piece, x_send.at[h, k], x_recv.at[h, k], peer))

    hs = range(len(parts))
    passed = 0
    for k in range(n_steps + 1):
        for h in hs:
            swap(h, k)
        if k and passed < n_t - 2:
            tokens.step(passed)
            passed += 1
    for h in hs:
        swaps[h, n_steps].wait_recv()

    slots = [(a, u, d, c) for a in range(n_t) for u in range(2**at.high) for d in range(2**at.low) for c in range(2)]
    for i in range(3):
        for p, s in enumerate(slots):
            wf[p * own:p * own + own, :] = packs[s[0], s[1], s[2], s[3], i * S:i * S + own, :].astype(f32)
        w[i] = wf[...].astype(bf)
    put(w, w_out)
    for p, s in enumerate(slots):
        rows = packs[s[0], s[1], s[2], s[3], misc:misc + 8, :].astype(f32)
        miscf[0, p:p + 1, :] = rows[0:1]
        miscf[1, p:p + 1, :] = rows[1:2]
        a, dp = p // n_dp, p % n_dp
        to = dp * n_t * part + a * part
        table[to:to + part, :] = packs[s[0], s[1], s[2], s[3], 3 * S:3 * S + part, :].astype(f32)
    bias = [spread_row(miscf[0, :, 128 * i:128 * i + 128], own, D, 0) for i in range(3)]
    rel = table[...].astype(bf)
    tableb[...] = rel
    put(tableb, table_out)
    krel[...] = (dot_nt(rel, w[1]) + bias[1]).astype(bf)
    qrel[...] = (dot_nt(rel, w[0]) + bias[0]).astype(bf)
    put(krel, krel_out)
    put(qrel, qrel_out)
    kt[...] = dot_tn(ox[...], krel[...]).astype(bf)
    put(kt, kt_out)
    qr[...] = dot_tn(pick(back_ref, R * t), qrel[...]).astype(bf)
    put(qr, qr_out)

    def project(tokens, i):
        return (dot_nt(tokens, w[i]) + bias[i]).astype(bf)

    qb[...] = project(tok_ref[...], 0)
    put(qb, q_out)
    width = n_all * inner // tiles
    for i in range(tiles):
        ibias_ref[i] = spread_row(miscf[0, :, 384:512], inner, width, i * (n_all // tiles))
    for i in range(2):
        gain_ref[i:i + 1, :] = spread_row(miscf[1, 0:n_dp, 128 * i:128 * i + 128], cols, D, 0)
    for i in range(4):
        shift_ref[i:i + 1, :] = spread_row(miscf[1, 0:n_dp, 256 + 128 * i:384 + 128 * i], cols, D, 0)

    for s in range(n_t):
        b = lax.rem(t - s + n_t, n_t)
        rows = pl.ds(pl.multiple_of(b * R, R), R)
        if s == 1:
            for i in range(passed, n_t - 1):
                tokens.step(i)
        src = tok_ref if s == 0 else toks.at[b]
        put(src, toks_out.at[b])
        kb[s] = project(src[...], 1)
        put(kb.at[s], k_out.at[rows])
        vb[s] = project(src[...], 2)
        put(vb.at[s], v_out.at[rows])
    for copy in outs:
        copy.wait()
    for copy in copies:
        copy.wait_send()
    column.drain()
    tokens.drain()

def begin(tokens, w_query, w_key, w_value, rel_table, qkv_bias, ff_bias, gains, shifts, ahead, back, n_t, n_dp, tiles):
    R, D = tokens.shape
    L = ahead.shape[1] // 2
    W = L + R
    own, inner, cols = w_query.shape[0], ff_bias.shape[1], gains.shape[1]
    part = rel_table.shape[0] // n_t
    n_all = n_t * n_dp
    width = n_all * inner // tiles
    PR = -(-(3 * eight(own) + eight(part) + 8) // 16) * 16
    bits = (n_dp // 2).bit_length() - 1
    low = bits // 2
    S = jax.ShapeDtypeStruct
    big = [(R, D), (L, D), (L, D), (NB, D), (NB, D), (W, D), (W, D), (n_t, R, D), (3, D, D), (W, NB), (W, NB), (NB, D)]
    v = lambda s, t=bf: pltpu.VMEM(s, t)
    dma = lambda *s: pltpu.SemaphoreType.DMA(s)
    return pl.pallas_call(
        functools.partial(begin_kernel, n_t, n_dp, own, part, cols, inner, tiles, L),
        out_shape=[S(s, bf) for s in big] + [S((tiles, 1, width), f32), S((2, D), f32), S((4, D), f32)],
        in_specs=[VM] * 11, out_specs=[ANY] * len(big) + [VM] * 3,
        scratch_shapes=[v((n_t, R, D)), v((n_t, 2**(bits - low), 2**low, 2, PR, D)), v((PR, D)), v((PR, D), f32), v((D, D), f32),
                        v((3, D, D)), v((n_t, R, D)), v((n_t, R, D)), v((R, D)), v((NB, D)), v((NB, D)), v((W, D)), v((W, D)),
                        v((NB, D), f32), v((NB, D)), v((2, n_all, D), f32), v((NB, W)), v((W, NB)), v((W, NB)),
                        dma(2, n_t - 1, 2), dma(2, n_t - 1, 2), dma(2, n_t - 1, 1), dma(2, n_t - 1, 1), dma(2, bits + 1), dma(2, bits + 1),
                        dma(10 + 3 * n_t)],
        compiler_params=pltpu.CompilerParams(collective_id=0, has_side_effects=True, vmem_limit_bytes=58 * 1024 * 1024),
        name="begin",
    )(tokens, w_query, w_key, w_value, rel_table, qkv_bias, ff_bias, gains, shifts, ahead, back)

def finish_kernel(n_t, n_dp, own, rel_rows, cols, inner, tiles,
                  dq_in, dk_in, dv_in, tok_in, toks_in, w_in, table_in, dqr_in, dkr_in, dres_in, sums_ref, bsum_ref,
                  tg_ref, gq_ref, gk_ref, gv_ref, rel_ref, qkvb_ref, ffb_ref, gains_ref, shifts_ref,
                  dq, dk, dv, tok, toks, w, table, dqr, dkr, dres, g, relf, m0, m1, miscs, pack, first, acc, got, total,
                  tok_got, tok_acc, tok_own, base, *rest):
    at = Place(n_t, n_dp)
    t = at.t
    n_steps = len(at.steps)
    bufs, (in_sem, tok_send, tok_recv, x_send, x_recv, z_send, z_recv) = rest[:2 * n_steps], rest[2 * n_steps:]
    R, D = tok.shape
    L = n_t * R
    n_all = n_t * n_dp
    S, S3 = eight(own), eight(rel_rows)
    misc = 3 * S
    PR = pack.shape[4]
    right = {"tensor": lax.rem(t + 1, n_t)}
    loads = []

    def load(src, dst):
        copy = pltpu.make_async_copy(src, dst, in_sem.at[len(loads)])
        copy.start()
        loads.append(copy)
        return copy

    def block(s):
        return lax.rem(t - 1 - s + 2 * n_t, n_t)

    l_w = load(w_in, w)
    l_kv = []
    for s in range(n_t):
        b = block(s)
        l_kv.append((load(dk_in.at[b], dk.at[b]), load(dv_in.at[b], dv.at[b])))
    l_toks = load(toks_in, toks)
    l_rest = [load(tok_in, tok), load(dq_in, dq), load(table_in, table), load(dqr_in, dqr), load(dkr_in, dkr), load(dres_in, dres)]
    meet(at.peers())
    copies = []

    def go(copy):
        copy.start()
        copies.append(copy)
        return copy

    half = R // 2
    token = {}

    def partial(s):
        for copy in l_kv[s]:
            copy.wait()
        b = block(s)
        return dot_nn(dk[b], w[1]) + dot_nn(dv[b], w[2])

    def send_token(s):
        for j in range(2):
            rows = pl.ds(j * half, half)
            if s:
                token[s - 1, j].wait_recv()
                tok_acc[s, rows] = (tok_own[rows].astype(f32) + tok_got[s - 1, rows].astype(f32)).astype(bf)
            token[s, j] = go(remote(tok_acc.at[s, rows], tok_got.at[s, rows], tok_send.at[s, j], tok_recv.at[s, j], right))

    l_w.wait()
    tok_acc[0] = partial(0).astype(bf)
    send_token(0)
    blocks = [None] * n_t
    tok_own[...] = partial(1).astype(bf)

    for s in range(2, n_t):
        for copy in l_kv[s]:
            copy.wait()
    l_kv = [()] * n_t
    l_toks.wait()
    for copy in l_rest:
        copy.wait()
    dqb, dkb = dqr[...].astype(bf), dkr[...].astype(bf)
    rel_table = table[...]
    g[0] = dot_tn(dq[...], tok[...]) + dot_tn(dqb, rel_table)
    g[1] = dot_tn(dk[...].reshape(L, D), toks[...].reshape(L, D)) + dot_tn(dkb, rel_table)
    g[2] = dot_tn(dv[...].reshape(L, D), toks[...].reshape(L, D))
    relf[...] = dot_nn(dqb, w[0]) + dot_nn(dkb, w[1])
    ones = lambda n: jnp.ones((8, n), bf)
    columns = [dot_nn(ones(R), dq[...])[0:1] + jnp.sum(dqr[...], axis=0, keepdims=True),
               dot_nn(ones(L), dk[...].reshape(L, D))[0:1] + jnp.sum(dkr[...], axis=0, keepdims=True),
               dot_nn(ones(L), dv[...].reshape(L, D))[0:1]]
    for i in range(3):
        m0[:, 128 * i:128 * i + 128] = fold_row(columns[i], own, n_all, 0)
    units = jnp.zeros((n_all, 128), f32)
    for i in range(tiles):
        units += fold_row(bsum_ref[i], inner, n_all, i * (n_all // tiles))
    m0[:, 384:512] = units
    for i in range(6):
        m1[:, 128 * i:128 * i + 128] = fold_row(sums_ref[i:i + 1, :], cols, n_dp, 0)
    miscs[...] = jnp.zeros_like(miscs)
    slots = [(a, u, d, c) for a in range(n_t) for u in range(2**at.high) for d in range(2**at.low) for c in range(2)]

    def padded(x, n):
        return jnp.concatenate([x, jnp.zeros((n - x.shape[0], D), f32)], axis=0) if n > x.shape[0] else x

    for p, s in enumerate(slots):
        dp = p % n_dp
        miscs[8 * p:8 * p + 1, 0:512] = m0[p:p + 1, :]
        miscs[8 * p + 1:8 * p + 2, :] = m1[dp:dp + 1, :]
        pieces = [padded(g[i, p * own:p * own + own, :], S) for i in range(3)]
        pieces += [miscs[8 * p:8 * p + 8, :], padded(relf[dp * rel_rows:dp * rel_rows + rel_rows, :], S3)]
        whole = padded(jnp.concatenate(pieces, axis=0), PR)
        pack[s[0], s[1], s[2], s[3]] = whole.astype(bf)

    parts = at.parts()
    hs = range(len(parts))
    per = n_t // len(parts)
    orders = [list(reversed(o)) for o in at.orders()][:len(parts)]
    swaps = {}
    left = {h: {"up": at.high, "down": at.low} for h in hs}

    def region(h, cut=None):
        out = []
        for kind in ("up", "down"):
            n = left[h][kind]
            here = getattr(at, kind)
            if cut is not None and cut[0] == kind:
                start = (here // 2**n) * 2**n + (1 - at.bit(cut)) * 2**(n - 1)
                out.append((start, 2**(n - 1)))
            else:
                out.append(((here // 2**n) * 2**n, 2**n))
        return out

    def start(h, k):
        if k == 0:
            src, dst, peer = pack.at[parts[h], :, :, 1 - at.core], first.at[parts[h]], at.twin
        else:
            cut = orders[h][k - 1]
            up, down = [pl.ds(*x) for x in region(h, cut)]
            src, dst, peer = acc.at[parts[h], up, down], bufs[h * n_steps + k - 1], at.peer(cut)
        swaps[h, k] = go(remote(src, dst, x_send.at[h, k], x_recv.at[h, k], peer))

    def absorb(h, k):
        swaps[h, k].wait_recv()
        if k:
            left[h][orders[h][k - 1][0]] -= 1
        (u0, nu), (d0, nd) = region(h)
        buf = first if k == 0 else bufs[h * n_steps + k - 1]

        @pl.loop(0, per * nu * nd)
        def _(m):
            a, u, d = m // (nu * nd), m // nd % nu, m % nd
            if k == 0:
                x, y = pack[h * per + a, u, d, at.core], buf[h * per + a, u, d]
            else:
                x, y = acc[h * per + a, u0 + u, d0 + d], buf[a, u, d]
            acc[h * per + a, u0 + u, d0 + d] = (x.astype(f32) + y.astype(f32)).astype(bf)

    for h in hs:
        start(h, 0)
    sent = 1
    if n_t > 2:
        send_token(1)
        sent = 2
        tok_own[...] = partial(2).astype(bf)
    base[...] = partial(n_t - 1) + dres[...] + dot_nn(dq[...], w[0])
    for k in range(n_steps + 1):
        for h in hs:
            absorb(h, k)
            if k < n_steps:
                start(h, k + 1)
        if k == n_steps:
            ring = [go(remote(acc.at[o, at.up, at.down], got.at[i], z_send.at[i], z_recv.at[i], {"tensor": o}))
                    for i, o in enumerate(at.others)]
        if k and sent < n_t - 1:
            send_token(sent)
            sent += 1
            if sent < n_t - 1:
                tok_own[...] = partial(sent).astype(bf)
    for copy in ring:
        copy.wait_recv()
    total[...] = acc[t, at.up, at.down].astype(f32)
    for i in range(n_t - 1):
        total[...] += got[i].astype(f32)
    for i, ref in enumerate((gq_ref, gk_ref, gv_ref)):
        ref[...] = total[i * S:i * S + own, :]
    rel_ref[...] = total[misc + 8:misc + 8 + rel_rows, :]
    for i in range(3):
        qkvb_ref[i:i + 1, :] = total[misc:misc + 1, 128 * i:128 * i + own]
    ffb_ref[...] = total[misc:misc + 1, 384:384 + inner]
    for i in range(2):
        gains_ref[i:i + 1, :] = total[misc + 1:misc + 2, 128 * i:128 * i + cols]
    for i in range(4):
        shifts_ref[i:i + 1, :] = total[misc + 1:misc + 2, 256 + 128 * i:256 + 128 * i + cols]
    while sent < n_t - 1:
        send_token(sent)
        sent += 1
        if sent < n_t - 1:
            tok_own[...] = partial(sent).astype(bf)
    for j in range(2):
        rows = pl.ds(j * half, half)
        token[n_t - 2, j].wait_recv()
        tg_ref[rows, :] = base[rows, :] + tok_got[n_t - 2, rows].astype(f32)
    for copy in copies:
        copy.wait_send()

def finish(dq, dk, dv, tok, toks, w, table, dqr, dkr, dres, sums, bsum, own, rel_rows, cols, inner, n_t, n_dp):
    R, D = tok.shape
    L = n_t * R
    n_all = n_t * n_dp
    tiles = bsum.shape[0]
    S3 = eight(rel_rows)
    PR = -(-(3 * eight(own) + 8 + S3) // 16) * 16
    bits = (n_dp // 2).bit_length() - 1
    low = bits // 2
    high = bits - low
    per = n_t // 2
    v = lambda s, x=bf: pltpu.VMEM(s, x)
    dma = lambda *s: pltpu.SemaphoreType.DMA(s)
    bufs = []
    for order in ([("up", high), ("down", low)], [("down", low), ("up", high)]):
        left = {"up": high, "down": low}
        for kind, n in order:
            for _ in range(n):
                left[kind] -= 1
                bufs.append(v((per, 2**left["up"], 2**left["down"], PR, D)))
    S = jax.ShapeDtypeStruct
    outs = [(R, D), (own, D), (own, D), (own, D), (rel_rows, D), (3, own), (1, inner), (2, cols), (4, cols)]
    blocks = lambda x: x.reshape(n_t, R, D)
    return pl.pallas_call(
        functools.partial(finish_kernel, n_t, n_dp, own, rel_rows, cols, inner, tiles),
        out_shape=[S(s, f32) for s in outs],
        in_specs=[ANY] * 10 + [VM] * 2, out_specs=[VM] * len(outs),
        scratch_shapes=[v((R, D)), v((n_t, R, D)), v((n_t, R, D)), v((R, D)), v((n_t, R, D)), v((3, D, D)), v((NB, D)),
                        v((NB, D), f32), v((NB, D), f32), v((R, D), f32), v((3, D, D), f32), v((NB, D), f32),
                        v((n_all, 512), f32), v((n_dp, D), f32), v((8 * n_all, D), f32),
                        v((n_t, 2**high, 2**low, 2, PR, D)), v((n_t, 2**high, 2**low, PR, D)), v((n_t, 2**high, 2**low, PR, D)),
                        v((n_t - 1, PR, D)), v((PR, D), f32),
                        v((n_t - 1, R, D)), v((n_t - 1, R, D)), v((R, D)), v((R, D), f32)] + bufs
                       + [dma(2 * n_t + 8), dma(n_t - 1, 2), dma(n_t - 1, 2), dma(2, bits + 1), dma(2, bits + 1), dma(n_t - 1), dma(n_t - 1)],
        compiler_params=pltpu.CompilerParams(collective_id=1, has_side_effects=True, vmem_limit_bytes=60 * 1024 * 1024),
        name="finish",
    )(dq, blocks(dk), blocks(dv), tok, blocks(toks), w, table, dqr, dkr, dres, sums, bsum)

GROUPS, TILES = 32, 4
ALL=("tensor","dp")

def fold(name, grid, place, terms, shapes, out_maps):
    tail = terms[0][0].shape[-2:]
    block = lambda x, where: pl.BlockSpec((1,) * (len(x.shape) - 2) + tail, lambda *i: tuple(where(*i)) + (0, 0))
    n = len(terms)

    def kernel(place_ref, *refs):
        for k in range(n):
            x, y, out = refs[2 * k], refs[2 * k + 1], refs[2 * n + k]
            out[...] = (x[...].astype(f32) + y[...].astype(f32)).reshape(out.shape).astype(bf)

    outs = [jax.ShapeDtypeStruct(s + tail, bf) for s in shapes]
    return pl.pallas_call(
        kernel, out_shape=outs,
        grid_spec=pltpu.PrefetchScalarGridSpec(
            num_scalar_prefetch=1, grid=grid,
            in_specs=[block(z, where) for x, y, where in terms for z in (x, y)],
            out_specs=[block(o, where) for o, where in zip(outs, out_maps)]),
        compiler_params=pltpu.CompilerParams(vmem_limit_bytes=32 * 1024 * 1024, dimension_semantics=("arbitrary",) * len(grid)),
        cost_estimate=pl.CostEstimate(flops=0, bytes_accessed=sum(6 * math.prod(o.shape) for o in outs), transcendentals=0),
        name=name,
    )(place, *[z for x, y, _ in terms for z in (x, y)])

def finish_plain(dq, dk, dv, tok, toks, w, table, dqr, dkr, dres, sums, bsum, own, rel_rows, cols, inner, n_t, n_dp):
    times = lambda s, a, b: jnp.einsum(s, a.astype(bf), b.astype(bf), preferred_element_type=f32)
    scatter = lambda x: lax.psum_scatter(x, ALL, scatter_dimension=0, tiled=True)
    grads = [times("tf,td->fd", dq, tok) + times("tf,td->fd", dqr, table),
             times("tf,td->fd", dk, toks) + times("tf,td->fd", dkr, table), times("tf,td->fd", dv, toks)]
    rel = times("bf,fd->bd", dqr, w[0]) + times("bf,fd->bd", dkr, w[1])
    spread = (times("tf,fd->td", dk, w[1]) + times("tf,fd->td", dv, w[2])).astype(bf)
    back_sum = lax.psum_scatter(spread, "tensor", scatter_dimension=0, tiled=True).astype(f32)
    tokens_grad = dres + times("tf,fd->td", dq, w[0]) + back_sum
    column = lambda x: jnp.sum(x.astype(f32), axis=0)
    bias = jnp.stack([column(dq) + column(dqr), column(dk) + column(dkr), column(dv)])
    every = lambda x: lax.psum(x, ALL)
    dp = lax.axis_index("dp")
    place = lax.axis_index("tensor") * n_dp + dp
    cut = lambda x, i, n: lax.dynamic_slice_in_dim(x, i * n, n, 1)
    rel = lax.dynamic_slice_in_dim(every(rel), dp * rel_rows, rel_rows, 0)
    return [tokens_grad] + [scatter(x) for x in grads] + [rel, cut(every(bias), place, own), cut(every(bsum.reshape(1, -1)), place, inner),
            cut(every(sums[:2]), dp, cols), cut(every(sums[2:6]), dp, cols)]

def local(tokens, w_query, w_key, w_value, w_out, qkv_bias, w_ff_in, w_ff_out, ff_bias, rel_table,
          gains, shifts, rel_bucket, lengths, out_grad):
    D = tokens.shape[1]
    n_t, n_dp = lax.axis_size("tensor"), lax.axis_size("dp")
    n_all = n_t * n_dp
    t = lax.axis_index("tensor")
    R = tokens.shape[0]
    L = (rel_bucket.shape[0] + 1) // 2
    W = L + R
    own_rows, cols, inner = w_query.shape[0], gains.shape[1], ff_bias.shape[0]
    none = jnp.full((1,), -1, jnp.int32)
    ahead = jnp.concatenate([rel_bucket, none])[None]
    back = jnp.concatenate([rel_bucket[::-1], none])[None]
    (query, key, value, key_rel, query_rel, key_table, query_table, gathered, weights, pick_x, pick_y, table,
     inner_bias, gain, shift) = begin(tokens, w_query, w_key, w_value, rel_table, qkv_bias, ff_bias.reshape(1, -1), gains, shifts,
                                      ahead, back, n_t, n_dp, TILES)
    gathered = gathered.reshape(L, D)
    late_rows = w_ff_in.shape[0]
    even = late_rows % 16 == 0 and own_rows % 8 == 0
    late = jnp.concatenate([w_ff_in, w_ff_out, w_out], axis=0)
    late_own = late.shape[0]
    late = jnp.pad(late, ((0, -late_own % 16), (0, 0)))
    late_all = lax.all_gather(late, ALL, axis=0, tiled=False)
    cut = lambda x, at, n: x[:, at:at + n].reshape(n_all * n, D)
    out_rows = cut(late_all, 2 * late_rows, own_rows)
    groups = n_all if even else GROUPS
    group_rows, group_own = n_all * late_rows // groups, D // groups
    if not even:
        sections = [cut(late_all, 0, late_rows), cut(late_all, late_rows, late_rows)]
        late_all = jnp.concatenate([x.reshape(groups, group_rows, D) for x in sections]
                                   + [jnp.zeros((groups, -(-group_own // 16) * 16, D), bf)], axis=1)
    mask = jnp.where(jnp.arange(L, dtype=jnp.int32) < lengths[0], 0.0, -1e9).astype(bf)
    mask = jnp.broadcast_to(mask[:, None], (L, 128))

    context, scale, shares = attention_forward(query, key, value, key_table, query_table, mask)
    layer_result_rows, d_resid_one, d_scaled, sums, bias_sums, keep, give = feed(
        context, tokens, out_grad, scale, out_rows, late_all, inner_bias, gain, shift, group_rows, group_own)
    back_args = (query, key, value, d_scaled, context, shares, key_rel, query_rel, pick_x, pick_y)
    pairs = D // 128
    if even and n_dp == 8 and n_t % 2 == 0 and pairs >= 4:
        dp = lax.axis_index("dp")
        place = jnp.stack([dp // 4, dp // 2 % 2]).astype(jnp.int32)
        swap = lambda x, mask: lax.ppermute(x, "dp", [(i, i ^ mask) for i in range(n_dp)])
        shape = (n_t, 2, 2, late.shape[0], D)
        keep, give = keep.reshape(shape), give.reshape(shape)
        got = swap(give, 1)
        half = n_t // 2
        *grads, keep = attention_backward(*back_args, p0=0, count=pairs - 4, through=[keep])
        stay_one, away_one, stay_two, away_two = fold(
            "fold", (half, 2), place,
            [(keep, got, lambda i, j, s: (i, s[0], j)), (keep, got, lambda i, j, s: (i, 1 - s[0], j)),
             (keep, got, lambda i, j, s: (half + i, j, s[1])), (keep, got, lambda i, j, s: (half + i, j, 1 - s[1]))],
            [(half, 2)] * 4, [lambda i, j, s: (i, j)] * 4)
        got_one, got_two = swap(away_one, 4), swap(away_two, 2)
        *grads, stay_one, stay_two = attention_backward(
            *back_args, p0=pairs - 4, count=2, before=grads, after=[away_one, away_two], through=[stay_one, stay_two])
        stay_one, away_one, stay_two, away_two = fold(
            "fold", (half,), place,
            [(stay_one, got_one, lambda i, s: (i, s[1])), (stay_one, got_one, lambda i, s: (i, 1 - s[1])),
             (stay_two, got_two, lambda i, s: (i, s[0])), (stay_two, got_two, lambda i, s: (i, 1 - s[0]))],
            [(half,)] * 4, [lambda i, s: (i,)] * 4)
        got_one, got_two = swap(away_one, 2), swap(away_two, 4)
        *grads, stay_one, stay_two = attention_backward(
            *back_args, p0=pairs - 2, count=1, before=grads, after=[away_one, away_two], through=[stay_one, stay_two])
        column = jnp.concatenate(fold(
            "fold", (half,), place,
            [(stay_one, got_one, lambda i, s: (i,)), (stay_two, got_two, lambda i, s: (i,))],
            [(half,)] * 2, [lambda i, s: (i,)] * 2), axis=0)
        late_sum = lax.psum_scatter(column, "tensor", scatter_dimension=0, tiled=True)[0]
        grads = attention_backward(*back_args, p0=pairs - 1, count=1, before=grads, after=[column])
    else:
        grads = attention_backward(*back_args)
        core = lax.axis_index("dp") % 2
        late_grad = jnp.where(core == 0, jnp.stack([keep, give], axis=1), jnp.stack([give, keep], axis=1))
        late_grad = late_grad.reshape(groups, -1, D)
        parted = lambda x: x.reshape(n_all, -1, D)
        if not even:
            late_grad = jnp.concatenate([
                parted(late_grad[:, :group_rows]), parted(late_grad[:, group_rows:2 * group_rows]),
                parted(late_grad[:, 2 * group_rows:2 * group_rows + group_own]),
                jnp.zeros((n_all, late.shape[0] - late_own, D), bf)], axis=1)
        late_sum = lax.psum_scatter(late_grad, ALL, scatter_dimension=0, tiled=True)[0]
    d_query, d_key, d_value, d_key_rel, d_query_rel = grads
    late_sum = late_sum.astype(f32)
    g_inner, g_outer, g_out = late_sum[:late_rows], late_sum[late_rows:2 * late_rows], late_sum[2 * late_rows:late_own]
    ends = (d_query, d_key, d_value, tokens, gathered, weights, table, d_query_rel, d_key_rel, d_resid_one, sums, bias_sums)
    rel_rows = rel_table.shape[0]
    finished = (finish if even else finish_plain)(*ends, own_rows, rel_rows, cols, inner, n_t, n_dp)
    tokens_grad, g_query, g_key, g_value, g_rel, g_qkv_bias, g_ff_bias, g_gains, g_shifts = finished
    return (layer_result_rows, tokens_grad, g_query, g_key, g_value, g_out,
            g_qkv_bias, g_inner, g_outer, g_ff_bias.reshape(inner), g_rel, g_gains, g_shifts)

def solution(mesh):
    rows, params = P(("dp", "tensor"), None), P(ALL, None)
    return jax.shard_map(
        local, mesh=mesh,
        in_specs=(rows, params, params, params, params, P(None, ALL), params, params, P(ALL), P("dp", None),
                  P(None, "dp"), P(None, "dp"), P(), P("dp"), rows),
        out_specs=(rows, rows, params, params, params, params, P(None, ALL), params, params, P(ALL), P("dp", None),
                   P(None, "dp"), P(None, "dp")),
        check_vma=False)
```

```python
import functools
import math

import jax
import jax.numpy as jnp
from jax import lax
from jax.experimental import pallas as pl
from jax.experimental.pallas import tpu as pltpu
from jax.sharding import PartitionSpec as P

bf = jnp.bfloat16
f32 = jnp.float32
DH=64; NB=256
SCALE=1.0/math.sqrt(3*DH)
LOG2E=math.log2(math.e)

def dot_nt(a,b):
    return lax.dot_general(a,b,(((1,),(1,)),((),())),preferred_element_type=f32)
def dot_nn(a,b):
    return lax.dot_general(a,b,(((1,),(0,)),((),())),preferred_element_type=f32)
def dot_tn(a,b):
    return lax.dot_general(a,b,(((0,),(0,)),((),())),preferred_element_type=f32)

def flip_matrix(n):
    a=lax.broadcasted_iota(jnp.int32,(n,n),0); b=lax.broadcasted_iota(jnp.int32,(n,n),1)
    return jnp.where(a+b==n-1,1.0,0.0).astype(bf)

def flip_rows(x):
    n,w=x.shape
    idx=7-lax.broadcasted_iota(jnp.int32,(8,w),0)
    return jnp.concatenate([jnp.take_along_axis(x[n-8-8*g:n-8*g],idx,axis=0) for g in range(n//8)],axis=0)

def fwd_kernel(R,L,B,C,mask_ref,q_ref,k_ref,v_ref,kt_ref,qr_ref,ctx_ref,scale_ref,e_ref,yt_ref,acc_ref,km_ref,y_ref,s_ref,x_ref,p_ref):
    hh=pl.program_id(1)
    lane=lambda n: lax.broadcasted_iota(jnp.int32,(n,128),1)
    def lanes(n): return (lane(n)//DH)==hh
    zero,one=jnp.zeros((),bf),jnp.ones((),bf)
    spare=(1-hh)*DH
    for i in range(L//C):
        at=slice(i*C,i*C+C)
        km_ref[at,:]=jnp.where(lane(C)==spare,mask_ref[at,:],k_ref[at,:])
    def yblock(i):
        at=slice(i*C,i*C+C)
        us=L-C-i*C
        kb=jnp.where(lanes(C),k_ref[at,:],zero)
        y=y_ref.at[i%2]
        y[...]=dot_nt(kb,qr_ref[us:us+R+C,:])
        for g in range(C//16):
            rows=slice(16*g,16*g+16)
            part=y[rows,:].astype(bf)
            s_part=pltpu.roll(part,R+1+16*g,1,stride=1,stride_axis=0)[:,:R]
            yt_ref[i%2,rows,:]=s_part
        return yt_ref[i%2].T
    for i in range(L//C):
        acc_ref[:,i*C:i*C+C]=yblock(i)
    v_one=jnp.where(lanes(L),v_ref[...],one)
    own=lanes(B)
    sp=lane(B)==spare
    accs=[]
    for i in range(R//B):
        r0=i*B
        qm=q_ref[r0:r0+B,:]
        q=jnp.where(own,qm,zero)
        qs=jnp.where(sp,one,q)
        ws=R-B-r0
        x,s=x_ref.at[i%2],s_ref.at[i%2]
        x[...]=dot_nt(q,kt_ref[ws:ws+L+B,:])
        s[...]=dot_nt(qs,km_ref[...])
        rr=R-B-r0
        p=p_ref.at[i%2]
        for g in range(B//16):
            rows=slice(16*g,16*g+16)
            xr=pltpu.roll(x[rows,:],(L+1+16*g)%(L+B),1,stride=1,stride_axis=0)[:,:L]
            raw=s[rows,:]+xr+acc_ref[r0+16*g:r0+16*g+16,:].astype(f32)
            s[rows,:]=raw
            top=raw[:,:128]
            for j in range(1,L//128):
                top=jnp.maximum(top,raw[:,128*j:128*j+128])
            p[rows,:]=top
        p[...]=jnp.broadcast_to(jnp.max(p[...],axis=1,keepdims=True)*(SCALE*LOG2E),(B,128))
        for g in range(B//16):
            rows=slice(16*g,16*g+16)
            peak=jnp.concatenate([p[rows,:]]*(L//128),axis=1)
            e=jnp.exp2(s[rows,:]*(SCALE*LOG2E)-peak)
            e=flip_rows(e).astype(bf)
            to=rr+B-16-16*g
            e_ref[0,to:to+16,:]=e
        accs.append(dot_nn(e_ref[0,rr:rr+B,:],v_one))
    acc=jnp.concatenate(accs[::-1],axis=0)
    inv=1.0/pltpu.roll(acc,DH,1)
    J=flip_matrix(R)
    ctx=dot_nn(J,(acc*inv).astype(bf)).astype(bf)
    mine=lanes(R)
    inv_hi=inv.astype(bf)
    sc=dot_nn(J,inv_hi)+dot_nn(J,(inv-inv_hi.astype(f32)).astype(bf))
    sc=sc*SCALE
    @pl.when(hh==0)
    def _():
        ctx_ref[...]=ctx
        scale_ref[...]=sc
    @pl.when(hh==1)
    def _():
        ctx_ref[...]=jnp.where(mine,ctx,ctx_ref[...])
        scale_ref[...]=jnp.where(mine,sc,scale_ref[...])

def attention_forward(q,k,v,kt,qr,mask,B=128,C=256):
    R,F=q.shape; L=k.shape[0]; W=L+R; pairs=F//128
    B=min(B,R)
    col=lambda n: pl.BlockSpec((n,128),lambda p,h:(0,p))
    flops=2*pairs*2*R*L*128*4
    return pl.pallas_call(functools.partial(fwd_kernel,R,L,B,C),
        grid=(pairs,2),
        in_specs=[pl.BlockSpec((L,128),lambda p,h:(0,0)),col(R),col(L),col(L),col(W),col(W)],
        out_specs=[col(R),col(R),pl.BlockSpec((1,R,L),lambda p,h:(2*p+h,0,0))],
        out_shape=[jax.ShapeDtypeStruct((R,F),bf),jax.ShapeDtypeStruct((R,F),f32),jax.ShapeDtypeStruct((2*pairs,R,L),bf)],
        scratch_shapes=[pltpu.VMEM((2,C,R),bf),pltpu.VMEM((R,L),bf),pltpu.VMEM((L,128),bf),pltpu.VMEM((2,C,R+C),f32),
                        pltpu.VMEM((2,B,L),f32),pltpu.VMEM((2,B,L+B),f32),pltpu.VMEM((2,B,128),f32)],
        compiler_params=pltpu.CompilerParams(vmem_limit_bytes=48*1024*1024,dimension_semantics=("arbitrary","arbitrary")),
        cost_estimate=pl.CostEstimate(flops=flops,bytes_accessed=2*pairs*R*L*2+10*L*F,transcendentals=2*pairs*R*L),
        name="attend",
    )(mask,q,k,v,kt,qr)

def bwd_kernel(R,L,B,C,q_ref,k_ref,v_ref,do_ref,ctx_ref,e_ref,kr_ref,qrel_ref,ox_ref,oy_ref,
               dq_ref,dk_ref,dv_ref,dkr_ref,dqr_ref,ds_ref,dor_ref,qrev_ref,dqa_ref,dka_ref,dva_ref,
               delta_ref,dp_ref,wide_ref,dst_ref,wide2_ref):
    hh=pl.program_id(1)
    def lanes(n): return (lax.broadcasted_iota(jnp.int32,(n,128),1)//DH)==hh
    zero=jnp.zeros((),bf)
    @pl.when(hh==0)
    def _():
        dqa_ref[...]=jnp.zeros_like(dqa_ref)
        dka_ref[...]=jnp.zeros_like(dka_ref)
        dva_ref[...]=jnp.zeros_like(dva_ref)
        dkr_ref[...]=jnp.zeros_like(dkr_ref)
        dqr_ref[...]=jnp.zeros_like(dqr_ref)
    J=flip_matrix(R)
    do=jnp.where(lanes(R),dot_nn(J,do_ref[...]).astype(bf),zero)
    ctx=dot_nn(J,ctx_ref[...])
    dor_ref[...]=do
    qrev_ref[...]=jnp.where(lanes(R),dot_nn(J,q_ref[...]).astype(bf),zero)
    delta_ref[...]=jnp.broadcast_to(jnp.sum(do.astype(f32)*ctx,axis=1,keepdims=True),(R,128))
    own=lanes(B)
    for i in range(R//B):
        r0=i*B
        dp,wide=dp_ref.at[i%2],wide_ref.at[i%2]
        dp[...]=dot_nt(dor_ref[r0:r0+B,:],v_ref[...])
        for g in range(B//16):
            rows=slice(16*g,16*g+16)
            at=slice(r0+16*g,r0+16*g+16)
            delta=jnp.concatenate([delta_ref[at,:]]*(L//128),axis=1)
            ds=(e_ref[0,at,:].astype(f32)*(dp[rows,:]-delta)).astype(bf)
            ds_ref[at,:]=ds
            part=jnp.concatenate([ds,jnp.zeros((16,B),bf)],axis=1)
            wide[rows,:]=pltpu.roll(part,16*g,1,stride=1,stride_axis=0)
        db=dot_nn(wide[...],ox_ref[r0:r0+L+B,:]).astype(bf)
        dq=dot_nn(ds_ref[r0:r0+B,:],k_ref[...])+dot_nn(db,kr_ref[...])
        dqa_ref[r0:r0+B,:]=jnp.where(own,dq,dqa_ref[r0:r0+B,:])
        dkr_ref[...]+=dot_tn(db,qrev_ref[r0:r0+B,:])
    ownk=lanes(C)
    qrel=jnp.where(lanes(NB),qrel_ref[...],zero)
    for i in range(L//C):
        at=slice(i*C,i*C+C)
        dst,wide=dst_ref.at[i%2],wide2_ref.at[i%2]
        dst[...]=ds_ref[:,at].T
        for g in range(C//16):
            rows=slice(16*g,16*g+16)
            part=jnp.concatenate([dst[rows,:],jnp.zeros((16,C),bf)],axis=1)
            wide[rows,:]=pltpu.roll(part,16*g,1,stride=1,stride_axis=0)
        db=dot_nn(wide[...],oy_ref[i*C:i*C+R+C,:]).astype(bf)
        dka_ref[at,:]+=dot_nn(dst[...],qrev_ref[...])+dot_nn(db,qrel)
        dva_ref[at,:]+=dot_tn(e_ref[0,:,at],dor_ref[...])
        kb=jnp.where(ownk,k_ref[at,:],zero)
        dqr_ref[...]+=dot_tn(db,kb)
    @pl.when(hh==1)
    def _():
        dq_ref[...]=dot_nn(J,dqa_ref[...].astype(bf)).astype(bf)
        dk_ref[...]=dka_ref[...].astype(bf)
        dv_ref[...]=(dva_ref[...]*(1.0/SCALE)).astype(bf)

def attention_backward(q,k,v,do,ctx,e,key_rel,query_rel,onehot_x,onehot_y,p0=0,count=None,before=None,after=None,through=None,B=128,C=128):
    R,F=q.shape; L=k.shape[0]; W=L+R; pairs=F//128
    count=pairs if count is None else count
    B=min(B,R)
    col=lambda n: pl.BlockSpec((n,128),lambda p,h:(0,p0+p))
    full=pl.BlockSpec((W,NB),lambda p,h:(0,0))
    flops=2*count*2*R*L*128*8
    args=[q,k,v,do,ctx,e,key_rel,query_rel,onehot_x,onehot_y]
    specs=[col(R),col(L),col(L),col(R),col(R),pl.BlockSpec((1,R,L),lambda p,h:(2*(p0+p)+h,0,0)),col(NB),col(NB),full,full]
    n_in=len(args)
    through=list(through or [])
    extra=list(before or [])+through+list(after or [])
    n_before=len(before or [])
    body=functools.partial(bwd_kernel,R,L,B,C)
    def kernel(*refs):
        rest=refs[n_in+len(extra):]
        body(*refs[:n_in],*rest[:5],*rest[5+len(through):])
    return pl.pallas_call(kernel,
        grid=(count,2),
        in_specs=specs+[pl.BlockSpec(memory_space=pl.ANY)]*len(extra),
        out_specs=[col(R),col(L),col(L),col(NB),col(NB)]+[pl.BlockSpec(memory_space=pl.ANY)]*len(through),
        out_shape=[jax.ShapeDtypeStruct((R,F),bf),jax.ShapeDtypeStruct((L,F),bf),jax.ShapeDtypeStruct((L,F),bf),
                   jax.ShapeDtypeStruct((NB,F),f32),jax.ShapeDtypeStruct((NB,F),f32)]+[jax.ShapeDtypeStruct(x.shape,x.dtype) for x in through],
        input_output_aliases={**({n_in+i:i for i in range(5)} if before else {}),**{n_in+n_before+i:5+i for i in range(len(through))}},
        scratch_shapes=[pltpu.VMEM((R,L),bf),pltpu.VMEM((R,128),bf),pltpu.VMEM((R,128),bf),
                        pltpu.VMEM((R,128),f32),pltpu.VMEM((L,128),f32),pltpu.VMEM((L,128),f32),
                        pltpu.VMEM((R,128),f32),pltpu.VMEM((2,B,L),f32),pltpu.VMEM((2,B,L+B),bf),pltpu.VMEM((2,C,R),bf),pltpu.VMEM((2,C,R+C),bf)],
        compiler_params=pltpu.CompilerParams(vmem_limit_bytes=48*1024*1024,dimension_semantics=("arbitrary","arbitrary")),
        cost_estimate=pl.CostEstimate(flops=flops,bytes_accessed=2*count*R*L*2+20*L*128*count,transcendentals=0),
        name="attend_back",
    )(*args,*extra)

EPS=1e-6

def gelu_parts(v):
    a=jnp.abs(v)
    t=1.0/(1.0+(0.3275911/math.sqrt(2.0))*a)
    bell=jnp.exp(-0.5*v*v)
    poly=t*(0.127414796+t*(-0.142248368+t*(0.7107068705+t*(-0.7265760135+t*0.5307027145))))
    tail=poly*bell
    phi=jnp.where(v>0,1.0-tail,tail)
    return v*phi, phi+v*bell*(1.0/math.sqrt(2.0*math.pi))

class Both:
    def __init__(self,*copies):
        self.copies=copies

    def start(self):
        for copy in self.copies:
            copy.start()

    def wait(self):
        for copy in self.copies:
            copy.wait()

def feed_kernel(R,D,tiles,per,rows_in,own_rows,ctx_ref,tok_ref,og_ref,scale_ref,wo_ref,late_ref,bias_ref,gain_ref,shift_ref,
                res_ref,dres_ref,do_ref,sums_ref,bsum_ref,keep_ref,give_ref,
                u1_ref,r1_ref,low_ref,acc_ref,pre_ref,gated_ref,gp_ref,dfeed_ref,stage_ref,tail_ref,datt_ref,sem):
    step=pl.program_id(0)
    core=lax.axis_index("dp")%2
    pairs=per//2
    width=per*rows_in
    CH=64
    def chunks(f):
        def body(i,c):
            f(pl.ds(pl.multiple_of(i*CH,CH),CH))
            return c
        lax.fori_loop(0,R//CH,body,0)
    mean=lambda x: jnp.mean(x,axis=1,keepdims=True)
    gain=lambda i: gain_ref[i:i+1,:]
    shift=lambda i: shift_ref[i:i+1,:]
    def add_sum(i,x):
        sums_ref[i:i+1,:]+=jnp.sum(x,axis=0,keepdims=True)
    @pl.when(step==0)
    def _():
        sums_ref[...]=jnp.zeros_like(sums_ref)
        acc_ref[...]=dot_nn(ctx_ref[...],wo_ref[...])
        def norm(at):
            v=tok_ref[at,:].astype(f32)+acc_ref[at,:]+shift(0)
            c=v-mean(v)
            r=lax.rsqrt(mean(c*c)+EPS)
            u=c*r
            u1_ref[at,:]=u
            r1_ref[at,:]=jnp.broadcast_to(r,(CH,128))
            h=u*gain(0)+shift(1)
            low_ref[at,:]=h.astype(bf)
            acc_ref[at,:]=h+shift(2)
        chunks(norm)
    w_in=late_ref[:,0:rows_in,:].reshape(width,D)
    w_outer=late_ref[:,rows_in:2*rows_in,:].reshape(width,D)
    @pl.when(step<tiles)
    def _():
        pre_ref[...]=dot_nt(low_ref[...],w_in)
        def act(at):
            g,gp=gelu_parts(pre_ref[at,:]+bias_ref[0])
            gated_ref[step,at,:]=g.astype(bf)
            gp_ref[step,at,:]=gp.astype(bf)
        chunks(act)
        acc_ref[...]+=dot_nn(gated_ref[step],w_outer)
    @pl.when(step==tiles-1)
    def _():
        def norm(at):
            v=acc_ref[at,:]
            c=v-mean(v)
            r=lax.rsqrt(mean(c*c)+EPS)
            u=c*r
            res_ref[at,:]=(u*gain(1)+shift(3)).astype(bf)
            top=og_ref[at,:].astype(f32)
            add_sum(1,top*u)
            add_sum(5,top)
            e=top*gain(1)
            d=(e-mean(e)-u*mean(e*u))*r
            add_sum(4,d)
            dfeed_ref[at,:]=d.astype(bf)
            acc_ref[at,:]=d
        chunks(norm)
    @pl.when(step>=tiles)
    def _():
        k=step-tiles
        slot=lax.rem(k,2)
        pre_ref[...]=dot_nt(dfeed_ref[...],w_outer)
        def act(at):
            d=(pre_ref[at,:]*gp_ref[k,at,:].astype(f32)).astype(bf)
            gp_ref[k,at,:]=d
        chunks(act)
        bsum_ref[0]=jnp.sum(gp_ref[k].astype(f32),axis=0,keepdims=True)
        def out(kk,s):
            to=(pl.ds(kk*pairs,pairs),pl.ds(0,2*rows_in))
            return Both(pltpu.make_async_copy(stage_ref.at[s,:,core],keep_ref.at[to],sem.at[s,0]),
                        pltpu.make_async_copy(stage_ref.at[s,:,1-core],give_ref.at[to],sem.at[s,1]))
        @pl.when(k>=2)
        def _():
            out(k-2,slot).wait()
        stage_ref[slot,:,:,0:rows_in,:]=dot_tn(gp_ref[k],low_ref[...]).astype(bf).reshape(pairs,2,rows_in,D)
        stage_ref[slot,:,:,rows_in:2*rows_in,:]=dot_tn(gated_ref[k],dfeed_ref[...]).astype(bf).reshape(pairs,2,rows_in,D)
        out(k,slot).start()
        acc_ref[...]+=dot_nn(gp_ref[k],w_in)
        @pl.when(k==tiles-1)
        def _():
            def norm(at):
                d=acc_ref[at,:]
                u=u1_ref[at,:]
                r=r1_ref[at,0:1]
                add_sum(0,d*u)
                add_sum(3,d)
                e=d*gain(0)
                g=(e-mean(e)-u*mean(e*u))*r
                add_sum(2,g)
                dres_ref[at,:]=g
                datt_ref[at,:]=g.astype(bf)
            chunks(norm)
            do_ref[...]=(dot_nt(datt_ref[...],wo_ref[...])*scale_ref[...]).astype(bf)
            outer=dot_tn(ctx_ref[...],datt_ref[...])
            n=D//own_rows
            gap=tail_ref.shape[2]-own_rows
            for p in range(n):
                piece=outer[p*own_rows:p*own_rows+own_rows,:]
                if gap:
                    piece=jnp.concatenate([piece,jnp.zeros((gap,D),f32)],axis=0)
                tail_ref[p//2,p%2]=piece.astype(bf)
            to=(slice(None),pl.ds(2*rows_in,tail_ref.shape[2]))
            last=Both(pltpu.make_async_copy(tail_ref.at[:,core],keep_ref.at[to],sem.at[2,0]),
                      pltpu.make_async_copy(tail_ref.at[:,1-core],give_ref.at[to],sem.at[2,1]))
            last.start()
            if tiles>1:
                out(k-1,1-slot).wait()
            out(k,slot).wait()
            last.wait()

def feed(ctx,tokens,out_grad,scale,out_rows,late,bias,gain,shift,rows_in,own_rows,tiles=4):
    R,D=ctx.shape
    n,rows_late,_=late.shape
    per=n//tiles
    width=per*rows_in
    tail=rows_late-2*rows_in
    vm=lambda s: pl.BlockSpec(s,lambda i: (0,)*len(s))
    return pl.pallas_call(functools.partial(feed_kernel,R,D,tiles,per,rows_in,own_rows),
        grid=(2*tiles,),
        in_specs=[vm((R,D)),vm((R,D)),vm((R,D)),vm((R,D)),vm((D,D)),
                  pl.BlockSpec((per,rows_late,D),lambda i:(lax.rem(i,tiles),0,0)),
                  pl.BlockSpec((1,1,width),lambda i:(lax.rem(i,tiles),0,0)),vm((2,D)),vm((4,D))],
        out_specs=[vm((R,D)),vm((R,D)),vm((R,D)),vm((8,D)),pl.BlockSpec((1,1,width),lambda i:(jnp.maximum(i-tiles,0),0,0)),
                   pl.BlockSpec(memory_space=pl.ANY),pl.BlockSpec(memory_space=pl.ANY)],
        out_shape=[jax.ShapeDtypeStruct((R,D),bf),jax.ShapeDtypeStruct((R,D),f32),jax.ShapeDtypeStruct((R,D),bf),
                   jax.ShapeDtypeStruct((8,D),f32),jax.ShapeDtypeStruct((tiles,1,width),f32),
                   jax.ShapeDtypeStruct((n//2,rows_late,D),bf),jax.ShapeDtypeStruct((n//2,rows_late,D),bf)],
        scratch_shapes=[pltpu.VMEM((R,D),f32),pltpu.VMEM((R,128),f32),pltpu.VMEM((R,D),bf),pltpu.VMEM((R,D),f32),
                        pltpu.VMEM((R,width),f32),pltpu.VMEM((tiles,R,width),bf),pltpu.VMEM((tiles,R,width),bf),
                        pltpu.VMEM((R,D),bf),pltpu.VMEM((2,per//2,2,2*rows_in,D),bf),pltpu.VMEM((n//2,2,tail,D),bf),pltpu.VMEM((R,D),bf),
                        pltpu.SemaphoreType.DMA((3,2))],
        compiler_params=pltpu.CompilerParams(vmem_limit_bytes=58*1024*1024,dimension_semantics=("arbitrary",)),
        cost_estimate=pl.CostEstimate(flops=2*R*D*n*rows_in*6+6*R*D*D,bytes_accessed=4*n*rows_late*D+20*R*D,transcendentals=2*R*n*rows_in),
        name="feed",
    )(ctx,tokens,out_grad,scale,out_rows,late,bias,gain,shift)

MESH = pl.DeviceIdType.MESH
ANY = pl.BlockSpec(memory_space=pl.ANY)
VM = pl.BlockSpec(memory_space=pltpu.VMEM)

def remote(src, dst, send, recv, peer):
    return pltpu.make_async_remote_copy(src_ref=src, dst_ref=dst, send_sem=send, recv_sem=recv,
                                        device_id=peer, device_id_type=MESH)

def meet(peers):
    barrier = pltpu.get_barrier_semaphore()
    for peer in peers:
        pl.semaphore_signal(barrier, inc=1, device_id=peer, device_id_type=MESH)
    pl.semaphore_wait(barrier, len(peers))

class Place:
    def __init__(self, n_t, n_dp):
        self.n_t, self.n_dp = n_t, n_dp
        bits = (n_dp // 2).bit_length() - 1
        self.low = bits // 2
        self.high = bits - self.low
        dp, self.t = lax.axis_index("dp"), lax.axis_index("tensor")
        self.core = dp % 2
        self.down = (dp // 2) % 2**self.low
        self.up = dp // 2 // 2**self.low
        self.others = [lax.rem(self.t + 1 + i, n_t) for i in range(n_t - 1)]
        self.twin = {"dp": dp - self.core + 1 - self.core}
        self.steps = [("down", i) for i in range(self.low)] + [("up", i) for i in range(self.high)]

    def bit(self, step):
        kind, i = step
        return (getattr(self, kind) // 2**i) % 2

    def peer(self, step):
        kind, i = step
        turn = (1 - 2 * self.bit(step)) * 2**i
        down = self.down + turn if kind == "down" else self.down
        up = self.up + turn if kind == "up" else self.up
        return {"dp": (up * 2**self.low + down) * 2 + self.core}

    def peers(self):
        return [{"tensor": o} for o in self.others] + [self.twin] + [self.peer(s) for s in self.steps]

    def orders(self):
        down = [s for s in self.steps if s[0] == "down"]
        up = [s for s in self.steps if s[0] == "up"]
        return [down + up, up + down]

    def spans(self, done):
        out = []
        for kind in ("up", "down"):
            n = sum(1 for s in done if s[0] == kind)
            here = getattr(self, kind)
            out.append(pl.ds((here // 2**n) * 2**n, 2**n))
        return out

    def parts(self):
        half = self.n_t // 2
        return [pl.ds(0, half), pl.ds(half, half)] if half else [pl.ds(0, 1)]

class Line:
    def __init__(self, t, n, own, slot, rows, pieces, send, recv):
        self.t, self.n, self.own, self.slot = t, n, own, slot
        self.rows, self.pieces, self.send, self.recv = rows, pieces, send, recv

    def piece(self, ref, j):
        size = self.rows // self.pieces
        return ref.at[pl.ds(j * size, size)]

    def copy(self, d, s, j, b, own):
        at = self.piece(self.slot(b), j)
        src = self.piece(self.own, j) if own else at
        peer = {"tensor": self.t + 1 - 2 * d}
        return remote(src, at, self.send.at[d, s, j], self.recv.at[d, s, j], peer)

    def post(self, s, j):
        for d in range(2):
            b = self.t - s + 2 * d * s
            go_on = (b >= 0) & (self.t + 1 < self.n) if d == 0 else (b < self.n) & (self.t > 0)

            @pl.when(go_on)
            def _():
                self.copy(d, s, j, b, s == 0).start()

    def take(self, s, j):
        for d in range(2):
            b = self.t - 1 - s if d == 0 else self.t + 1 + s

            @pl.when(b >= 0 if d == 0 else b < self.n)
            def _():
                self.copy(d, s, j, b, False).wait_recv()

    def step(self, s):
        for j in range(self.pieces):
            self.take(s, j)
            if s + 1 < self.n - 1:
                self.post(s + 1, j)

    def drain(self):
        for s in range(self.n - 1):
            for j in range(self.pieces):
                for d in range(2):
                    b = self.t - s + 2 * d * s

                    @pl.when((b >= 0) & (self.t + 1 < self.n) if d == 0 else (b < self.n) & (self.t > 0))
                    def _():
                        self.copy(d, s, j, b, s == 0).wait_send()

def lanes_of(count, width, shape, tall):
    wide_axis = 0 if tall else 1
    f = lax.broadcasted_iota(jnp.int32, shape, wide_axis)
    r = lax.broadcasted_iota(jnp.int32, shape, 1 - wide_axis)
    return jnp.where(f % count == r, 1.0, 0.0).astype(bf)

def spread_row(table, count, width, first):
    n = table.shape[0]
    full = dot_nn(table.astype(bf), lanes_of(count, width, (128, width), False))
    p = lax.broadcasted_iota(jnp.int32, (n, width), 0)
    f = lax.broadcasted_iota(jnp.int32, (n, width), 1)
    return jnp.sum(jnp.where(first + f // count == p, full, 0.0), axis=0, keepdims=True)

def fold_row(row, count, n, first):
    width = row.shape[1]
    p = lax.broadcasted_iota(jnp.int32, (n, width), 0)
    f = lax.broadcasted_iota(jnp.int32, (n, width), 1)
    full = jnp.where(first + f // count == p, jnp.broadcast_to(row, (n, width)), 0.0)
    return dot_nn(full.astype(bf), lanes_of(count, width, (width, 128), True))

def eight(n):
    return -(-n // 8) * 8

def begin_kernel(n_t, n_dp, own, part, cols, inner, tiles, L,
                 tok_ref, wq_ref, wk_ref, wv_ref, rel_ref, qkvb_ref, ffb_ref, gains_ref, shifts_ref, ahead_ref, back_ref, late_ref,
                 q_out, k_out, v_out, krel_out, qrel_out, kt_out, qr_out, toks_out, w_out, ox_out, oy_out, table_out, late_all,
                 ibias_ref, gain_ref, shift_ref,
                 toks, packs, pack, packf, wf, w, kb, vb, qb, krel, qrel, kt, qr, table, tableb, miscf, ox, ox_tall, oy_tall,
                 tok_send, tok_recv, z_send, z_recv, x_send, x_recv, out_sem, lz_send, lz_recv, lx_send, lx_recv, lc_send, lc_recv):
    at = Place(n_t, n_dp)
    t = at.t
    R, D = tok_ref.shape
    W = L + R
    n_all = n_t * n_dp
    S, S2 = eight(own), eight(part)
    misc = 3 * S + S2

    packf[...] = jnp.zeros_like(packf)
    for i, ref in enumerate((wq_ref, wk_ref, wv_ref)):
        packf[i * S:i * S + own, :] = ref[...].astype(f32)
    for i in range(n_t):
        @pl.when(t == i)
        def _():
            packf[3 * S:3 * S + part, :] = rel_ref[...].astype(f32)[i * part:(i + 1) * part]
    for i in range(3):
        packf[misc:misc + 1, 128 * i:128 * i + own] = qkvb_ref[i:i + 1, :].astype(f32)
    packf[misc:misc + 1, 384:384 + inner] = ffb_ref[...].astype(f32)
    for i in range(2):
        packf[misc + 1:misc + 2, 128 * i:128 * i + cols] = gains_ref[i:i + 1, :].astype(f32)
    for i in range(4):
        packf[misc + 1:misc + 2, 256 + 128 * i:256 + 128 * i + cols] = shifts_ref[i:i + 1, :].astype(f32)
    pack[...] = packf[...].astype(bf)

    meet(at.peers())
    copies = []

    def go(copy):
        copy.start()
        copies.append(copy)
        return copy

    here = packs.at[t, at.up, at.down, at.core]
    column = Line(t, n_t, pack, lambda i: packs.at[i, at.up, at.down, at.core], pack.shape[0], 1, z_send, z_recv)
    tokens = Line(t, n_t, tok_ref, lambda i: toks.at[i], R, 2, tok_send, tok_recv)
    late = Line(t, n_t, late_ref, lambda i: late_all.at[i, at.up, at.down, at.core], late_ref.shape[0], 1, lz_send, lz_recv)
    column.post(0, 0)
    late.post(0, 0)
    own_late = pltpu.make_async_copy(late_ref, late_all.at[t, at.up, at.down, at.core], out_sem.at[out_sem.shape[0] - 1])
    own_late.start()
    own_pack = pltpu.make_async_copy(pack, here, out_sem.at[0])
    own_pack.start()
    outs = []

    def put(src, dst):
        copy = pltpu.make_async_copy(src, dst, out_sem.at[1 + len(outs)])
        copy.start()
        outs.append(copy)

    def pick(line, start):
        rows = line[:, pl.ds(pl.multiple_of(start, 128), W)]
        ids = lax.broadcasted_iota(jnp.int32, (NB, W), 0)
        return jnp.where(ids == rows, 1.0, 0.0).astype(bf)

    ox[...] = pick(back_ref, L - R - R * t)
    ox_tall[...] = ox[...].T
    oy_tall[...] = pick(ahead_ref, L - R - R * t).T
    put(ox_tall, ox_out)
    put(oy_tall, oy_out)

    for s in range(n_t - 1):
        column.step(s)
        if s < n_t - 2:
            late.step(s)
        if s == n_t - 3 or n_t < 3:
            for j in range(2):
                tokens.post(0, j)
    own_pack.wait()
    parts, orders = at.parts(), at.orders()
    n_steps = len(at.steps)
    swaps = {}

    def swap(h, k):
        if k:
            swaps[h, k - 1].wait_recv()
        up, down = at.spans(orders[h][:k])
        if k < n_steps:
            piece, peer = packs.at[parts[h], up, down, at.core], at.peer(orders[h][k])
        else:
            piece, peer = packs.at[parts[h], :, :, at.core], at.twin
        swaps[h, k] = go(remote(piece, piece, x_send.at[h, k], x_recv.at[h, k], peer))

    hs = range(len(parts))
    moves = {}

    def late_twin(h, k):
        up, down = at.spans(orders[h][:k])
        if k:
            kind, i = orders[h][k - 1]
            base = (getattr(at, kind) // 2**(i + 1)) * 2**(i + 1)
            other = pl.ds(base + (1 - at.bit((kind, i))) * 2**i, 2**i)
            up, down = (other, down) if kind == "up" else (up, other)
        piece = late_all.at[parts[h], up, down, at.core]
        moves[h, k, "twin"] = go(remote(piece, piece, lc_send.at[h, k], lc_recv.at[h, k], at.twin))

    def late_swap(k):
        for h in hs:
            if k:
                moves[h, k - 1, "swap"].wait_recv()
            if k < n_steps:
                up, down = at.spans(orders[h][:k])
                piece = late_all.at[parts[h], up, down, at.core]
                moves[h, k, "swap"] = go(remote(piece, piece, lx_send.at[h, k], lx_recv.at[h, k], at.peer(orders[h][k])))
            late_twin(h, k)

    for h in hs:
        swap(h, 0)
    late.step(n_t - 2)
    own_late.wait()
    late_swap(0)
    passed = 0
    for k in range(1, n_steps + 1):
        for h in hs:
            swap(h, k)
    if n_t > 2:
        tokens.step(0)
        passed = 1
    for h in hs:
        swaps[h, n_steps].wait_recv()

    slots = [(a, u, d, c) for a in range(n_t) for u in range(2**at.high) for d in range(2**at.low) for c in range(2)]
    for i in range(3):
        for p, s in enumerate(slots):
            wf[p * own:p * own + own, :] = packs[s[0], s[1], s[2], s[3], i * S:i * S + own, :].astype(f32)
        w[i] = wf[...].astype(bf)
    put(w, w_out)
    for p, s in enumerate(slots):
        rows = packs[s[0], s[1], s[2], s[3], misc:misc + 8, :].astype(f32)
        miscf[0, p:p + 1, :] = rows[0:1]
        miscf[1, p:p + 1, :] = rows[1:2]
        a, dp = p // n_dp, p % n_dp
        to = dp * n_t * part + a * part
        table[to:to + part, :] = packs[s[0], s[1], s[2], s[3], 3 * S:3 * S + part, :].astype(f32)
    if n_steps:
        late_swap(1)
    bias = [spread_row(miscf[0, :, 128 * i:128 * i + 128], own, D, 0) for i in range(3)]
    rel = table[...].astype(bf)
    tableb[...] = rel
    put(tableb, table_out)
    krel[...] = (dot_nt(rel, w[1]) + bias[1]).astype(bf)
    qrel[...] = (dot_nt(rel, w[0]) + bias[0]).astype(bf)
    put(krel, krel_out)
    put(qrel, qrel_out)
    kt[...] = dot_tn(ox[...], krel[...]).astype(bf)
    put(kt, kt_out)
    qr[...] = dot_tn(pick(back_ref, R * t), qrel[...]).astype(bf)
    put(qr, qr_out)
    if n_t > 3:
        tokens.step(1)
        passed = 2

    def project(tokens, i):
        return (dot_nt(tokens, w[i]) + bias[i]).astype(bf)

    qb[...] = project(tok_ref[...], 0)
    put(qb, q_out)
    width = n_all * inner // tiles
    for i in range(tiles):
        ibias_ref[i] = spread_row(miscf[0, :, 384:512], inner, width, i * (n_all // tiles))
    for i in range(2):
        gain_ref[i:i + 1, :] = spread_row(miscf[1, 0:n_dp, 128 * i:128 * i + 128], cols, D, 0)
    for i in range(4):
        shift_ref[i:i + 1, :] = spread_row(miscf[1, 0:n_dp, 256 + 128 * i:384 + 128 * i], cols, D, 0)

    for s in range(n_t):
        b = lax.rem(t - s + n_t, n_t)
        rows = pl.ds(pl.multiple_of(b * R, R), R)
        if s == 1:
            for k in range(2, n_steps + 1):
                late_swap(k)
            for i in range(passed, n_t - 1):
                tokens.step(i)
        src = tok_ref if s == 0 else toks.at[b]
        put(src, toks_out.at[b])
        kb[s] = project(src[...], 1)
        put(kb.at[s], k_out.at[rows])
        vb[s] = project(src[...], 2)
        put(vb.at[s], v_out.at[rows])
    for h in hs:
        for k in range(n_steps + 1):
            moves[h, k, "twin"].wait_recv()
    for copy in outs:
        copy.wait()
    for copy in copies:
        copy.wait_send()
    column.drain()
    late.drain()
    tokens.drain()

def begin(tokens, w_query, w_key, w_value, rel_table, qkv_bias, ff_bias, gains, shifts, ahead, back, late, n_t, n_dp, tiles):
    R, D = tokens.shape
    L = ahead.shape[1] // 2
    W = L + R
    own, inner, cols = w_query.shape[0], ff_bias.shape[1], gains.shape[1]
    part = rel_table.shape[0] // n_t
    n_all = n_t * n_dp
    width = n_all * inner // tiles
    PR = -(-(3 * eight(own) + eight(part) + 8) // 16) * 16
    bits = (n_dp // 2).bit_length() - 1
    low = bits // 2
    S = jax.ShapeDtypeStruct
    big = [(R, D), (L, D), (L, D), (NB, D), (NB, D), (W, D), (W, D), (n_t, R, D), (3, D, D), (W, NB), (W, NB), (NB, D),
           (n_t, 2**(bits - low), 2**low, 2, late.shape[0], D)]
    v = lambda s, t=bf: pltpu.VMEM(s, t)
    dma = lambda *s: pltpu.SemaphoreType.DMA(s)
    return pl.pallas_call(
        functools.partial(begin_kernel, n_t, n_dp, own, part, cols, inner, tiles, L),
        out_shape=[S(s, bf) for s in big] + [S((tiles, 1, width), f32), S((2, D), f32), S((4, D), f32)],
        in_specs=[VM] * 11 + [ANY], out_specs=[ANY] * len(big) + [VM] * 3,
        scratch_shapes=[v((n_t, R, D)), v((n_t, 2**(bits - low), 2**low, 2, PR, D)), v((PR, D)), v((PR, D), f32), v((D, D), f32),
                        v((3, D, D)), v((n_t, R, D)), v((n_t, R, D)), v((R, D)), v((NB, D)), v((NB, D)), v((W, D)), v((W, D)),
                        v((NB, D), f32), v((NB, D)), v((2, n_all, D), f32), v((NB, W)), v((W, NB)), v((W, NB)),
                        dma(2, n_t - 1, 2), dma(2, n_t - 1, 2), dma(2, n_t - 1, 1), dma(2, n_t - 1, 1), dma(2, bits + 1), dma(2, bits + 1),
                        dma(11 + 3 * n_t), dma(2, n_t - 1, 1), dma(2, n_t - 1, 1), dma(2, max(bits, 1)), dma(2, max(bits, 1)), dma(2, bits + 1), dma(2, bits + 1)],
        compiler_params=pltpu.CompilerParams(collective_id=0, has_side_effects=True, vmem_limit_bytes=58 * 1024 * 1024),
        name="begin",
    )(tokens, w_query, w_key, w_value, rel_table, qkv_bias, ff_bias, gains, shifts, ahead, back, late)

def finish_kernel(n_t, n_dp, own, rel_rows, cols, inner, tiles,
                  dq_in, dk_in, dv_in, tok_in, toks_in, w_in, table_in, dqr_in, dkr_in, dres_in, sums_ref, bsum_ref,
                  tg_ref, gq_ref, gk_ref, gv_ref, rel_ref, qkvb_ref, ffb_ref, gains_ref, shifts_ref,
                  dq, dk, dv, tok, toks, w, table, dqr, dkr, dres, g, relf, m0, m1, miscs, pack, first, acc, got, total,
                  tok_got, tok_acc, tok_own, base, *rest):
    at = Place(n_t, n_dp)
    t = at.t
    n_steps = len(at.steps)
    bufs, (in_sem, tok_send, tok_recv, x_send, x_recv, z_send, z_recv) = rest[:2 * n_steps], rest[2 * n_steps:]
    R, D = tok.shape
    L = n_t * R
    n_all = n_t * n_dp
    S, S3 = eight(own), eight(rel_rows)
    misc = 3 * S
    PR = pack.shape[4]
    right = {"tensor": lax.rem(t + 1, n_t)}
    loads = []

    def load(src, dst):
        copy = pltpu.make_async_copy(src, dst, in_sem.at[len(loads)])
        copy.start()
        loads.append(copy)
        return copy

    def block(s):
        return lax.rem(t - 1 - s + 2 * n_t, n_t)

    l_w = load(w_in, w)
    l_kv = []
    for s in range(n_t):
        b = block(s)
        l_kv.append((load(dk_in.at[b], dk.at[b]), load(dv_in.at[b], dv.at[b])))
    l_toks = load(toks_in, toks)
    l_rest = [load(tok_in, tok), load(dq_in, dq), load(table_in, table), load(dqr_in, dqr), load(dkr_in, dkr), load(dres_in, dres)]
    meet(at.peers())
    copies = []

    def go(copy):
        copy.start()
        copies.append(copy)
        return copy

    half = R // 2
    token = {}

    def partial(s):
        for copy in l_kv[s]:
            copy.wait()
        b = block(s)
        return dot_nn(dk[b], w[1]) + dot_nn(dv[b], w[2])

    def send_token(s):
        for j in range(2):
            rows = pl.ds(j * half, half)
            if s:
                token[s - 1, j].wait_recv()
                tok_acc[s, rows] = (tok_own[rows].astype(f32) + tok_got[s - 1, rows].astype(f32)).astype(bf)
            token[s, j] = go(remote(tok_acc.at[s, rows], tok_got.at[s, rows], tok_send.at[s, j], tok_recv.at[s, j], right))

    l_w.wait()
    tok_acc[0] = partial(0).astype(bf)
    send_token(0)
    blocks = [None] * n_t
    tok_own[...] = partial(1).astype(bf)

    for s in range(2, n_t):
        for copy in l_kv[s]:
            copy.wait()
    l_kv = [()] * n_t
    l_toks.wait()
    for copy in l_rest:
        copy.wait()
    dqb, dkb = dqr[...].astype(bf), dkr[...].astype(bf)
    rel_table = table[...]
    g[0] = dot_tn(dq[...], tok[...]) + dot_tn(dqb, rel_table)
    g[1] = dot_tn(dk[...].reshape(L, D), toks[...].reshape(L, D)) + dot_tn(dkb, rel_table)
    g[2] = dot_tn(dv[...].reshape(L, D), toks[...].reshape(L, D))
    relf[...] = dot_nn(dqb, w[0]) + dot_nn(dkb, w[1])
    ones = lambda n: jnp.ones((8, n), bf)
    columns = [dot_nn(ones(R), dq[...])[0:1] + jnp.sum(dqr[...], axis=0, keepdims=True),
               dot_nn(ones(L), dk[...].reshape(L, D))[0:1] + jnp.sum(dkr[...], axis=0, keepdims=True),
               dot_nn(ones(L), dv[...].reshape(L, D))[0:1]]
    for i in range(3):
        m0[:, 128 * i:128 * i + 128] = fold_row(columns[i], own, n_all, 0)
    units = jnp.zeros((n_all, 128), f32)
    for i in range(tiles):
        units += fold_row(bsum_ref[i], inner, n_all, i * (n_all // tiles))
    m0[:, 384:512] = units
    for i in range(6):
        m1[:, 128 * i:128 * i + 128] = fold_row(sums_ref[i:i + 1, :], cols, n_dp, 0)
    miscs[...] = jnp.zeros_like(miscs)
    slots = [(a, u, d, c) for a in range(n_t) for u in range(2**at.high) for d in range(2**at.low) for c in range(2)]

    def padded(x, n):
        return jnp.concatenate([x, jnp.zeros((n - x.shape[0], D), f32)], axis=0) if n > x.shape[0] else x

    for p, s in enumerate(slots):
        dp = p % n_dp
        miscs[8 * p:8 * p + 1, 0:512] = m0[p:p + 1, :]
        miscs[8 * p + 1:8 * p + 2, :] = m1[dp:dp + 1, :]
        pieces = [padded(g[i, p * own:p * own + own, :], S) for i in range(3)]
        pieces += [miscs[8 * p:8 * p + 8, :], padded(relf[dp * rel_rows:dp * rel_rows + rel_rows, :], S3)]
        whole = padded(jnp.concatenate(pieces, axis=0), PR)
        pack[s[0], s[1], s[2], s[3]] = whole.astype(bf)

    parts = at.parts()
    hs = range(len(parts))
    per = n_t // len(parts)
    orders = [list(reversed(o)) for o in at.orders()][:len(parts)]
    swaps = {}
    left = {h: {"up": at.high, "down": at.low} for h in hs}

    def region(h, cut=None):
        out = []
        for kind in ("up", "down"):
            n = left[h][kind]
            here = getattr(at, kind)
            if cut is not None and cut[0] == kind:
                start = (here // 2**n) * 2**n + (1 - at.bit(cut)) * 2**(n - 1)
                out.append((start, 2**(n - 1)))
            else:
                out.append(((here // 2**n) * 2**n, 2**n))
        return out

    def start(h, k):
        if k == 0:
            src, dst, peer = pack.at[parts[h], :, :, 1 - at.core], first.at[parts[h]], at.twin
        else:
            cut = orders[h][k - 1]
            up, down = [pl.ds(*x) for x in region(h, cut)]
            src, dst, peer = acc.at[parts[h], up, down], bufs[h * n_steps + k - 1], at.peer(cut)
        swaps[h, k] = go(remote(src, dst, x_send.at[h, k], x_recv.at[h, k], peer))

    def absorb(h, k):
        swaps[h, k].wait_recv()
        if k:
            left[h][orders[h][k - 1][0]] -= 1
        (u0, nu), (d0, nd) = region(h)
        buf = first if k == 0 else bufs[h * n_steps + k - 1]

        @pl.loop(0, per * nu * nd)
        def _(m):
            a, u, d = m // (nu * nd), m // nd % nu, m % nd
            if k == 0:
                x, y = pack[h * per + a, u, d, at.core], buf[h * per + a, u, d]
            else:
                x, y = acc[h * per + a, u0 + u, d0 + d], buf[a, u, d]
            acc[h * per + a, u0 + u, d0 + d] = (x.astype(f32) + y.astype(f32)).astype(bf)

    for h in hs:
        start(h, 0)
    sent = 1
    if n_t > 2:
        send_token(1)
        sent = 2
        tok_own[...] = partial(2).astype(bf)
    base[...] = partial(n_t - 1) + dres[...] + dot_nn(dq[...], w[0])
    for k in range(n_steps + 1):
        for h in hs:
            absorb(h, k)
            if k < n_steps:
                start(h, k + 1)
        if k == n_steps:
            ring = [go(remote(acc.at[o, at.up, at.down], got.at[i], z_send.at[i], z_recv.at[i], {"tensor": o}))
                    for i, o in enumerate(at.others)]
        if k and sent < n_t - 1:
            send_token(sent)
            sent += 1
            if sent < n_t - 1:
                tok_own[...] = partial(sent).astype(bf)
    for copy in ring:
        copy.wait_recv()
    total[...] = acc[t, at.up, at.down].astype(f32)
    for i in range(n_t - 1):
        total[...] += got[i].astype(f32)
    for i, ref in enumerate((gq_ref, gk_ref, gv_ref)):
        ref[...] = total[i * S:i * S + own, :]
    rel_ref[...] = total[misc + 8:misc + 8 + rel_rows, :]
    for i in range(3):
        qkvb_ref[i:i + 1, :] = total[misc:misc + 1, 128 * i:128 * i + own]
    ffb_ref[...] = total[misc:misc + 1, 384:384 + inner]
    for i in range(2):
        gains_ref[i:i + 1, :] = total[misc + 1:misc + 2, 128 * i:128 * i + cols]
    for i in range(4):
        shifts_ref[i:i + 1, :] = total[misc + 1:misc + 2, 256 + 128 * i:256 + 128 * i + cols]
    while sent < n_t - 1:
        send_token(sent)
        sent += 1
        if sent < n_t - 1:
            tok_own[...] = partial(sent).astype(bf)
    for j in range(2):
        rows = pl.ds(j * half, half)
        token[n_t - 2, j].wait_recv()
        tg_ref[rows, :] = base[rows, :] + tok_got[n_t - 2, rows].astype(f32)
    for copy in copies:
        copy.wait_send()

def finish(dq, dk, dv, tok, toks, w, table, dqr, dkr, dres, sums, bsum, own, rel_rows, cols, inner, n_t, n_dp):
    R, D = tok.shape
    L = n_t * R
    n_all = n_t * n_dp
    tiles = bsum.shape[0]
    S3 = eight(rel_rows)
    PR = -(-(3 * eight(own) + 8 + S3) // 16) * 16
    bits = (n_dp // 2).bit_length() - 1
    low = bits // 2
    high = bits - low
    per = n_t // 2
    v = lambda s, x=bf: pltpu.VMEM(s, x)
    dma = lambda *s: pltpu.SemaphoreType.DMA(s)
    bufs = []
    for order in ([("up", high), ("down", low)], [("down", low), ("up", high)]):
        left = {"up": high, "down": low}
        for kind, n in order:
            for _ in range(n):
                left[kind] -= 1
                bufs.append(v((per, 2**left["up"], 2**left["down"], PR, D)))
    S = jax.ShapeDtypeStruct
    outs = [(R, D), (own, D), (own, D), (own, D), (rel_rows, D), (3, own), (1, inner), (2, cols), (4, cols)]
    blocks = lambda x: x.reshape(n_t, R, D)
    return pl.pallas_call(
        functools.partial(finish_kernel, n_t, n_dp, own, rel_rows, cols, inner, tiles),
        out_shape=[S(s, f32) for s in outs],
        in_specs=[ANY] * 10 + [VM] * 2, out_specs=[VM] * len(outs),
        scratch_shapes=[v((R, D)), v((n_t, R, D)), v((n_t, R, D)), v((R, D)), v((n_t, R, D)), v((3, D, D)), v((NB, D)),
                        v((NB, D), f32), v((NB, D), f32), v((R, D), f32), v((3, D, D), f32), v((NB, D), f32),
                        v((n_all, 512), f32), v((n_dp, D), f32), v((8 * n_all, D), f32),
                        v((n_t, 2**high, 2**low, 2, PR, D)), v((n_t, 2**high, 2**low, PR, D)), v((n_t, 2**high, 2**low, PR, D)),
                        v((n_t - 1, PR, D)), v((PR, D), f32),
                        v((n_t - 1, R, D)), v((n_t - 1, R, D)), v((R, D)), v((R, D), f32)] + bufs
                       + [dma(2 * n_t + 8), dma(n_t - 1, 2), dma(n_t - 1, 2), dma(2, bits + 1), dma(2, bits + 1), dma(n_t - 1), dma(n_t - 1)],
        compiler_params=pltpu.CompilerParams(collective_id=1, has_side_effects=True, vmem_limit_bytes=60 * 1024 * 1024),
        name="finish",
    )(dq, blocks(dk), blocks(dv), tok, blocks(toks), w, table, dqr, dkr, dres, sums, bsum)

GROUPS, TILES = 32, 4
ALL=("tensor","dp")

def fold(name, grid, place, terms, shapes, out_maps):
    tail = terms[0][0].shape[-2:]
    block = lambda x, where: pl.BlockSpec((1,) * (len(x.shape) - 2) + tail, lambda *i: tuple(where(*i)) + (0, 0))
    n = len(terms)

    def kernel(place_ref, *refs):
        for k in range(n):
            x, y, out = refs[2 * k], refs[2 * k + 1], refs[2 * n + k]
            out[...] = (x[...].astype(f32) + y[...].astype(f32)).reshape(out.shape).astype(bf)

    outs = [jax.ShapeDtypeStruct(s + tail, bf) for s in shapes]
    return pl.pallas_call(
        kernel, out_shape=outs,
        grid_spec=pltpu.PrefetchScalarGridSpec(
            num_scalar_prefetch=1, grid=grid,
            in_specs=[block(z, where) for x, y, where in terms for z in (x, y)],
            out_specs=[block(o, where) for o, where in zip(outs, out_maps)]),
        compiler_params=pltpu.CompilerParams(vmem_limit_bytes=32 * 1024 * 1024, dimension_semantics=("arbitrary",) * len(grid)),
        cost_estimate=pl.CostEstimate(flops=0, bytes_accessed=sum(6 * math.prod(o.shape) for o in outs), transcendentals=0),
        name=name,
    )(place, *[z for x, y, _ in terms for z in (x, y)])

def finish_plain(dq, dk, dv, tok, toks, w, table, dqr, dkr, dres, sums, bsum, own, rel_rows, cols, inner, n_t, n_dp):
    times = lambda s, a, b: jnp.einsum(s, a.astype(bf), b.astype(bf), preferred_element_type=f32)
    scatter = lambda x: lax.psum_scatter(x, ALL, scatter_dimension=0, tiled=True)
    grads = [times("tf,td->fd", dq, tok) + times("tf,td->fd", dqr, table),
             times("tf,td->fd", dk, toks) + times("tf,td->fd", dkr, table), times("tf,td->fd", dv, toks)]
    rel = times("bf,fd->bd", dqr, w[0]) + times("bf,fd->bd", dkr, w[1])
    spread = (times("tf,fd->td", dk, w[1]) + times("tf,fd->td", dv, w[2])).astype(bf)
    back_sum = lax.psum_scatter(spread, "tensor", scatter_dimension=0, tiled=True).astype(f32)
    tokens_grad = dres + times("tf,fd->td", dq, w[0]) + back_sum
    column = lambda x: jnp.sum(x.astype(f32), axis=0)
    bias = jnp.stack([column(dq) + column(dqr), column(dk) + column(dkr), column(dv)])
    every = lambda x: lax.psum(x, ALL)
    dp = lax.axis_index("dp")
    place = lax.axis_index("tensor") * n_dp + dp
    cut = lambda x, i, n: lax.dynamic_slice_in_dim(x, i * n, n, 1)
    rel = lax.dynamic_slice_in_dim(every(rel), dp * rel_rows, rel_rows, 0)
    return [tokens_grad] + [scatter(x) for x in grads] + [rel, cut(every(bias), place, own), cut(every(bsum.reshape(1, -1)), place, inner),
            cut(every(sums[:2]), dp, cols), cut(every(sums[2:6]), dp, cols)]

def local(tokens, w_query, w_key, w_value, w_out, qkv_bias, w_ff_in, w_ff_out, ff_bias, rel_table,
          gains, shifts, rel_bucket, lengths, out_grad):
    D = tokens.shape[1]
    n_t, n_dp = lax.axis_size("tensor"), lax.axis_size("dp")
    n_all = n_t * n_dp
    t = lax.axis_index("tensor")
    R = tokens.shape[0]
    L = (rel_bucket.shape[0] + 1) // 2
    W = L + R
    own_rows, cols, inner = w_query.shape[0], gains.shape[1], ff_bias.shape[0]
    none = jnp.full((1,), -1, jnp.int32)
    ahead = jnp.concatenate([rel_bucket, none])[None]
    back = jnp.concatenate([rel_bucket[::-1], none])[None]
    late_rows = w_ff_in.shape[0]
    even = late_rows % 16 == 0 and own_rows % 8 == 0
    late = jnp.concatenate([w_ff_in, w_ff_out, w_out], axis=0)
    late_own = late.shape[0]
    late = jnp.pad(late, ((0, -late_own % 16), (0, 0)))
    (query, key, value, key_rel, query_rel, key_table, query_table, gathered, weights, pick_x, pick_y, table,
     late_all, inner_bias, gain, shift) = begin(tokens, w_query, w_key, w_value, rel_table, qkv_bias, ff_bias.reshape(1, -1), gains, shifts,
                                      ahead, back, late, n_t, n_dp, TILES)
    gathered = gathered.reshape(L, D)
    late_all = late_all.reshape(n_all, -1, D)
    cut = lambda x, at, n: x[:, at:at + n].reshape(n_all * n, D)
    out_rows = cut(late_all, 2 * late_rows, own_rows)
    groups = n_all if even else GROUPS
    group_rows, group_own = n_all * late_rows // groups, D // groups
    if not even:
        sections = [cut(late_all, 0, late_rows), cut(late_all, late_rows, late_rows)]
        late_all = jnp.concatenate([x.reshape(groups, group_rows, D) for x in sections]
                                   + [jnp.zeros((groups, -(-group_own // 16) * 16, D), bf)], axis=1)
    mask = jnp.where(jnp.arange(L, dtype=jnp.int32) < lengths[0], 0.0, -1e9).astype(bf)
    mask = jnp.broadcast_to(mask[:, None], (L, 128))

    context, scale, shares = attention_forward(query, key, value, key_table, query_table, mask)
    layer_result_rows, d_resid_one, d_scaled, sums, bias_sums, keep, give = feed(
        context, tokens, out_grad, scale, out_rows, late_all, inner_bias, gain, shift, group_rows, group_own)
    back_args = (query, key, value, d_scaled, context, shares, key_rel, query_rel, pick_x, pick_y)
    pairs = D // 128
    if even and n_dp == 8 and n_t % 2 == 0 and pairs >= 4:
        dp = lax.axis_index("dp")
        place = jnp.stack([dp // 4, dp // 2 % 2]).astype(jnp.int32)
        swap = lambda x, mask: lax.ppermute(x, "dp", [(i, i ^ mask) for i in range(n_dp)])
        shape = (n_t, 2, 2, late.shape[0], D)
        keep, give = keep.reshape(shape), give.reshape(shape)
        got = swap(give, 1)
        half = n_t // 2
        *grads, keep = attention_backward(*back_args, p0=0, count=pairs - 4, through=[keep])
        stay_one, away_one, stay_two, away_two = fold(
            "fold", (half, 2), place,
            [(keep, got, lambda i, j, s: (i, s[0], j)), (keep, got, lambda i, j, s: (i, 1 - s[0], j)),
             (keep, got, lambda i, j, s: (half + i, j, s[1])), (keep, got, lambda i, j, s: (half + i, j, 1 - s[1]))],
            [(half, 2)] * 4, [lambda i, j, s: (i, j)] * 4)
        got_one, got_two = swap(away_one, 4), swap(away_two, 2)
        *grads, stay_one, stay_two = attention_backward(
            *back_args, p0=pairs - 4, count=2, before=grads, after=[away_one, away_two], through=[stay_one, stay_two])
        stay_one, away_one, stay_two, away_two = fold(
            "fold", (half,), place,
            [(stay_one, got_one, lambda i, s: (i, s[1])), (stay_one, got_one, lambda i, s: (i, 1 - s[1])),
             (stay_two, got_two, lambda i, s: (i, s[0])), (stay_two, got_two, lambda i, s: (i, 1 - s[0]))],
            [(half,)] * 4, [lambda i, s: (i,)] * 4)
        got_one, got_two = swap(away_one, 2), swap(away_two, 4)
        *grads, stay_one, stay_two = attention_backward(
            *back_args, p0=pairs - 2, count=1, before=grads, after=[away_one, away_two], through=[stay_one, stay_two])
        column = jnp.concatenate(fold(
            "fold", (half,), place,
            [(stay_one, got_one, lambda i, s: (i,)), (stay_two, got_two, lambda i, s: (i,))],
            [(half,)] * 2, [lambda i, s: (i,)] * 2), axis=0)
        late_sum = lax.psum_scatter(column, "tensor", scatter_dimension=0, tiled=True)[0]
        grads = attention_backward(*back_args, p0=pairs - 1, count=1, before=grads, after=[column])
    else:
        grads = attention_backward(*back_args)
        core = lax.axis_index("dp") % 2
        late_grad = jnp.where(core == 0, jnp.stack([keep, give], axis=1), jnp.stack([give, keep], axis=1))
        late_grad = late_grad.reshape(groups, -1, D)
        parted = lambda x: x.reshape(n_all, -1, D)
        if not even:
            late_grad = jnp.concatenate([
                parted(late_grad[:, :group_rows]), parted(late_grad[:, group_rows:2 * group_rows]),
                parted(late_grad[:, 2 * group_rows:2 * group_rows + group_own]),
                jnp.zeros((n_all, late.shape[0] - late_own, D), bf)], axis=1)
        late_sum = lax.psum_scatter(late_grad, ALL, scatter_dimension=0, tiled=True)[0]
    d_query, d_key, d_value, d_key_rel, d_query_rel = grads
    late_sum = late_sum.astype(f32)
    g_inner, g_outer, g_out = late_sum[:late_rows], late_sum[late_rows:2 * late_rows], late_sum[2 * late_rows:late_own]
    ends = (d_query, d_key, d_value, tokens, gathered, weights, table, d_query_rel, d_key_rel, d_resid_one, sums, bias_sums)
    rel_rows = rel_table.shape[0]
    finished = (finish if even else finish_plain)(*ends, own_rows, rel_rows, cols, inner, n_t, n_dp)
    tokens_grad, g_query, g_key, g_value, g_rel, g_qkv_bias, g_ff_bias, g_gains, g_shifts = finished
    return (layer_result_rows, tokens_grad, g_query, g_key, g_value, g_out,
            g_qkv_bias, g_inner, g_outer, g_ff_bias.reshape(inner), g_rel, g_gains, g_shifts)

def solution(mesh):
    rows, params = P(("dp", "tensor"), None), P(ALL, None)
    return jax.shard_map(
        local, mesh=mesh,
        in_specs=(rows, params, params, params, params, P(None, ALL), params, params, P(ALL), P("dp", None),
                  P(None, "dp"), P(None, "dp"), P(), P("dp"), rows),
        out_specs=(rows, rows, params, params, params, params, P(None, ALL), params, params, P(ALL), P("dp", None),
                   P(None, "dp"), P(None, "dp")),
        check_vma=False)
```

```python
import functools
import math

import jax
import jax.numpy as jnp
from jax import lax
from jax.experimental import pallas as pl
from jax.experimental.pallas import tpu as pltpu
from jax.sharding import PartitionSpec as P

bf = jnp.bfloat16
f32 = jnp.float32
DH=64; NB=256
SCALE=1.0/math.sqrt(3*DH)
LOG2E=math.log2(math.e)

def dot_nt(a,b):
    return lax.dot_general(a,b,(((1,),(1,)),((),())),preferred_element_type=f32)
def dot_nn(a,b):
    return lax.dot_general(a,b,(((1,),(0,)),((),())),preferred_element_type=f32)
def dot_tn(a,b):
    return lax.dot_general(a,b,(((0,),(0,)),((),())),preferred_element_type=f32)

def flip_matrix(n):
    a=lax.broadcasted_iota(jnp.int32,(n,n),0); b=lax.broadcasted_iota(jnp.int32,(n,n),1)
    return jnp.where(a+b==n-1,1.0,0.0).astype(bf)

def flip_rows(x):
    n,w=x.shape
    idx=7-lax.broadcasted_iota(jnp.int32,(8,w),0)
    return jnp.concatenate([jnp.take_along_axis(x[n-8-8*g:n-8*g],idx,axis=0) for g in range(n//8)],axis=0)

def fwd_kernel(R,L,B,C,mask_ref,q_ref,k_ref,v_ref,kt_ref,qr_ref,ctx_ref,scale_ref,e_ref,yt_ref,acc_ref,km_ref,y_ref,s_ref,x_ref,p_ref):
    hh=pl.program_id(1)
    lane=lambda n: lax.broadcasted_iota(jnp.int32,(n,128),1)
    def lanes(n): return (lane(n)//DH)==hh
    zero,one=jnp.zeros((),bf),jnp.ones((),bf)
    spare=(1-hh)*DH
    for i in range(L//C):
        at=slice(i*C,i*C+C)
        km_ref[at,:]=jnp.where(lane(C)==spare,mask_ref[at,:],k_ref[at,:])
    def yblock(i):
        at=slice(i*C,i*C+C)
        us=L-C-i*C
        kb=jnp.where(lanes(C),k_ref[at,:],zero)
        y=y_ref.at[i%2]
        y[...]=dot_nt(kb,qr_ref[us:us+R+C,:])
        for g in range(C//16):
            rows=slice(16*g,16*g+16)
            part=y[rows,:].astype(bf)
            s_part=pltpu.roll(part,R+1+16*g,1,stride=1,stride_axis=0)[:,:R]
            yt_ref[i%2,rows,:]=s_part
        return yt_ref[i%2].T
    for i in range(L//C):
        acc_ref[:,i*C:i*C+C]=yblock(i)
    v_one=jnp.where(lanes(L),v_ref[...],one)
    own=lanes(B)
    sp=lane(B)==spare
    accs=[]
    for i in range(R//B):
        r0=i*B
        qm=q_ref[r0:r0+B,:]
        q=jnp.where(own,qm,zero)
        qs=jnp.where(sp,one,q)
        ws=R-B-r0
        x,s=x_ref.at[i%2],s_ref.at[i%2]
        x[...]=dot_nt(q,kt_ref[ws:ws+L+B,:])
        s[...]=dot_nt(qs,km_ref[...])
        rr=R-B-r0
        p=p_ref.at[i%2]
        for g in range(B//16):
            rows=slice(16*g,16*g+16)
            xr=pltpu.roll(x[rows,:],(L+1+16*g)%(L+B),1,stride=1,stride_axis=0)[:,:L]
            raw=s[rows,:]+xr+acc_ref[r0+16*g:r0+16*g+16,:].astype(f32)
            s[rows,:]=raw
            top=raw[:,:128]
            for j in range(1,L//128):
                top=jnp.maximum(top,raw[:,128*j:128*j+128])
            p[rows,:]=top
        p[...]=jnp.broadcast_to(jnp.max(p[...],axis=1,keepdims=True)*(SCALE*LOG2E),(B,128))
        for g in range(B//16):
            rows=slice(16*g,16*g+16)
            peak=jnp.concatenate([p[rows,:]]*(L//128),axis=1)
            e=jnp.exp2(s[rows,:]*(SCALE*LOG2E)-peak)
            e=flip_rows(e).astype(bf)
            to=rr+B-16-16*g
            e_ref[0,to:to+16,:]=e
        accs.append(dot_nn(e_ref[0,rr:rr+B,:],v_one))
    acc=jnp.concatenate(accs[::-1],axis=0)
    inv=1.0/pltpu.roll(acc,DH,1)
    J=flip_matrix(R)
    ctx=dot_nn(J,(acc*inv).astype(bf)).astype(bf)
    mine=lanes(R)
    inv_hi=inv.astype(bf)
    sc=dot_nn(J,inv_hi)+dot_nn(J,(inv-inv_hi.astype(f32)).astype(bf))
    sc=sc*SCALE
    @pl.when(hh==0)
    def _():
        ctx_ref[...]=ctx
        scale_ref[...]=sc
    @pl.when(hh==1)
    def _():
        ctx_ref[...]=jnp.where(mine,ctx,ctx_ref[...])
        scale_ref[...]=jnp.where(mine,sc,scale_ref[...])

def attention_forward(q,k,v,kt,qr,mask,B=128,C=256):
    R,F=q.shape; L=k.shape[0]; W=L+R; pairs=F//128
    B=min(B,R)
    col=lambda n: pl.BlockSpec((n,128),lambda p,h:(0,p))
    flops=2*pairs*2*R*L*128*4
    return pl.pallas_call(functools.partial(fwd_kernel,R,L,B,C),
        grid=(pairs,2),
        in_specs=[pl.BlockSpec((L,128),lambda p,h:(0,0)),col(R),col(L),col(L),col(W),col(W)],
        out_specs=[col(R),col(R),pl.BlockSpec((1,R,L),lambda p,h:(2*p+h,0,0))],
        out_shape=[jax.ShapeDtypeStruct((R,F),bf),jax.ShapeDtypeStruct((R,F),f32),jax.ShapeDtypeStruct((2*pairs,R,L),bf)],
        scratch_shapes=[pltpu.VMEM((2,C,R),bf),pltpu.VMEM((R,L),bf),pltpu.VMEM((L,128),bf),pltpu.VMEM((2,C,R+C),f32),
                        pltpu.VMEM((2,B,L),f32),pltpu.VMEM((2,B,L+B),f32),pltpu.VMEM((2,B,128),f32)],
        compiler_params=pltpu.CompilerParams(vmem_limit_bytes=60*1024*1024,dimension_semantics=("arbitrary","arbitrary")),
        cost_estimate=pl.CostEstimate(flops=flops,bytes_accessed=2*pairs*R*L*2+10*L*F,transcendentals=2*pairs*R*L),
        name="attend",
    )(mask,q,k,v,kt,qr)

def bwd_kernel(R,L,B,C,q_ref,k_ref,v_ref,do_ref,ctx_ref,e_ref,kr_ref,qrel_ref,ox_ref,oy_ref,
               dq_ref,dk_ref,dv_ref,dkr_ref,dqr_ref,ds_ref,dor_ref,qrev_ref,dqa_ref,dka_ref,dva_ref,
               delta_ref,dp_ref,wide_ref,dst_ref,wide2_ref):
    hh=pl.program_id(1)
    def lanes(n): return (lax.broadcasted_iota(jnp.int32,(n,128),1)//DH)==hh
    zero=jnp.zeros((),bf)
    @pl.when(hh==0)
    def _():
        dqa_ref[...]=jnp.zeros_like(dqa_ref)
        dka_ref[...]=jnp.zeros_like(dka_ref)
        dva_ref[...]=jnp.zeros_like(dva_ref)
        dkr_ref[...]=jnp.zeros_like(dkr_ref)
        dqr_ref[...]=jnp.zeros_like(dqr_ref)
    J=flip_matrix(R)
    do=jnp.where(lanes(R),dot_nn(J,do_ref[...]).astype(bf),zero)
    ctx=dot_nn(J,ctx_ref[...])
    dor_ref[...]=do
    qrev_ref[...]=jnp.where(lanes(R),dot_nn(J,q_ref[...]).astype(bf),zero)
    delta_ref[...]=jnp.broadcast_to(jnp.sum(do.astype(f32)*ctx,axis=1,keepdims=True),(R,128))
    own=lanes(B)
    for i in range(R//B):
        r0=i*B
        dp,wide=dp_ref.at[i%2],wide_ref.at[i%2]
        dp[...]=dot_nt(dor_ref[r0:r0+B,:],v_ref[...])
        for g in range(B//16):
            rows=slice(16*g,16*g+16)
            at=slice(r0+16*g,r0+16*g+16)
            delta=jnp.concatenate([delta_ref[at,:]]*(L//128),axis=1)
            ds=(e_ref[0,at,:].astype(f32)*(dp[rows,:]-delta)).astype(bf)
            ds_ref[at,:]=ds
            part=jnp.concatenate([ds,jnp.zeros((16,B),bf)],axis=1)
            wide[rows,:]=pltpu.roll(part,16*g,1,stride=1,stride_axis=0)
        db=dot_nn(wide[...],ox_ref[r0:r0+L+B,:]).astype(bf)
        dq=dot_nn(ds_ref[r0:r0+B,:],k_ref[...])+dot_nn(db,kr_ref[...])
        dqa_ref[r0:r0+B,:]=jnp.where(own,dq,dqa_ref[r0:r0+B,:])
        dkr_ref[...]+=dot_tn(db,qrev_ref[r0:r0+B,:])
    ownk=lanes(C)
    qrel=jnp.where(lanes(NB),qrel_ref[...],zero)
    for i in range(L//C):
        at=slice(i*C,i*C+C)
        dst,wide=dst_ref.at[i%2],wide2_ref.at[i%2]
        dst[...]=ds_ref[:,at].T
        for g in range(C//16):
            rows=slice(16*g,16*g+16)
            part=jnp.concatenate([dst[rows,:],jnp.zeros((16,C),bf)],axis=1)
            wide[rows,:]=pltpu.roll(part,16*g,1,stride=1,stride_axis=0)
        db=dot_nn(wide[...],oy_ref[i*C:i*C+R+C,:]).astype(bf)
        dka_ref[at,:]+=dot_nn(dst[...],qrev_ref[...])+dot_nn(db,qrel)
        dva_ref[at,:]+=dot_tn(e_ref[0,:,at],dor_ref[...])
        kb=jnp.where(ownk,k_ref[at,:],zero)
        dqr_ref[...]+=dot_tn(db,kb)
    @pl.when(hh==1)
    def _():
        dq_ref[...]=dot_nn(J,dqa_ref[...].astype(bf)).astype(bf)
        dk_ref[...]=dka_ref[...].astype(bf)
        dv_ref[...]=(dva_ref[...]*(1.0/SCALE)).astype(bf)

def attention_backward(q,k,v,do,ctx,e,key_rel,query_rel,onehot_x,onehot_y,p0=0,count=None,before=None,after=None,through=None,B=128,C=128):
    R,F=q.shape; L=k.shape[0]; W=L+R; pairs=F//128
    count=pairs if count is None else count
    B=min(B,R)
    col=lambda n: pl.BlockSpec((n,128),lambda p,h:(0,p0+p))
    full=pl.BlockSpec((W,NB),lambda p,h:(0,0))
    flops=2*count*2*R*L*128*8
    args=[q,k,v,do,ctx,e,key_rel,query_rel,onehot_x,onehot_y]
    specs=[col(R),col(L),col(L),col(R),col(R),pl.BlockSpec((1,R,L),lambda p,h:(2*(p0+p)+h,0,0)),col(NB),col(NB),full,full]
    n_in=len(args)
    through=list(through or [])
    extra=list(before or [])+through+list(after or [])
    n_before=len(before or [])
    body=functools.partial(bwd_kernel,R,L,B,C)
    def kernel(*refs):
        rest=refs[n_in+len(extra):]
        body(*refs[:n_in],*rest[:5],*rest[5+len(through):])
    return pl.pallas_call(kernel,
        grid=(count,2),
        in_specs=specs+[pl.BlockSpec(memory_space=pl.ANY)]*len(extra),
        out_specs=[col(R),col(L),col(L),col(NB),col(NB)]+[pl.BlockSpec(memory_space=pl.ANY)]*len(through),
        out_shape=[jax.ShapeDtypeStruct((R,F),bf),jax.ShapeDtypeStruct((L,F),bf),jax.ShapeDtypeStruct((L,F),bf),
                   jax.ShapeDtypeStruct((NB,F),f32),jax.ShapeDtypeStruct((NB,F),f32)]+[jax.ShapeDtypeStruct(x.shape,x.dtype) for x in through],
        input_output_aliases={**({n_in+i:i for i in range(5)} if before else {}),**{n_in+n_before+i:5+i for i in range(len(through))}},
        scratch_shapes=[pltpu.VMEM((R,L),bf),pltpu.VMEM((R,128),bf),pltpu.VMEM((R,128),bf),
                        pltpu.VMEM((R,128),f32),pltpu.VMEM((L,128),f32),pltpu.VMEM((L,128),f32),
                        pltpu.VMEM((R,128),f32),pltpu.VMEM((2,B,L),f32),pltpu.VMEM((2,B,L+B),bf),pltpu.VMEM((2,C,R),bf),pltpu.VMEM((2,C,R+C),bf)],
        compiler_params=pltpu.CompilerParams(vmem_limit_bytes=48*1024*1024,dimension_semantics=("arbitrary","arbitrary")),
        cost_estimate=pl.CostEstimate(flops=flops,bytes_accessed=2*count*R*L*2+20*L*128*count,transcendentals=0),
        name="attend_back",
    )(*args,*extra)

EPS=1e-6

def gelu_parts(v):
    a=jnp.abs(v)
    t=1.0/(1.0+(0.3275911/math.sqrt(2.0))*a)
    bell=jnp.exp(-0.5*v*v)
    poly=t*(0.127414796+t*(-0.142248368+t*(0.7107068705+t*(-0.7265760135+t*0.5307027145))))
    tail=poly*bell
    phi=jnp.where(v>0,1.0-tail,tail)
    return v*phi, phi+v*bell*(1.0/math.sqrt(2.0*math.pi))

class Both:
    def __init__(self,*copies):
        self.copies=copies

    def start(self):
        for copy in self.copies:
            copy.start()

    def wait(self):
        for copy in self.copies:
            copy.wait()

def feed_kernel(R,D,tiles,per,rows_in,own_rows,ctx_ref,tok_ref,og_ref,scale_ref,wl_ref,late_ref,bias_ref,gain_ref,shift_ref,
                res_ref,dres_ref,do_ref,sums_ref,bsum_ref,keep_ref,give_ref,
                u1_ref,r1_ref,low_ref,acc_ref,pre_ref,gated_ref,gp_ref,dfeed_ref,stage_ref,tail_ref,datt_ref,wf_ref,wo_ref,sem):
    step=pl.program_id(0)
    core=lax.axis_index("dp")%2
    pairs=per//2
    width=per*rows_in
    CH=64
    def chunks(f):
        def body(i,c):
            f(pl.ds(pl.multiple_of(i*CH,CH),CH))
            return c
        lax.fori_loop(0,R//CH,body,0,unroll=4)
    mean=lambda x: jnp.mean(x,axis=1,keepdims=True)
    gain=lambda i: gain_ref[i:i+1,:]
    shift=lambda i: shift_ref[i:i+1,:]
    def add_sum(i,x):
        sums_ref[i:i+1,:]+=jnp.sum(x,axis=0,keepdims=True)
    @pl.when(step==0)
    def _():
        sums_ref[...]=jnp.zeros_like(sums_ref)
        for p in range(D//own_rows):
            wf_ref[p*own_rows:(p+1)*own_rows,:]=wl_ref[p].astype(f32)[0:own_rows]
        wo_ref[...]=wf_ref[...].astype(bf)
        acc_ref[...]=dot_nn(ctx_ref[...],wo_ref[...])
        def norm(at):
            v=tok_ref[at,:].astype(f32)+acc_ref[at,:]+shift(0)
            c=v-mean(v)
            r=lax.rsqrt(mean(c*c)+EPS)
            u=c*r
            u1_ref[at,:]=u
            r1_ref[at,:]=jnp.broadcast_to(r,(CH,128))
            h=u*gain(0)+shift(1)
            low_ref[at,:]=h.astype(bf)
            acc_ref[at,:]=h+shift(2)
        chunks(norm)
    w_in=late_ref[:,0:rows_in,:].reshape(width,D)
    w_outer=late_ref[:,rows_in:2*rows_in,:].reshape(width,D)
    @pl.when(step<tiles)
    def _():
        pre_ref[...]=dot_nt(low_ref[...],w_in)
        def act(at):
            g,gp=gelu_parts(pre_ref[at,:]+bias_ref[0])
            gated_ref[step,at,:]=g.astype(bf)
            gp_ref[step,at,:]=gp.astype(bf)
        chunks(act)
        acc_ref[...]+=dot_nn(gated_ref[step],w_outer)
    @pl.when(step==tiles-1)
    def _():
        def norm(at):
            v=acc_ref[at,:]
            c=v-mean(v)
            r=lax.rsqrt(mean(c*c)+EPS)
            u=c*r
            res_ref[at,:]=(u*gain(1)+shift(3)).astype(bf)
            top=og_ref[at,:].astype(f32)
            add_sum(1,top*u)
            add_sum(5,top)
            e=top*gain(1)
            d=(e-mean(e)-u*mean(e*u))*r
            add_sum(4,d)
            dfeed_ref[at,:]=d.astype(bf)
            acc_ref[at,:]=d
        chunks(norm)
    @pl.when(step>=tiles)
    def _():
        k=step-tiles
        slot=lax.rem(k,2)
        pre_ref[...]=dot_nt(dfeed_ref[...],w_outer)
        def act(at):
            d=(pre_ref[at,:]*gp_ref[k,at,:].astype(f32)).astype(bf)
            gp_ref[k,at,:]=d
        chunks(act)
        bsum_ref[0]=jnp.sum(gp_ref[k].astype(f32),axis=0,keepdims=True)
        def out(kk,s):
            to=(pl.ds(kk*pairs,pairs),pl.ds(0,2*rows_in))
            return Both(pltpu.make_async_copy(stage_ref.at[s,:,core],keep_ref.at[to],sem.at[s,0]),
                        pltpu.make_async_copy(stage_ref.at[s,:,1-core],give_ref.at[to],sem.at[s,1]))
        @pl.when(k>=2)
        def _():
            out(k-2,slot).wait()
        stage_ref[slot,:,:,0:rows_in,:]=dot_tn(gp_ref[k],low_ref[...]).astype(bf).reshape(pairs,2,rows_in,D)
        stage_ref[slot,:,:,rows_in:2*rows_in,:]=dot_tn(gated_ref[k],dfeed_ref[...]).astype(bf).reshape(pairs,2,rows_in,D)
        out(k,slot).start()
        acc_ref[...]+=dot_nn(gp_ref[k],w_in)
        @pl.when(k==tiles-1)
        def _():
            def norm(at):
                d=acc_ref[at,:]
                u=u1_ref[at,:]
                r=r1_ref[at,0:1]
                add_sum(0,d*u)
                add_sum(3,d)
                e=d*gain(0)
                g=(e-mean(e)-u*mean(e*u))*r
                add_sum(2,g)
                dres_ref[at,:]=g
                datt_ref[at,:]=g.astype(bf)
            chunks(norm)
            do_ref[...]=(dot_nt(datt_ref[...],wo_ref[...])*scale_ref[...]).astype(bf)
            outer=dot_tn(ctx_ref[...],datt_ref[...])
            n=D//own_rows
            gap=tail_ref.shape[2]-own_rows
            for p in range(n):
                piece=outer[p*own_rows:p*own_rows+own_rows,:]
                if gap:
                    piece=jnp.concatenate([piece,jnp.zeros((gap,D),f32)],axis=0)
                tail_ref[p//2,p%2]=piece.astype(bf)
            to=(slice(None),pl.ds(2*rows_in,tail_ref.shape[2]))
            last=Both(pltpu.make_async_copy(tail_ref.at[:,core],keep_ref.at[to],sem.at[2,0]),
                      pltpu.make_async_copy(tail_ref.at[:,1-core],give_ref.at[to],sem.at[2,1]))
            last.start()
            if tiles>1:
                out(k-1,1-slot).wait()
            out(k,slot).wait()
            last.wait()

def feed(ctx,tokens,out_grad,scale,late,bias,gain,shift,rows_in,own_rows,tiles=4):
    R,D=ctx.shape
    n,rows_late,_=late.shape
    per=n//tiles
    width=per*rows_in
    tail=rows_late-2*rows_in
    vm=lambda s: pl.BlockSpec(s,lambda i: (0,)*len(s))
    return pl.pallas_call(functools.partial(feed_kernel,R,D,tiles,per,rows_in,own_rows),
        grid=(2*tiles,),
        in_specs=[vm((R,D)),vm((R,D)),vm((R,D)),vm((R,D)),pl.BlockSpec((n,tail,D),lambda i:(0,2*rows_in//tail,0)),
                  pl.BlockSpec((per,rows_late,D),lambda i:(lax.rem(i,tiles),0,0)),
                  pl.BlockSpec((1,1,width),lambda i:(lax.rem(i,tiles),0,0)),vm((2,D)),vm((4,D))],
        out_specs=[vm((R,D)),vm((R,D)),vm((R,D)),vm((8,D)),pl.BlockSpec((1,1,width),lambda i:(jnp.maximum(i-tiles,0),0,0)),
                   pl.BlockSpec(memory_space=pl.ANY),pl.BlockSpec(memory_space=pl.ANY)],
        out_shape=[jax.ShapeDtypeStruct((R,D),bf),jax.ShapeDtypeStruct((R,D),f32),jax.ShapeDtypeStruct((R,D),bf),
                   jax.ShapeDtypeStruct((8,D),f32),jax.ShapeDtypeStruct((tiles,1,width),f32),
                   jax.ShapeDtypeStruct((n//2,rows_late,D),bf),jax.ShapeDtypeStruct((n//2,rows_late,D),bf)],
        scratch_shapes=[pltpu.VMEM((R,D),f32),pltpu.VMEM((R,128),f32),pltpu.VMEM((R,D),bf),pltpu.VMEM((R,D),f32),
                        pltpu.VMEM((R,width),f32),pltpu.VMEM((tiles,R,width),bf),pltpu.VMEM((tiles,R,width),bf),
                        pltpu.VMEM((R,D),bf),pltpu.VMEM((2,per//2,2,2*rows_in,D),bf),pltpu.VMEM((n//2,2,tail,D),bf),pltpu.VMEM((R,D),bf),pltpu.VMEM((D,D),f32),pltpu.VMEM((D,D),bf),
                        pltpu.SemaphoreType.DMA((3,2))],
        compiler_params=pltpu.CompilerParams(vmem_limit_bytes=58*1024*1024,dimension_semantics=("arbitrary",)),
        cost_estimate=pl.CostEstimate(flops=2*R*D*n*rows_in*6+6*R*D*D,bytes_accessed=4*n*rows_late*D+20*R*D,transcendentals=2*R*n*rows_in),
        name="feed",
    )(ctx,tokens,out_grad,scale,late,late,bias,gain,shift)

MESH = pl.DeviceIdType.MESH
ANY = pl.BlockSpec(memory_space=pl.ANY)
VM = pl.BlockSpec(memory_space=pltpu.VMEM)

def remote(src, dst, send, recv, peer):
    return pltpu.make_async_remote_copy(src_ref=src, dst_ref=dst, send_sem=send, recv_sem=recv,
                                        device_id=peer, device_id_type=MESH)

def meet(peers):
    barrier = pltpu.get_barrier_semaphore()
    for peer in peers:
        pl.semaphore_signal(barrier, inc=1, device_id=peer, device_id_type=MESH)
    pl.semaphore_wait(barrier, len(peers))

class Place:
    def __init__(self, n_t, n_dp):
        self.n_t, self.n_dp = n_t, n_dp
        bits = (n_dp // 2).bit_length() - 1
        self.low = bits // 2
        self.high = bits - self.low
        dp, self.t = lax.axis_index("dp"), lax.axis_index("tensor")
        self.core = dp % 2
        self.down = (dp // 2) % 2**self.low
        self.up = dp // 2 // 2**self.low
        self.others = [lax.rem(self.t + 1 + i, n_t) for i in range(n_t - 1)]
        self.twin = {"dp": dp - self.core + 1 - self.core}
        self.steps = [("down", i) for i in range(self.low)] + [("up", i) for i in range(self.high)]

    def bit(self, step):
        kind, i = step
        return (getattr(self, kind) // 2**i) % 2

    def peer(self, step):
        kind, i = step
        turn = (1 - 2 * self.bit(step)) * 2**i
        down = self.down + turn if kind == "down" else self.down
        up = self.up + turn if kind == "up" else self.up
        return {"dp": (up * 2**self.low + down) * 2 + self.core}

    def peers(self):
        return [{"tensor": o} for o in self.others] + [self.twin] + [self.peer(s) for s in self.steps]

    def orders(self):
        down = [s for s in self.steps if s[0] == "down"]
        up = [s for s in self.steps if s[0] == "up"]
        return [down + up, up + down]

    def spans(self, done):
        out = []
        for kind in ("up", "down"):
            n = sum(1 for s in done if s[0] == kind)
            here = getattr(self, kind)
            out.append(pl.ds((here // 2**n) * 2**n, 2**n))
        return out

    def parts(self):
        half = self.n_t // 2
        return [pl.ds(0, half), pl.ds(half, half)] if half else [pl.ds(0, 1)]

class Line:
    def __init__(self, t, n, own, slot, rows, pieces, send, recv):
        self.t, self.n, self.own, self.slot = t, n, own, slot
        self.rows, self.pieces, self.send, self.recv = rows, pieces, send, recv

    def piece(self, ref, j):
        size = self.rows // self.pieces
        return ref.at[pl.ds(j * size, size)]

    def copy(self, d, s, j, b, own):
        at = self.piece(self.slot(b), j)
        src = self.piece(self.own, j) if own else at
        peer = {"tensor": self.t + 1 - 2 * d}
        return remote(src, at, self.send.at[d, s, j], self.recv.at[d, s, j], peer)

    def post(self, s, j):
        for d in range(2):
            b = self.t - s + 2 * d * s
            go_on = (b >= 0) & (self.t + 1 < self.n) if d == 0 else (b < self.n) & (self.t > 0)

            @pl.when(go_on)
            def _():
                self.copy(d, s, j, b, s == 0).start()

    def take(self, s, j):
        for d in range(2):
            b = self.t - 1 - s if d == 0 else self.t + 1 + s

            @pl.when(b >= 0 if d == 0 else b < self.n)
            def _():
                self.copy(d, s, j, b, False).wait_recv()

    def step(self, s):
        for j in range(self.pieces):
            self.take(s, j)
            if s + 1 < self.n - 1:
                self.post(s + 1, j)

    def drain(self):
        for s in range(self.n - 1):
            for j in range(self.pieces):
                for d in range(2):
                    b = self.t - s + 2 * d * s

                    @pl.when((b >= 0) & (self.t + 1 < self.n) if d == 0 else (b < self.n) & (self.t > 0))
                    def _():
                        self.copy(d, s, j, b, s == 0).wait_send()

def lanes_of(count, width, shape, tall):
    wide_axis = 0 if tall else 1
    f = lax.broadcasted_iota(jnp.int32, shape, wide_axis)
    r = lax.broadcasted_iota(jnp.int32, shape, 1 - wide_axis)
    return jnp.where(f % count == r, 1.0, 0.0).astype(bf)

def spread_row(table, count, width, first):
    n = table.shape[0]
    full = dot_nn(table.astype(bf), lanes_of(count, width, (128, width), False))
    p = lax.broadcasted_iota(jnp.int32, (n, width), 0)
    f = lax.broadcasted_iota(jnp.int32, (n, width), 1)
    return jnp.sum(jnp.where(first + f // count == p, full, 0.0), axis=0, keepdims=True)

def fold_row(row, count, n, first):
    width = row.shape[1]
    p = lax.broadcasted_iota(jnp.int32, (n, width), 0)
    f = lax.broadcasted_iota(jnp.int32, (n, width), 1)
    full = jnp.where(first + f // count == p, jnp.broadcast_to(row, (n, width)), 0.0)
    return dot_nn(full.astype(bf), lanes_of(count, width, (width, 128), True))

def eight(n):
    return -(-n // 8) * 8

def begin_kernel(n_t, n_dp, own, part, cols, inner, tiles, L,
                 tok_ref, wq_ref, wk_ref, wv_ref, rel_ref, qkvb_ref, ffb_ref, gains_ref, shifts_ref, ahead_ref, back_ref, fin_ref, fout_ref, wo_ref,
                 q_out, k_out, v_out, krel_out, qrel_out, kt_out, qr_out, toks_out, w_out, ox_out, oy_out, table_out, late_all,
                 ibias_ref, gain_ref, shift_ref,
                 toks, packs, pack, packf, wf, w, kb, vb, qb, krel, qrel, kt, qr, table, tableb, miscf, ox, ox_tall, oy_tall,
                 tok_send, tok_recv, z_send, z_recv, x_send, x_recv, out_sem, lz_send, lz_recv, lx_send, lx_recv, lc_send, lc_recv, late_ref, latef):
    at = Place(n_t, n_dp)
    t = at.t
    R, D = tok_ref.shape
    W = L + R
    n_all = n_t * n_dp
    S, S2 = eight(own), eight(part)
    misc = 3 * S + S2

    packf[...] = jnp.zeros_like(packf)
    for i, ref in enumerate((wq_ref, wk_ref, wv_ref)):
        packf[i * S:i * S + own, :] = ref[...].astype(f32)
    for i in range(n_t):
        @pl.when(t == i)
        def _():
            packf[3 * S:3 * S + part, :] = rel_ref[...].astype(f32)[i * part:(i + 1) * part]
    for i in range(3):
        packf[misc:misc + 1, 128 * i:128 * i + own] = qkvb_ref[i:i + 1, :].astype(f32)
    packf[misc:misc + 1, 384:384 + inner] = ffb_ref[...].astype(f32)
    for i in range(2):
        packf[misc + 1:misc + 2, 128 * i:128 * i + cols] = gains_ref[i:i + 1, :].astype(f32)
    for i in range(4):
        packf[misc + 1:misc + 2, 256 + 128 * i:256 + 128 * i + cols] = shifts_ref[i:i + 1, :].astype(f32)
    pack[...] = packf[...].astype(bf)
    latef[...] = jnp.zeros_like(latef)
    at_row = 0
    for ref in (fin_ref, fout_ref, wo_ref):
        latef[at_row:at_row + ref.shape[0], :] = ref[...].astype(f32)
        at_row += ref.shape[0]
    late_ref[...] = latef[...].astype(bf)

    meet(at.peers())
    copies = []

    def go(copy):
        copy.start()
        copies.append(copy)
        return copy

    here = packs.at[t, at.up, at.down, at.core]
    column = Line(t, n_t, pack, lambda i: packs.at[i, at.up, at.down, at.core], pack.shape[0], 1, z_send, z_recv)
    tokens = Line(t, n_t, tok_ref, lambda i: toks.at[i], R, 2, tok_send, tok_recv)
    late = Line(t, n_t, late_ref, lambda i: late_all.at[i, at.up, at.down, at.core], late_ref.shape[0], 1, lz_send, lz_recv)
    column.post(0, 0)
    late.post(0, 0)
    own_late = pltpu.make_async_copy(late_ref, late_all.at[t, at.up, at.down, at.core], out_sem.at[out_sem.shape[0] - 1])
    own_late.start()
    own_pack = pltpu.make_async_copy(pack, here, out_sem.at[0])
    own_pack.start()
    outs = []

    def put(src, dst):
        copy = pltpu.make_async_copy(src, dst, out_sem.at[1 + len(outs)])
        copy.start()
        outs.append(copy)

    def pick(line, start):
        rows = line[:, pl.ds(pl.multiple_of(start, 128), W)]
        ids = lax.broadcasted_iota(jnp.int32, (NB, W), 0)
        return jnp.where(ids == rows, 1.0, 0.0).astype(bf)

    ox[...] = pick(back_ref, L - R - R * t)
    ox_tall[...] = ox[...].T
    oy_tall[...] = pick(ahead_ref, L - R - R * t).T
    put(ox_tall, ox_out)
    put(oy_tall, oy_out)

    for s in range(n_t - 1):
        column.step(s)
        if s < n_t - 2:
            late.step(s)
        if s == n_t - 3 or n_t < 3:
            for j in range(2):
                tokens.post(0, j)
    own_pack.wait()
    parts, orders = at.parts(), at.orders()
    n_steps = len(at.steps)
    swaps = {}

    def swap(h, k):
        if k:
            swaps[h, k - 1].wait_recv()
        up, down = at.spans(orders[h][:k])
        if k < n_steps:
            piece, peer = packs.at[parts[h], up, down, at.core], at.peer(orders[h][k])
        else:
            piece, peer = packs.at[parts[h], :, :, at.core], at.twin
        swaps[h, k] = go(remote(piece, piece, x_send.at[h, k], x_recv.at[h, k], peer))

    hs = range(len(parts))
    moves = {}

    def late_twin(h, k):
        up, down = at.spans(orders[h][:k])
        if k:
            kind, i = orders[h][k - 1]
            base = (getattr(at, kind) // 2**(i + 1)) * 2**(i + 1)
            other = pl.ds(base + (1 - at.bit((kind, i))) * 2**i, 2**i)
            up, down = (other, down) if kind == "up" else (up, other)
        piece = late_all.at[parts[h], up, down, at.core]
        moves[h, k, "twin"] = go(remote(piece, piece, lc_send.at[h, k], lc_recv.at[h, k], at.twin))

    def late_swap(k):
        for h in hs:
            if k:
                moves[h, k - 1, "swap"].wait_recv()
            if k < n_steps:
                up, down = at.spans(orders[h][:k])
                piece = late_all.at[parts[h], up, down, at.core]
                moves[h, k, "swap"] = go(remote(piece, piece, lx_send.at[h, k], lx_recv.at[h, k], at.peer(orders[h][k])))
            late_twin(h, k)

    for h in hs:
        swap(h, 0)
    late.step(n_t - 2)
    own_late.wait()
    late_swap(0)
    passed = 0
    for k in range(1, n_steps + 1):
        for h in hs:
            swap(h, k)
    if n_t > 2:
        tokens.step(0)
        passed = 1
    for h in hs:
        swaps[h, n_steps].wait_recv()

    slots = [(a, u, d, c) for a in range(n_t) for u in range(2**at.high) for d in range(2**at.low) for c in range(2)]
    for i in range(3):
        for p, s in enumerate(slots):
            wf[p * own:p * own + own, :] = packs[s[0], s[1], s[2], s[3], i * S:i * S + own, :].astype(f32)
        w[i] = wf[...].astype(bf)
    put(w, w_out)
    for p, s in enumerate(slots):
        rows = packs[s[0], s[1], s[2], s[3], misc:misc + 8, :].astype(f32)
        miscf[0, p:p + 1, :] = rows[0:1]
        miscf[1, p:p + 1, :] = rows[1:2]
        a, dp = p // n_dp, p % n_dp
        to = dp * n_t * part + a * part
        table[to:to + part, :] = packs[s[0], s[1], s[2], s[3], 3 * S:3 * S + part, :].astype(f32)
    if n_steps:
        late_swap(1)
    bias = [spread_row(miscf[0, :, 128 * i:128 * i + 128], own, D, 0) for i in range(3)]
    rel = table[...].astype(bf)
    tableb[...] = rel
    put(tableb, table_out)
    krel[...] = (dot_nt(rel, w[1]) + bias[1]).astype(bf)
    qrel[...] = (dot_nt(rel, w[0]) + bias[0]).astype(bf)
    put(krel, krel_out)
    put(qrel, qrel_out)
    kt[...] = dot_tn(ox[...], krel[...]).astype(bf)
    put(kt, kt_out)
    qr[...] = dot_tn(pick(back_ref, R * t), qrel[...]).astype(bf)
    put(qr, qr_out)
    if n_t > 3:
        tokens.step(1)
        passed = 2

    def project(tokens, i):
        return (dot_nt(tokens, w[i]) + bias[i]).astype(bf)

    qb[...] = project(tok_ref[...], 0)
    put(qb, q_out)
    width = n_all * inner // tiles
    for i in range(tiles):
        ibias_ref[i] = spread_row(miscf[0, :, 384:512], inner, width, i * (n_all // tiles))
    for i in range(2):
        gain_ref[i:i + 1, :] = spread_row(miscf[1, 0:n_dp, 128 * i:128 * i + 128], cols, D, 0)
    for i in range(4):
        shift_ref[i:i + 1, :] = spread_row(miscf[1, 0:n_dp, 256 + 128 * i:384 + 128 * i], cols, D, 0)

    for s in range(n_t):
        b = lax.rem(t - s + n_t, n_t)
        rows = pl.ds(pl.multiple_of(b * R, R), R)
        if s == 1:
            for k in range(2, n_steps + 1):
                late_swap(k)
            for i in range(passed, n_t - 1):
                tokens.step(i)
        src = tok_ref if s == 0 else toks.at[b]
        put(src, toks_out.at[b])
        kb[s] = project(src[...], 1)
        put(kb.at[s], k_out.at[rows])
        vb[s] = project(src[...], 2)
        put(vb.at[s], v_out.at[rows])
    for h in hs:
        for k in range(n_steps + 1):
            moves[h, k, "twin"].wait_recv()
    for copy in outs:
        copy.wait()
    for copy in copies:
        copy.wait_send()
    column.drain()
    late.drain()
    tokens.drain()

def begin(tokens, w_query, w_key, w_value, rel_table, qkv_bias, ff_bias, gains, shifts, ahead, back, w_ff_in, w_ff_out, w_out, n_t, n_dp, tiles):
    R, D = tokens.shape
    L = ahead.shape[1] // 2
    W = L + R
    own, inner, cols = w_query.shape[0], ff_bias.shape[1], gains.shape[1]
    part = rel_table.shape[0] // n_t
    n_all = n_t * n_dp
    width = n_all * inner // tiles
    PR = -(-(3 * eight(own) + eight(part) + 8) // 16) * 16
    LR = -(-(2 * w_ff_in.shape[0] + own) // 16) * 16
    bits = (n_dp // 2).bit_length() - 1
    low = bits // 2
    S = jax.ShapeDtypeStruct
    big = [(R, D), (L, D), (L, D), (NB, D), (NB, D), (W, D), (W, D), (n_t, R, D), (3, D, D), (W, NB), (W, NB), (NB, D),
           (n_t, 2**(bits - low), 2**low, 2, LR, D)]
    v = lambda s, t=bf: pltpu.VMEM(s, t)
    dma = lambda *s: pltpu.SemaphoreType.DMA(s)
    return pl.pallas_call(
        functools.partial(begin_kernel, n_t, n_dp, own, part, cols, inner, tiles, L),
        out_shape=[S(s, bf) for s in big] + [S((tiles, 1, width), f32), S((2, D), f32), S((4, D), f32)],
        in_specs=[VM] * 14, out_specs=[ANY] * len(big) + [VM] * 3,
        scratch_shapes=[v((n_t, R, D)), v((n_t, 2**(bits - low), 2**low, 2, PR, D)), v((PR, D)), v((PR, D), f32), v((D, D), f32),
                        v((3, D, D)), v((n_t, R, D)), v((n_t, R, D)), v((R, D)), v((NB, D)), v((NB, D)), v((W, D)), v((W, D)),
                        v((NB, D), f32), v((NB, D)), v((2, n_all, D), f32), v((NB, W)), v((W, NB)), v((W, NB)),
                        dma(2, n_t - 1, 2), dma(2, n_t - 1, 2), dma(2, n_t - 1, 1), dma(2, n_t - 1, 1), dma(2, bits + 1), dma(2, bits + 1),
                        dma(11 + 3 * n_t), dma(2, n_t - 1, 1), dma(2, n_t - 1, 1), dma(2, max(bits, 1)), dma(2, max(bits, 1)), dma(2, bits + 1), dma(2, bits + 1),
                        v((LR, D)), v((LR, D), f32)],
        compiler_params=pltpu.CompilerParams(collective_id=0, has_side_effects=True, vmem_limit_bytes=58 * 1024 * 1024),
        name="begin",
    )(tokens, w_query, w_key, w_value, rel_table, qkv_bias, ff_bias, gains, shifts, ahead, back, w_ff_in, w_ff_out, w_out)

def finish_kernel(n_t, n_dp, own, rel_rows, cols, inner, tiles,
                  dq_in, dk_in, dv_in, tok_in, toks_in, w_in, table_in, dqr_in, dkr_in, dres_in, sums_ref, bsum_ref,
                  tg_ref, gq_ref, gk_ref, gv_ref, rel_ref, qkvb_ref, ffb_ref, gains_ref, shifts_ref,
                  dq, dk, dv, tok, toks, w, table, dqr, dkr, dres, g, relf, m0, m1, miscs, pack, first, acc, got, total,
                  tok_got, tok_acc, tok_own, base, *rest):
    at = Place(n_t, n_dp)
    t = at.t
    n_steps = len(at.steps)
    bufs, (in_sem, tok_send, tok_recv, x_send, x_recv, z_send, z_recv) = rest[:2 * n_steps], rest[2 * n_steps:]
    R, D = tok.shape
    L = n_t * R
    n_all = n_t * n_dp
    S, S3 = eight(own), eight(rel_rows)
    misc = 3 * S
    PR = pack.shape[4]
    right = {"tensor": lax.rem(t + 1, n_t)}
    loads = []

    def load(src, dst):
        copy = pltpu.make_async_copy(src, dst, in_sem.at[len(loads)])
        copy.start()
        loads.append(copy)
        return copy

    def block(s):
        return lax.rem(t - 1 - s + 2 * n_t, n_t)

    l_w = load(w_in, w)
    l_kv = []
    for s in range(n_t):
        b = block(s)
        l_kv.append((load(dk_in.at[b], dk.at[b]), load(dv_in.at[b], dv.at[b])))
    l_toks = load(toks_in, toks)
    l_rest = [load(tok_in, tok), load(dq_in, dq), load(table_in, table), load(dqr_in, dqr), load(dkr_in, dkr), load(dres_in, dres)]
    meet(at.peers())
    copies = []

    def go(copy):
        copy.start()
        copies.append(copy)
        return copy

    half = R // 2
    token = {}

    def partial(s):
        for copy in l_kv[s]:
            copy.wait()
        b = block(s)
        return dot_nn(dk[b], w[1]) + dot_nn(dv[b], w[2])

    def send_token(s):
        for j in range(2):
            rows = pl.ds(j * half, half)
            if s:
                token[s - 1, j].wait_recv()
                tok_acc[s, rows] = (tok_own[rows].astype(f32) + tok_got[s - 1, rows].astype(f32)).astype(bf)
            token[s, j] = go(remote(tok_acc.at[s, rows], tok_got.at[s, rows], tok_send.at[s, j], tok_recv.at[s, j], right))

    l_w.wait()
    tok_acc[0] = partial(0).astype(bf)
    send_token(0)
    for s in range(1, n_t):
        for copy in l_kv[s]:
            copy.wait()
    l_kv = [()] * n_t
    l_toks.wait()
    for copy in l_rest:
        copy.wait()
    dqb, dkb = dqr[...].astype(bf), dkr[...].astype(bf)
    rel_table = table[...]
    g[0] = dot_tn(dq[...], tok[...]) + dot_tn(dqb, rel_table)
    g[1] = dot_tn(dk[...].reshape(L, D), toks[...].reshape(L, D)) + dot_tn(dkb, rel_table)
    g[2] = dot_tn(dv[...].reshape(L, D), toks[...].reshape(L, D))
    relf[...] = dot_nn(dqb, w[0]) + dot_nn(dkb, w[1])
    ones = lambda n: jnp.ones((8, n), bf)
    columns = [dot_nn(ones(R), dq[...])[0:1] + jnp.sum(dqr[...], axis=0, keepdims=True),
               dot_nn(ones(L), dk[...].reshape(L, D))[0:1] + jnp.sum(dkr[...], axis=0, keepdims=True),
               dot_nn(ones(L), dv[...].reshape(L, D))[0:1]]
    for i in range(3):
        m0[:, 128 * i:128 * i + 128] = fold_row(columns[i], own, n_all, 0)
    units = jnp.zeros((n_all, 128), f32)
    for i in range(tiles):
        units += fold_row(bsum_ref[i], inner, n_all, i * (n_all // tiles))
    m0[:, 384:512] = units
    for i in range(6):
        m1[:, 128 * i:128 * i + 128] = fold_row(sums_ref[i:i + 1, :], cols, n_dp, 0)
    miscs[...] = jnp.zeros_like(miscs)
    slots = [(a, u, d, c) for a in range(n_t) for u in range(2**at.high) for d in range(2**at.low) for c in range(2)]

    def padded(x, n):
        return jnp.concatenate([x, jnp.zeros((n - x.shape[0], D), f32)], axis=0) if n > x.shape[0] else x

    parts = at.parts()
    hs = range(len(parts))
    per = n_t // len(parts)
    orders = [list(reversed(o)) for o in at.orders()][:len(parts)]
    swaps = {}
    left = {h: {"up": at.high, "down": at.low} for h in hs}

    def region(h, cut=None):
        out = []
        for kind in ("up", "down"):
            n = left[h][kind]
            here = getattr(at, kind)
            if cut is not None and cut[0] == kind:
                start = (here // 2**n) * 2**n + (1 - at.bit(cut)) * 2**(n - 1)
                out.append((start, 2**(n - 1)))
            else:
                out.append(((here // 2**n) * 2**n, 2**n))
        return out

    def start(h, k):
        if k == 0:
            src, dst, peer = pack.at[parts[h], :, :, 1 - at.core], first.at[parts[h]], at.twin
        else:
            cut = orders[h][k - 1]
            up, down = [pl.ds(*x) for x in region(h, cut)]
            src, dst, peer = acc.at[parts[h], up, down], bufs[h * n_steps + k - 1], at.peer(cut)
        swaps[h, k] = go(remote(src, dst, x_send.at[h, k], x_recv.at[h, k], peer))

    def absorb(h, k):
        swaps[h, k].wait_recv()
        if k:
            left[h][orders[h][k - 1][0]] -= 1
        (u0, nu), (d0, nd) = region(h)
        buf = first if k == 0 else bufs[h * n_steps + k - 1]

        @pl.loop(0, per * nu * nd)
        def _(m):
            a, u, d = m // (nu * nd), m // nd % nu, m % nd
            if k == 0:
                x, y = pack[h * per + a, u, d, at.core], buf[h * per + a, u, d]
            else:
                x, y = acc[h * per + a, u0 + u, d0 + d], buf[a, u, d]
            acc[h * per + a, u0 + u, d0 + d] = (x.astype(f32) + y.astype(f32)).astype(bf)

    for p, s in enumerate(slots):
        dp = p % n_dp
        miscs[8 * p:8 * p + 1, 0:512] = m0[p:p + 1, :]
        miscs[8 * p + 1:8 * p + 2, :] = m1[dp:dp + 1, :]
        pieces = [padded(g[i, p * own:p * own + own, :], S) for i in range(3)]
        pieces += [miscs[8 * p:8 * p + 8, :], padded(relf[dp * rel_rows:dp * rel_rows + rel_rows, :], S3)]
        whole = padded(jnp.concatenate(pieces, axis=0), PR)
        pack[s[0], s[1], s[2], s[3]] = whole.astype(bf)
        if (p + 1) % (per * n_dp) == 0:
            start(p // (per * n_dp), 0)
    tok_own[...] = partial(1).astype(bf)
    sent = 1
    if n_t > 2:
        send_token(1)
        sent = 2
        tok_own[...] = partial(2).astype(bf)
    base[...] = partial(n_t - 1) + dres[...] + dot_nn(dq[...], w[0])
    for k in range(n_steps + 1):
        for h in hs:
            absorb(h, k)
            if k < n_steps:
                start(h, k + 1)
        if k == n_steps:
            ring = [go(remote(acc.at[o, at.up, at.down], got.at[i], z_send.at[i], z_recv.at[i], {"tensor": o}))
                    for i, o in enumerate(at.others)]
        if k and sent < n_t - 1:
            send_token(sent)
            sent += 1
            if sent < n_t - 1:
                tok_own[...] = partial(sent).astype(bf)
    for copy in ring:
        copy.wait_recv()
    total[...] = acc[t, at.up, at.down].astype(f32)
    for i in range(n_t - 1):
        total[...] += got[i].astype(f32)
    for i, ref in enumerate((gq_ref, gk_ref, gv_ref)):
        ref[...] = total[i * S:i * S + own, :]
    rel_ref[...] = total[misc + 8:misc + 8 + rel_rows, :]
    for i in range(3):
        qkvb_ref[i:i + 1, :] = total[misc:misc + 1, 128 * i:128 * i + own]
    ffb_ref[...] = total[misc:misc + 1, 384:384 + inner]
    for i in range(2):
        gains_ref[i:i + 1, :] = total[misc + 1:misc + 2, 128 * i:128 * i + cols]
    for i in range(4):
        shifts_ref[i:i + 1, :] = total[misc + 1:misc + 2, 256 + 128 * i:256 + 128 * i + cols]
    while sent < n_t - 1:
        send_token(sent)
        sent += 1
        if sent < n_t - 1:
            tok_own[...] = partial(sent).astype(bf)
    for j in range(2):
        rows = pl.ds(j * half, half)
        token[n_t - 2, j].wait_recv()
        tg_ref[rows, :] = base[rows, :] + tok_got[n_t - 2, rows].astype(f32)
    for copy in copies:
        copy.wait_send()

def finish(dq, dk, dv, tok, toks, w, table, dqr, dkr, dres, sums, bsum, own, rel_rows, cols, inner, n_t, n_dp):
    R, D = tok.shape
    L = n_t * R
    n_all = n_t * n_dp
    tiles = bsum.shape[0]
    S3 = eight(rel_rows)
    PR = -(-(3 * eight(own) + 8 + S3) // 16) * 16
    bits = (n_dp // 2).bit_length() - 1
    low = bits // 2
    high = bits - low
    per = n_t // 2
    v = lambda s, x=bf: pltpu.VMEM(s, x)
    dma = lambda *s: pltpu.SemaphoreType.DMA(s)
    bufs = []
    for order in ([("up", high), ("down", low)], [("down", low), ("up", high)]):
        left = {"up": high, "down": low}
        for kind, n in order:
            for _ in range(n):
                left[kind] -= 1
                bufs.append(v((per, 2**left["up"], 2**left["down"], PR, D)))
    S = jax.ShapeDtypeStruct
    outs = [(R, D), (own, D), (own, D), (own, D), (rel_rows, D), (3, own), (1, inner), (2, cols), (4, cols)]
    blocks = lambda x: x.reshape(n_t, R, D)
    return pl.pallas_call(
        functools.partial(finish_kernel, n_t, n_dp, own, rel_rows, cols, inner, tiles),
        out_shape=[S(s, f32) for s in outs],
        in_specs=[ANY] * 10 + [VM] * 2, out_specs=[VM] * len(outs),
        scratch_shapes=[v((R, D)), v((n_t, R, D)), v((n_t, R, D)), v((R, D)), v((n_t, R, D)), v((3, D, D)), v((NB, D)),
                        v((NB, D), f32), v((NB, D), f32), v((R, D), f32), v((3, D, D), f32), v((NB, D), f32),
                        v((n_all, 512), f32), v((n_dp, D), f32), v((8 * n_all, D), f32),
                        v((n_t, 2**high, 2**low, 2, PR, D)), v((n_t, 2**high, 2**low, PR, D)), v((n_t, 2**high, 2**low, PR, D)),
                        v((n_t - 1, PR, D)), v((PR, D), f32),
                        v((n_t - 1, R, D)), v((n_t - 1, R, D)), v((R, D)), v((R, D), f32)] + bufs
                       + [dma(2 * n_t + 8), dma(n_t - 1, 2), dma(n_t - 1, 2), dma(2, bits + 1), dma(2, bits + 1), dma(n_t - 1), dma(n_t - 1)],
        compiler_params=pltpu.CompilerParams(collective_id=1, has_side_effects=True, vmem_limit_bytes=60 * 1024 * 1024),
        name="finish",
    )(dq, blocks(dk), blocks(dv), tok, blocks(toks), w, table, dqr, dkr, dres, sums, bsum)

GROUPS, TILES = 32, 4
ALL=("tensor","dp")

def fold(name, grid, place, terms, shapes, out_maps):
    tail = terms[0][0].shape[-2:]
    block = lambda x, where: pl.BlockSpec((1,) * (len(x.shape) - 2) + tail, lambda *i: tuple(where(*i)) + (0, 0))
    n = len(terms)

    def kernel(place_ref, *refs):
        for k in range(n):
            x, y, out = refs[2 * k], refs[2 * k + 1], refs[2 * n + k]
            out[...] = (x[...].astype(f32) + y[...].astype(f32)).reshape(out.shape).astype(bf)

    outs = [jax.ShapeDtypeStruct(s + tail, bf) for s in shapes]
    return pl.pallas_call(
        kernel, out_shape=outs,
        grid_spec=pltpu.PrefetchScalarGridSpec(
            num_scalar_prefetch=1, grid=grid,
            in_specs=[block(z, where) for x, y, where in terms for z in (x, y)],
            out_specs=[block(o, where) for o, where in zip(outs, out_maps)]),
        compiler_params=pltpu.CompilerParams(vmem_limit_bytes=32 * 1024 * 1024, dimension_semantics=("arbitrary",) * len(grid)),
        cost_estimate=pl.CostEstimate(flops=0, bytes_accessed=sum(6 * math.prod(o.shape) for o in outs), transcendentals=0),
        name=name,
    )(place, *[z for x, y, _ in terms for z in (x, y)])

def finish_plain(dq, dk, dv, tok, toks, w, table, dqr, dkr, dres, sums, bsum, own, rel_rows, cols, inner, n_t, n_dp):
    times = lambda s, a, b: jnp.einsum(s, a.astype(bf), b.astype(bf), preferred_element_type=f32)
    scatter = lambda x: lax.psum_scatter(x, ALL, scatter_dimension=0, tiled=True)
    grads = [times("tf,td->fd", dq, tok) + times("tf,td->fd", dqr, table),
             times("tf,td->fd", dk, toks) + times("tf,td->fd", dkr, table), times("tf,td->fd", dv, toks)]
    rel = times("bf,fd->bd", dqr, w[0]) + times("bf,fd->bd", dkr, w[1])
    spread = (times("tf,fd->td", dk, w[1]) + times("tf,fd->td", dv, w[2])).astype(bf)
    back_sum = lax.psum_scatter(spread, "tensor", scatter_dimension=0, tiled=True).astype(f32)
    tokens_grad = dres + times("tf,fd->td", dq, w[0]) + back_sum
    column = lambda x: jnp.sum(x.astype(f32), axis=0)
    bias = jnp.stack([column(dq) + column(dqr), column(dk) + column(dkr), column(dv)])
    every = lambda x: lax.psum(x, ALL)
    dp = lax.axis_index("dp")
    place = lax.axis_index("tensor") * n_dp + dp
    cut = lambda x, i, n: lax.dynamic_slice_in_dim(x, i * n, n, 1)
    rel = lax.dynamic_slice_in_dim(every(rel), dp * rel_rows, rel_rows, 0)
    return [tokens_grad] + [scatter(x) for x in grads] + [rel, cut(every(bias), place, own), cut(every(bsum.reshape(1, -1)), place, inner),
            cut(every(sums[:2]), dp, cols), cut(every(sums[2:6]), dp, cols)]

def local(tokens, w_query, w_key, w_value, w_out, qkv_bias, w_ff_in, w_ff_out, ff_bias, rel_table,
          gains, shifts, rel_bucket, lengths, out_grad):
    D = tokens.shape[1]
    n_t, n_dp = lax.axis_size("tensor"), lax.axis_size("dp")
    n_all = n_t * n_dp
    t = lax.axis_index("tensor")
    R = tokens.shape[0]
    L = (rel_bucket.shape[0] + 1) // 2
    W = L + R
    own_rows, cols, inner = w_query.shape[0], gains.shape[1], ff_bias.shape[0]
    none = jnp.full((1,), -1, jnp.int32)
    ahead = jnp.concatenate([rel_bucket, none])[None]
    back = jnp.concatenate([rel_bucket[::-1], none])[None]
    late_rows = w_ff_in.shape[0]
    even = late_rows % 16 == 0 and own_rows % 8 == 0
    late_own = 2 * late_rows + own_rows
    late_all_rows = late_own + -late_own % 16
    (query, key, value, key_rel, query_rel, key_table, query_table, gathered, weights, pick_x, pick_y, table,
     late_all, inner_bias, gain, shift) = begin(tokens, w_query, w_key, w_value, rel_table, qkv_bias, ff_bias.reshape(1, -1), gains, shifts,
                                      ahead, back, w_ff_in, w_ff_out, w_out, n_t, n_dp, TILES)
    gathered = gathered.reshape(L, D)
    late_all = late_all.reshape(n_all, -1, D)
    cut = lambda x, at, n: x[:, at:at + n].reshape(n_all * n, D)
    groups = n_all if even else GROUPS
    group_rows, group_own = n_all * late_rows // groups, D // groups
    if not even:
        sections = [cut(late_all, 0, late_rows), cut(late_all, late_rows, late_rows), cut(late_all, 2 * late_rows, own_rows)]
        late_all = jnp.concatenate([x.reshape(groups, -1, D) for x in sections]
                                   + [jnp.zeros((groups, -group_own % 16, D), bf)], axis=1)
    mask = jnp.where(jnp.arange(L, dtype=jnp.int32) < lengths[0], 0.0, -1e9).astype(bf)
    mask = jnp.broadcast_to(mask[:, None], (L, 128))

    context, scale, shares = attention_forward(query, key, value, key_table, query_table, mask)
    layer_result_rows, d_resid_one, d_scaled, sums, bias_sums, keep, give = feed(
        context, tokens, out_grad, scale, late_all, inner_bias, gain, shift, group_rows, group_own)
    back_args = (query, key, value, d_scaled, context, shares, key_rel, query_rel, pick_x, pick_y)
    pairs = D // 128
    if even and n_dp == 8 and n_t % 2 == 0 and pairs >= 6:
        dp = lax.axis_index("dp")
        place = jnp.stack([dp // 4, dp // 2 % 2]).astype(jnp.int32)
        swap = lambda x, mask: lax.ppermute(x, "dp", [(i, i ^ mask) for i in range(n_dp)])
        shape = (n_t, 2, 2, late_all_rows, D)
        keep, give = keep.reshape(shape), give.reshape(shape)
        got = swap(give, 1)
        half = n_t // 2
        *grads, keep = attention_backward(*back_args, p0=0, count=pairs - 5, through=[keep])
        stay_one, away_one, stay_two, away_two = fold(
            "fold", (half, 2), place,
            [(keep, got, lambda i, j, s: (i, s[0], j)), (keep, got, lambda i, j, s: (i, 1 - s[0], j)),
             (keep, got, lambda i, j, s: (half + i, j, s[1])), (keep, got, lambda i, j, s: (half + i, j, 1 - s[1]))],
            [(half, 2)] * 4, [lambda i, j, s: (i, j)] * 4)
        got_one, got_two = swap(away_one, 4), swap(away_two, 2)
        *grads, stay_one, stay_two = attention_backward(
            *back_args, p0=pairs - 5, count=2, before=grads, after=[away_one, away_two], through=[stay_one, stay_two])
        stay_one, away_one, stay_two, away_two = fold(
            "fold", (half,), place,
            [(stay_one, got_one, lambda i, s: (i, s[1])), (stay_one, got_one, lambda i, s: (i, 1 - s[1])),
             (stay_two, got_two, lambda i, s: (i, s[0])), (stay_two, got_two, lambda i, s: (i, 1 - s[0]))],
            [(half,)] * 4, [lambda i, s: (i,)] * 4)
        got_one, got_two = swap(away_one, 2), swap(away_two, 4)
        *grads, stay_one, stay_two = attention_backward(
            *back_args, p0=pairs - 3, count=1, before=grads, after=[away_one, away_two], through=[stay_one, stay_two])
        column = jnp.concatenate(fold(
            "fold", (half,), place,
            [(stay_one, got_one, lambda i, s: (i,)), (stay_two, got_two, lambda i, s: (i,))],
            [(half,)] * 2, [lambda i, s: (i,)] * 2), axis=0)
        late_sum = lax.psum_scatter(column, "tensor", scatter_dimension=0, tiled=True)[0]
        grads = attention_backward(*back_args, p0=pairs - 2, count=2, before=grads, after=[column])
    else:
        grads = attention_backward(*back_args)
        core = lax.axis_index("dp") % 2
        late_grad = jnp.where(core == 0, jnp.stack([keep, give], axis=1), jnp.stack([give, keep], axis=1))
        late_grad = late_grad.reshape(groups, -1, D)
        parted = lambda x: x.reshape(n_all, -1, D)
        if not even:
            late_grad = jnp.concatenate([
                parted(late_grad[:, :group_rows]), parted(late_grad[:, group_rows:2 * group_rows]),
                parted(late_grad[:, 2 * group_rows:2 * group_rows + group_own]),
                jnp.zeros((n_all, late_all_rows - late_own, D), bf)], axis=1)
        late_sum = lax.psum_scatter(late_grad, ALL, scatter_dimension=0, tiled=True)[0]
    d_query, d_key, d_value, d_key_rel, d_query_rel = grads
    late_sum = late_sum.astype(f32)
    g_inner, g_outer, g_out = late_sum[:late_rows], late_sum[late_rows:2 * late_rows], late_sum[2 * late_rows:late_own]
    ends = (d_query, d_key, d_value, tokens, gathered, weights, table, d_query_rel, d_key_rel, d_resid_one, sums, bias_sums)
    rel_rows = rel_table.shape[0]
    finished = (finish if even else finish_plain)(*ends, own_rows, rel_rows, cols, inner, n_t, n_dp)
    tokens_grad, g_query, g_key, g_value, g_rel, g_qkv_bias, g_ff_bias, g_gains, g_shifts = finished
    return (layer_result_rows, tokens_grad, g_query, g_key, g_value, g_out,
            g_qkv_bias, g_inner, g_outer, g_ff_bias.reshape(inner), g_rel, g_gains, g_shifts)

def solution(mesh):
    rows, params = P(("dp", "tensor"), None), P(ALL, None)
    return jax.shard_map(
        local, mesh=mesh,
        in_specs=(rows, params, params, params, params, P(None, ALL), params, params, P(ALL), P("dp", None),
                  P(None, "dp"), P(None, "dp"), P(), P("dp"), rows),
        out_specs=(rows, rows, params, params, params, params, P(None, ALL), params, params, P(ALL), P("dp", None),
                   P(None, "dp"), P(None, "dp")),
        check_vma=False)
```

```python
import functools
import math

import jax
import jax.numpy as jnp
from jax import lax
from jax.experimental import pallas as pl
from jax.experimental.pallas import tpu as pltpu
from jax.sharding import PartitionSpec as P

bf = jnp.bfloat16
f32 = jnp.float32
DH=64; NB=256
SCALE=1.0/math.sqrt(3*DH)
LOG2E=math.log2(math.e)

def dot_nt(a,b):
    return lax.dot_general(a,b,(((1,),(1,)),((),())),preferred_element_type=f32)
def dot_nn(a,b):
    return lax.dot_general(a,b,(((1,),(0,)),((),())),preferred_element_type=f32)
def dot_tn(a,b):
    return lax.dot_general(a,b,(((0,),(0,)),((),())),preferred_element_type=f32)

def flip_matrix(n):
    a=lax.broadcasted_iota(jnp.int32,(n,n),0); b=lax.broadcasted_iota(jnp.int32,(n,n),1)
    return jnp.where(a+b==n-1,1.0,0.0).astype(bf)

def flip_rows(x):
    n,w=x.shape
    idx=7-lax.broadcasted_iota(jnp.int32,(8,w),0)
    return jnp.concatenate([jnp.take_along_axis(x[n-8-8*g:n-8*g],idx,axis=0) for g in range(n//8)],axis=0)

def fwd_kernel(R,L,B,C,mask_ref,q_ref,k_ref,v_ref,kt_ref,qr_ref,ctx_ref,scale_ref,e_ref,yt_ref,acc_ref,km_ref,y_ref,s_ref,x_ref,p_ref):
    hh=pl.program_id(1)
    lane=lambda n: lax.broadcasted_iota(jnp.int32,(n,128),1)
    def lanes(n): return (lane(n)//DH)==hh
    zero,one=jnp.zeros((),bf),jnp.ones((),bf)
    spare=(1-hh)*DH
    for i in range(L//C):
        at=slice(i*C,i*C+C)
        km_ref[at,:]=jnp.where(lane(C)==spare,mask_ref[at,:],k_ref[at,:])
    def yblock(i):
        at=slice(i*C,i*C+C)
        us=L-C-i*C
        kb=jnp.where(lanes(C),k_ref[at,:],zero)
        y=y_ref.at[i%2]
        y[...]=dot_nt(kb,qr_ref[us:us+R+C,:])
        for g in range(C//16):
            rows=slice(16*g,16*g+16)
            part=y[rows,:].astype(bf)
            s_part=pltpu.roll(part,R+1+16*g,1,stride=1,stride_axis=0)[:,:R]
            yt_ref[i%2,rows,:]=s_part
        return yt_ref[i%2].T
    for i in range(L//C):
        acc_ref[:,i*C:i*C+C]=yblock(i)
    v_one=jnp.where(lanes(L),v_ref[...],one)
    own=lanes(B)
    sp=lane(B)==spare
    accs=[]
    for i in range(R//B):
        r0=i*B
        qm=q_ref[r0:r0+B,:]
        q=jnp.where(own,qm,zero)
        qs=jnp.where(sp,one,q)
        ws=R-B-r0
        x,s=x_ref.at[i%2],s_ref.at[i%2]
        x[...]=dot_nt(q,kt_ref[ws:ws+L+B,:])
        s[...]=dot_nt(qs,km_ref[...])
        rr=R-B-r0
        p=p_ref.at[i%2]
        for g in range(B//16):
            rows=slice(16*g,16*g+16)
            xr=pltpu.roll(x[rows,:],(L+1+16*g)%(L+B),1,stride=1,stride_axis=0)[:,:L]
            raw=s[rows,:]+xr+acc_ref[r0+16*g:r0+16*g+16,:].astype(f32)
            s[rows,:]=raw
            top=raw[:,:128]
            for j in range(1,L//128):
                top=jnp.maximum(top,raw[:,128*j:128*j+128])
            p[rows,:]=top
        p[...]=jnp.broadcast_to(jnp.max(p[...],axis=1,keepdims=True)*(SCALE*LOG2E),(B,128))
        for g in range(B//16):
            rows=slice(16*g,16*g+16)
            peak=jnp.concatenate([p[rows,:]]*(L//128),axis=1)
            e=jnp.exp2(s[rows,:]*(SCALE*LOG2E)-peak)
            e=flip_rows(e).astype(bf)
            to=rr+B-16-16*g
            e_ref[0,to:to+16,:]=e
        accs.append(dot_nn(e_ref[0,rr:rr+B,:],v_one))
    acc=jnp.concatenate(accs[::-1],axis=0)
    inv=1.0/pltpu.roll(acc,DH,1)
    J=flip_matrix(R)
    ctx=dot_nn(J,(acc*inv).astype(bf)).astype(bf)
    mine=lanes(R)
    inv_hi=inv.astype(bf)
    sc=dot_nn(J,inv_hi)+dot_nn(J,(inv-inv_hi.astype(f32)).astype(bf))
    sc=sc*SCALE
    @pl.when(hh==0)
    def _():
        ctx_ref[...]=ctx
        scale_ref[...]=sc
    @pl.when(hh==1)
    def _():
        ctx_ref[...]=jnp.where(mine,ctx,ctx_ref[...])
        scale_ref[...]=jnp.where(mine,sc,scale_ref[...])

def attention_forward(q,k,v,kt,qr,mask,B=128,C=256):
    R,F=q.shape; L=k.shape[0]; W=L+R; pairs=F//128
    B=min(B,R)
    col=lambda n: pl.BlockSpec((n,128),lambda p,h:(0,p))
    flops=2*pairs*2*R*L*128*4
    return pl.pallas_call(functools.partial(fwd_kernel,R,L,B,C),
        grid=(pairs,2),
        in_specs=[pl.BlockSpec((L,128),lambda p,h:(0,0)),col(R),col(L),col(L),col(W),col(W)],
        out_specs=[col(R),col(R),pl.BlockSpec((1,R,L),lambda p,h:(2*p+h,0,0))],
        out_shape=[jax.ShapeDtypeStruct((R,F),bf),jax.ShapeDtypeStruct((R,F),f32),jax.ShapeDtypeStruct((2*pairs,R,L),bf)],
        scratch_shapes=[pltpu.VMEM((2,C,R),bf),pltpu.VMEM((R,L),bf),pltpu.VMEM((L,128),bf),pltpu.VMEM((2,C,R+C),f32),
                        pltpu.VMEM((2,B,L),f32),pltpu.VMEM((2,B,L+B),f32),pltpu.VMEM((2,B,128),f32)],
        compiler_params=pltpu.CompilerParams(vmem_limit_bytes=60*1024*1024,dimension_semantics=("arbitrary","arbitrary")),
        cost_estimate=pl.CostEstimate(flops=flops,bytes_accessed=2*pairs*R*L*2+10*L*F,transcendentals=2*pairs*R*L),
        name="attend",
    )(mask,q,k,v,kt,qr)

def bwd_kernel(R,L,B,C,q_ref,k_ref,v_ref,do_ref,ctx_ref,e_ref,kr_ref,qrel_ref,ox_ref,oy_ref,
               dq_ref,dk_ref,dv_ref,dkr_ref,dqr_ref,ds_ref,dor_ref,qrev_ref,dqa_ref,dka_ref,dva_ref,
               delta_ref,dp_ref,wide_ref,dst_ref,wide2_ref):
    hh=pl.program_id(1)
    def lanes(n): return (lax.broadcasted_iota(jnp.int32,(n,128),1)//DH)==hh
    zero=jnp.zeros((),bf)
    @pl.when(hh==0)
    def _():
        dqa_ref[...]=jnp.zeros_like(dqa_ref)
        dka_ref[...]=jnp.zeros_like(dka_ref)
        dva_ref[...]=jnp.zeros_like(dva_ref)
        dkr_ref[...]=jnp.zeros_like(dkr_ref)
        dqr_ref[...]=jnp.zeros_like(dqr_ref)
    J=flip_matrix(R)
    do=jnp.where(lanes(R),dot_nn(J,do_ref[...]).astype(bf),zero)
    ctx=dot_nn(J,ctx_ref[...])
    dor_ref[...]=do
    qrev_ref[...]=jnp.where(lanes(R),dot_nn(J,q_ref[...]).astype(bf),zero)
    delta_ref[...]=jnp.broadcast_to(jnp.sum(do.astype(f32)*ctx,axis=1,keepdims=True),(R,128))
    own=lanes(B)
    for i in range(R//B):
        r0=i*B
        dp,wide=dp_ref.at[i%2],wide_ref.at[i%2]
        dp[...]=dot_nt(dor_ref[r0:r0+B,:],v_ref[...])
        for g in range(B//16):
            rows=slice(16*g,16*g+16)
            at=slice(r0+16*g,r0+16*g+16)
            delta=jnp.concatenate([delta_ref[at,:]]*(L//128),axis=1)
            ds=(e_ref[0,at,:].astype(f32)*(dp[rows,:]-delta)).astype(bf)
            ds_ref[at,:]=ds
            part=jnp.concatenate([ds,jnp.zeros((16,B),bf)],axis=1)
            wide[rows,:]=pltpu.roll(part,16*g,1,stride=1,stride_axis=0)
        db=dot_nn(wide[...],ox_ref[r0:r0+L+B,:]).astype(bf)
        dq=dot_nn(ds_ref[r0:r0+B,:],k_ref[...])+dot_nn(db,kr_ref[...])
        dqa_ref[r0:r0+B,:]=jnp.where(own,dq,dqa_ref[r0:r0+B,:])
        dkr_ref[...]+=dot_tn(db,qrev_ref[r0:r0+B,:])
    ownk=lanes(C)
    qrel=jnp.where(lanes(NB),qrel_ref[...],zero)
    for i in range(L//C):
        at=slice(i*C,i*C+C)
        dst,wide=dst_ref.at[i%2],wide2_ref.at[i%2]
        dst[...]=ds_ref[:,at].T
        for g in range(C//16):
            rows=slice(16*g,16*g+16)
            part=jnp.concatenate([dst[rows,:],jnp.zeros((16,C),bf)],axis=1)
            wide[rows,:]=pltpu.roll(part,16*g,1,stride=1,stride_axis=0)
        db=dot_nn(wide[...],oy_ref[i*C:i*C+R+C,:]).astype(bf)
        dka_ref[at,:]+=dot_nn(dst[...],qrev_ref[...])+dot_nn(db,qrel)
        dva_ref[at,:]+=dot_tn(e_ref[0,:,at],dor_ref[...])
        kb=jnp.where(ownk,k_ref[at,:],zero)
        dqr_ref[...]+=dot_tn(db,kb)
    @pl.when(hh==1)
    def _():
        dq_ref[...]=dot_nn(J,dqa_ref[...].astype(bf)).astype(bf)
        dk_ref[...]=dka_ref[...].astype(bf)
        dv_ref[...]=(dva_ref[...]*(1.0/SCALE)).astype(bf)

def attention_backward(q,k,v,do,ctx,e,key_rel,query_rel,onehot_x,onehot_y,p0=0,count=None,before=None,after=None,through=None,B=128,C=128):
    R,F=q.shape; L=k.shape[0]; W=L+R; pairs=F//128
    count=pairs if count is None else count
    B=min(B,R)
    col=lambda n: pl.BlockSpec((n,128),lambda p,h:(0,p0+p))
    full=pl.BlockSpec((W,NB),lambda p,h:(0,0))
    flops=2*count*2*R*L*128*8
    args=[q,k,v,do,ctx,e,key_rel,query_rel,onehot_x,onehot_y]
    specs=[col(R),col(L),col(L),col(R),col(R),pl.BlockSpec((1,R,L),lambda p,h:(2*(p0+p)+h,0,0)),col(NB),col(NB),full,full]
    n_in=len(args)
    through=list(through or [])
    extra=list(before or [])+through+list(after or [])
    n_before=len(before or [])
    body=functools.partial(bwd_kernel,R,L,B,C)
    def kernel(*refs):
        rest=refs[n_in+len(extra):]
        body(*refs[:n_in],*rest[:5],*rest[5+len(through):])
    return pl.pallas_call(kernel,
        grid=(count,2),
        in_specs=specs+[pl.BlockSpec(memory_space=pl.ANY)]*len(extra),
        out_specs=[col(R),col(L),col(L),col(NB),col(NB)]+[pl.BlockSpec(memory_space=pl.ANY)]*len(through),
        out_shape=[jax.ShapeDtypeStruct((R,F),bf),jax.ShapeDtypeStruct((L,F),bf),jax.ShapeDtypeStruct((L,F),bf),
                   jax.ShapeDtypeStruct((NB,F),f32),jax.ShapeDtypeStruct((NB,F),f32)]+[jax.ShapeDtypeStruct(x.shape,x.dtype) for x in through],
        input_output_aliases={**({n_in+i:i for i in range(5)} if before else {}),**{n_in+n_before+i:5+i for i in range(len(through))}},
        scratch_shapes=[pltpu.VMEM((R,L),bf),pltpu.VMEM((R,128),bf),pltpu.VMEM((R,128),bf),
                        pltpu.VMEM((R,128),f32),pltpu.VMEM((L,128),f32),pltpu.VMEM((L,128),f32),
                        pltpu.VMEM((R,128),f32),pltpu.VMEM((2,B,L),f32),pltpu.VMEM((2,B,L+B),bf),pltpu.VMEM((2,C,R),bf),pltpu.VMEM((2,C,R+C),bf)],
        compiler_params=pltpu.CompilerParams(vmem_limit_bytes=(48 if before else 60)*1024*1024,dimension_semantics=("arbitrary","arbitrary")),
        cost_estimate=pl.CostEstimate(flops=flops,bytes_accessed=2*count*R*L*2+20*L*128*count,transcendentals=0),
        name="attend_back",
    )(*args,*extra)

EPS=1e-6

def gelu_parts(v):
    a=jnp.abs(v)
    t=1.0/(1.0+(0.3275911/math.sqrt(2.0))*a)
    bell=jnp.exp(-0.5*v*v)
    poly=t*(0.127414796+t*(-0.142248368+t*(0.7107068705+t*(-0.7265760135+t*0.5307027145))))
    tail=poly*bell
    phi=jnp.where(v>0,1.0-tail,tail)
    return v*phi, phi+v*bell*(1.0/math.sqrt(2.0*math.pi))

class Both:
    def __init__(self,*copies):
        self.copies=copies

    def start(self):
        for copy in self.copies:
            copy.start()

    def wait(self):
        for copy in self.copies:
            copy.wait()

def feed_kernel(R,D,tiles,per,rows_in,own_rows,ctx_ref,tok_ref,og_ref,scale_ref,wl_ref,late_ref,bias_ref,gain_ref,shift_ref,
                res_ref,dres_ref,do_ref,sums_ref,bsum_ref,keep_ref,give_ref,
                u1_ref,r1_ref,low_ref,acc_ref,pre_ref,gated_ref,gp_ref,dfeed_ref,stage_ref,tail_ref,datt_ref,wf_ref,wo_ref,sem):
    step=pl.program_id(0)
    core=lax.axis_index("dp")%2
    pairs=per//2
    width=per*rows_in
    CH=64
    def chunks(f):
        def body(i,c):
            f(pl.ds(pl.multiple_of(i*CH,CH),CH))
            return c
        lax.fori_loop(0,R//CH,body,0,unroll=4)
    mean=lambda x: jnp.mean(x,axis=1,keepdims=True)
    gain=lambda i: gain_ref[i:i+1,:]
    shift=lambda i: shift_ref[i:i+1,:]
    def add_sum(i,x):
        sums_ref[i:i+1,:]+=jnp.sum(x,axis=0,keepdims=True)
    @pl.when(step==0)
    def _():
        sums_ref[...]=jnp.zeros_like(sums_ref)
        for p in range(D//own_rows):
            wf_ref[p*own_rows:(p+1)*own_rows,:]=wl_ref[p].astype(f32)[0:own_rows]
        wo_ref[...]=wf_ref[...].astype(bf)
        acc_ref[...]=dot_nn(ctx_ref[...],wo_ref[...])
        def norm(at):
            v=tok_ref[at,:].astype(f32)+acc_ref[at,:]+shift(0)
            c=v-mean(v)
            r=lax.rsqrt(mean(c*c)+EPS)
            u=c*r
            u1_ref[at,:]=u
            r1_ref[at,:]=jnp.broadcast_to(r,(CH,128))
            h=u*gain(0)+shift(1)
            low_ref[at,:]=h.astype(bf)
            acc_ref[at,:]=h+shift(2)
        chunks(norm)
    w_in=late_ref[:,0:rows_in,:].reshape(width,D)
    w_outer=late_ref[:,rows_in:2*rows_in,:].reshape(width,D)
    @pl.when(step<tiles)
    def _():
        pre_ref[...]=dot_nt(low_ref[...],w_in)
        def act(at):
            g,gp=gelu_parts(pre_ref[at,:]+bias_ref[0])
            gated_ref[step,at,:]=g.astype(bf)
            gp_ref[step,at,:]=gp.astype(bf)
        chunks(act)
        acc_ref[...]+=dot_nn(gated_ref[step],w_outer)
    @pl.when(step==tiles-1)
    def _():
        def norm(at):
            v=acc_ref[at,:]
            c=v-mean(v)
            r=lax.rsqrt(mean(c*c)+EPS)
            u=c*r
            res_ref[at,:]=(u*gain(1)+shift(3)).astype(bf)
            top=og_ref[at,:].astype(f32)
            add_sum(1,top*u)
            add_sum(5,top)
            e=top*gain(1)
            d=(e-mean(e)-u*mean(e*u))*r
            add_sum(4,d)
            dfeed_ref[at,:]=d.astype(bf)
            acc_ref[at,:]=d
        chunks(norm)
    @pl.when(step>=tiles)
    def _():
        k=step-tiles
        slot=lax.rem(k,2)
        pre_ref[...]=dot_nt(dfeed_ref[...],w_outer)
        def act(at):
            d=(pre_ref[at,:]*gp_ref[k,at,:].astype(f32)).astype(bf)
            gp_ref[k,at,:]=d
        chunks(act)
        bsum_ref[0]=jnp.sum(gp_ref[k].astype(f32),axis=0,keepdims=True)
        def out(kk,s):
            to=(pl.ds(kk*pairs,pairs),pl.ds(0,2*rows_in))
            return Both(pltpu.make_async_copy(stage_ref.at[s,:,core],keep_ref.at[to],sem.at[s,0]),
                        pltpu.make_async_copy(stage_ref.at[s,:,1-core],give_ref.at[to],sem.at[s,1]))
        @pl.when(k>=2)
        def _():
            out(k-2,slot).wait()
        stage_ref[slot,:,:,0:rows_in,:]=dot_tn(gp_ref[k],low_ref[...]).astype(bf).reshape(pairs,2,rows_in,D)
        stage_ref[slot,:,:,rows_in:2*rows_in,:]=dot_tn(gated_ref[k],dfeed_ref[...]).astype(bf).reshape(pairs,2,rows_in,D)
        out(k,slot).start()
        acc_ref[...]+=dot_nn(gp_ref[k],w_in)
        @pl.when(k==tiles-1)
        def _():
            def norm(at):
                d=acc_ref[at,:]
                u=u1_ref[at,:]
                r=r1_ref[at,0:1]
                add_sum(0,d*u)
                add_sum(3,d)
                e=d*gain(0)
                g=(e-mean(e)-u*mean(e*u))*r
                add_sum(2,g)
                dres_ref[at,:]=g
                datt_ref[at,:]=g.astype(bf)
            chunks(norm)
            do_ref[...]=(dot_nt(datt_ref[...],wo_ref[...])*scale_ref[...]).astype(bf)
            outer=dot_tn(ctx_ref[...],datt_ref[...])
            n=D//own_rows
            gap=tail_ref.shape[2]-own_rows
            for p in range(n):
                piece=outer[p*own_rows:p*own_rows+own_rows,:]
                if gap:
                    piece=jnp.concatenate([piece,jnp.zeros((gap,D),f32)],axis=0)
                tail_ref[p//2,p%2]=piece.astype(bf)
            to=(slice(None),pl.ds(2*rows_in,tail_ref.shape[2]))
            last=Both(pltpu.make_async_copy(tail_ref.at[:,core],keep_ref.at[to],sem.at[2,0]),
                      pltpu.make_async_copy(tail_ref.at[:,1-core],give_ref.at[to],sem.at[2,1]))
            last.start()
            if tiles>1:
                out(k-1,1-slot).wait()
            out(k,slot).wait()
            last.wait()

def feed(ctx,tokens,out_grad,scale,late,bias,gain,shift,rows_in,own_rows,tiles=4):
    R,D=ctx.shape
    n,rows_late,_=late.shape
    per=n//tiles
    width=per*rows_in
    tail=rows_late-2*rows_in
    vm=lambda s: pl.BlockSpec(s,lambda i: (0,)*len(s))
    return pl.pallas_call(functools.partial(feed_kernel,R,D,tiles,per,rows_in,own_rows),
        grid=(2*tiles,),
        in_specs=[vm((R,D)),vm((R,D)),vm((R,D)),vm((R,D)),pl.BlockSpec((n,tail,D),lambda i:(0,2*rows_in//tail,0)),
                  pl.BlockSpec((per,rows_late,D),lambda i:(lax.rem(i,tiles),0,0)),
                  pl.BlockSpec((1,1,width),lambda i:(lax.rem(i,tiles),0,0)),vm((2,D)),vm((4,D))],
        out_specs=[vm((R,D)),vm((R,D)),vm((R,D)),vm((8,D)),pl.BlockSpec((1,1,width),lambda i:(jnp.maximum(i-tiles,0),0,0)),
                   pl.BlockSpec(memory_space=pl.ANY),pl.BlockSpec(memory_space=pl.ANY)],
        out_shape=[jax.ShapeDtypeStruct((R,D),bf),jax.ShapeDtypeStruct((R,D),f32),jax.ShapeDtypeStruct((R,D),bf),
                   jax.ShapeDtypeStruct((8,D),f32),jax.ShapeDtypeStruct((tiles,1,width),f32),
                   jax.ShapeDtypeStruct((n//2,rows_late,D),bf),jax.ShapeDtypeStruct((n//2,rows_late,D),bf)],
        scratch_shapes=[pltpu.VMEM((R,D),f32),pltpu.VMEM((R,128),f32),pltpu.VMEM((R,D),bf),pltpu.VMEM((R,D),f32),
                        pltpu.VMEM((R,width),f32),pltpu.VMEM((tiles,R,width),bf),pltpu.VMEM((tiles,R,width),bf),
                        pltpu.VMEM((R,D),bf),pltpu.VMEM((2,per//2,2,2*rows_in,D),bf),pltpu.VMEM((n//2,2,tail,D),bf),pltpu.VMEM((R,D),bf),pltpu.VMEM((D,D),f32),pltpu.VMEM((D,D),bf),
                        pltpu.SemaphoreType.DMA((3,2))],
        compiler_params=pltpu.CompilerParams(vmem_limit_bytes=58*1024*1024,dimension_semantics=("arbitrary",)),
        cost_estimate=pl.CostEstimate(flops=2*R*D*n*rows_in*6+6*R*D*D,bytes_accessed=4*n*rows_late*D+20*R*D,transcendentals=2*R*n*rows_in),
        name="feed",
    )(ctx,tokens,out_grad,scale,late,late,bias,gain,shift)

MESH = pl.DeviceIdType.MESH
ANY = pl.BlockSpec(memory_space=pl.ANY)
VM = pl.BlockSpec(memory_space=pltpu.VMEM)

def remote(src, dst, send, recv, peer):
    return pltpu.make_async_remote_copy(src_ref=src, dst_ref=dst, send_sem=send, recv_sem=recv,
                                        device_id=peer, device_id_type=MESH)

def meet(peers):
    barrier = pltpu.get_barrier_semaphore()
    for peer in peers:
        pl.semaphore_signal(barrier, inc=1, device_id=peer, device_id_type=MESH)
    pl.semaphore_wait(barrier, len(peers))

class Place:
    def __init__(self, n_t, n_dp):
        self.n_t, self.n_dp = n_t, n_dp
        bits = (n_dp // 2).bit_length() - 1
        self.low = bits // 2
        self.high = bits - self.low
        dp, self.t = lax.axis_index("dp"), lax.axis_index("tensor")
        self.core = dp % 2
        self.down = (dp // 2) % 2**self.low
        self.up = dp // 2 // 2**self.low
        self.others = [lax.rem(self.t + 1 + i, n_t) for i in range(n_t - 1)]
        self.twin = {"dp": dp - self.core + 1 - self.core}
        self.steps = [("down", i) for i in range(self.low)] + [("up", i) for i in range(self.high)]

    def bit(self, step):
        kind, i = step
        return (getattr(self, kind) // 2**i) % 2

    def peer(self, step):
        kind, i = step
        turn = (1 - 2 * self.bit(step)) * 2**i
        down = self.down + turn if kind == "down" else self.down
        up = self.up + turn if kind == "up" else self.up
        return {"dp": (up * 2**self.low + down) * 2 + self.core}

    def peers(self):
        return [{"tensor": o} for o in self.others] + [self.twin] + [self.peer(s) for s in self.steps]

    def orders(self):
        down = [s for s in self.steps if s[0] == "down"]
        up = [s for s in self.steps if s[0] == "up"]
        return [down + up, up + down]

    def spans(self, done):
        out = []
        for kind in ("up", "down"):
            n = sum(1 for s in done if s[0] == kind)
            here = getattr(self, kind)
            out.append(pl.ds((here // 2**n) * 2**n, 2**n))
        return out

    def parts(self):
        half = self.n_t // 2
        return [pl.ds(0, half), pl.ds(half, half)] if half else [pl.ds(0, 1)]

class Line:
    def __init__(self, t, n, own, slot, rows, pieces, send, recv):
        self.t, self.n, self.own, self.slot = t, n, own, slot
        self.rows, self.pieces, self.send, self.recv = rows, pieces, send, recv

    def piece(self, ref, j):
        size = self.rows // self.pieces
        return ref.at[pl.ds(j * size, size)]

    def copy(self, d, s, j, b, own):
        at = self.piece(self.slot(b), j)
        src = self.piece(self.own, j) if own else at
        peer = {"tensor": self.t + 1 - 2 * d}
        return remote(src, at, self.send.at[d, s, j], self.recv.at[d, s, j], peer)

    def post(self, s, j):
        for d in range(2):
            b = self.t - s + 2 * d * s
            go_on = (b >= 0) & (self.t + 1 < self.n) if d == 0 else (b < self.n) & (self.t > 0)

            @pl.when(go_on)
            def _():
                self.copy(d, s, j, b, s == 0).start()

    def take(self, s, j):
        for d in range(2):
            b = self.t - 1 - s if d == 0 else self.t + 1 + s

            @pl.when(b >= 0 if d == 0 else b < self.n)
            def _():
                self.copy(d, s, j, b, False).wait_recv()

    def step(self, s):
        for j in range(self.pieces):
            self.take(s, j)
            if s + 1 < self.n - 1:
                self.post(s + 1, j)

    def drain(self):
        for s in range(self.n - 1):
            for j in range(self.pieces):
                for d in range(2):
                    b = self.t - s + 2 * d * s

                    @pl.when((b >= 0) & (self.t + 1 < self.n) if d == 0 else (b < self.n) & (self.t > 0))
                    def _():
                        self.copy(d, s, j, b, s == 0).wait_send()

def lanes_of(count, width, shape, tall):
    wide_axis = 0 if tall else 1
    f = lax.broadcasted_iota(jnp.int32, shape, wide_axis)
    r = lax.broadcasted_iota(jnp.int32, shape, 1 - wide_axis)
    return jnp.where(f % count == r, 1.0, 0.0).astype(bf)

def spread_row(table, count, width, first):
    n = table.shape[0]
    full = dot_nn(table.astype(bf), lanes_of(count, width, (128, width), False))
    p = lax.broadcasted_iota(jnp.int32, (n, width), 0)
    f = lax.broadcasted_iota(jnp.int32, (n, width), 1)
    return jnp.sum(jnp.where(first + f // count == p, full, 0.0), axis=0, keepdims=True)

def fold_row(row, count, n, first):
    width = row.shape[1]
    p = lax.broadcasted_iota(jnp.int32, (n, width), 0)
    f = lax.broadcasted_iota(jnp.int32, (n, width), 1)
    full = jnp.where(first + f // count == p, jnp.broadcast_to(row, (n, width)), 0.0)
    return dot_nn(full.astype(bf), lanes_of(count, width, (width, 128), True))

def eight(n):
    return -(-n // 8) * 8

def begin_kernel(n_t, n_dp, own, part, cols, inner, tiles, L,
                 tok_ref, wq_ref, wk_ref, wv_ref, rel_ref, qkvb_ref, ffb_ref, gains_ref, shifts_ref, ahead_ref, back_ref, fin_ref, fout_ref, wo_ref,
                 q_out, k_out, v_out, krel_out, qrel_out, kt_out, qr_out, toks_out, w_out, ox_out, oy_out, table_out, late_all,
                 ibias_ref, gain_ref, shift_ref,
                 toks, packs, pack, packf, wf, w, kb, vb, qb, krel, qrel, kt, qr, table, tableb, miscf, ox, ox_tall, oy_tall,
                 tok_send, tok_recv, z_send, z_recv, x_send, x_recv, out_sem, lz_send, lz_recv, lx_send, lx_recv, lc_send, lc_recv, late_ref, latef):
    at = Place(n_t, n_dp)
    t = at.t
    R, D = tok_ref.shape
    W = L + R
    n_all = n_t * n_dp
    S, S2 = eight(own), eight(part)
    misc = 3 * S + S2

    packf[...] = jnp.zeros_like(packf)
    for i, ref in enumerate((wq_ref, wk_ref, wv_ref)):
        packf[i * S:i * S + own, :] = ref[...].astype(f32)
    for i in range(n_t):
        @pl.when(t == i)
        def _():
            packf[3 * S:3 * S + part, :] = rel_ref[...].astype(f32)[i * part:(i + 1) * part]
    for i in range(3):
        packf[misc:misc + 1, 128 * i:128 * i + own] = qkvb_ref[i:i + 1, :].astype(f32)
    packf[misc:misc + 1, 384:384 + inner] = ffb_ref[...].astype(f32)
    for i in range(2):
        packf[misc + 1:misc + 2, 128 * i:128 * i + cols] = gains_ref[i:i + 1, :].astype(f32)
    for i in range(4):
        packf[misc + 1:misc + 2, 256 + 128 * i:256 + 128 * i + cols] = shifts_ref[i:i + 1, :].astype(f32)
    pack[...] = packf[...].astype(bf)
    latef[...] = jnp.zeros_like(latef)
    at_row = 0
    for ref in (fin_ref, fout_ref, wo_ref):
        latef[at_row:at_row + ref.shape[0], :] = ref[...].astype(f32)
        at_row += ref.shape[0]
    late_ref[...] = latef[...].astype(bf)

    meet(at.peers())
    copies = []

    def go(copy):
        copy.start()
        copies.append(copy)
        return copy

    here = packs.at[t, at.up, at.down, at.core]
    column = Line(t, n_t, pack, lambda i: packs.at[i, at.up, at.down, at.core], pack.shape[0], 1, z_send, z_recv)
    tokens = Line(t, n_t, tok_ref, lambda i: toks.at[i], R, 2, tok_send, tok_recv)
    late = Line(t, n_t, late_ref, lambda i: late_all.at[i, at.up, at.down, at.core], late_ref.shape[0], 1, lz_send, lz_recv)
    column.post(0, 0)
    late.post(0, 0)
    own_late = pltpu.make_async_copy(late_ref, late_all.at[t, at.up, at.down, at.core], out_sem.at[out_sem.shape[0] - 1])
    own_late.start()
    own_pack = pltpu.make_async_copy(pack, here, out_sem.at[0])
    own_pack.start()
    outs = []

    def put(src, dst):
        copy = pltpu.make_async_copy(src, dst, out_sem.at[1 + len(outs)])
        copy.start()
        outs.append(copy)

    def pick(line, start):
        rows = line[:, pl.ds(pl.multiple_of(start, 128), W)]
        ids = lax.broadcasted_iota(jnp.int32, (NB, W), 0)
        return jnp.where(ids == rows, 1.0, 0.0).astype(bf)

    ox[...] = pick(back_ref, L - R - R * t)
    ox_tall[...] = ox[...].T
    oy_tall[...] = pick(ahead_ref, L - R - R * t).T
    put(ox_tall, ox_out)
    put(oy_tall, oy_out)

    for s in range(n_t - 1):
        column.step(s)
        if s < n_t - 2:
            late.step(s)
        if s == n_t - 3 or n_t < 3:
            for j in range(2):
                tokens.post(0, j)
    own_pack.wait()
    parts, orders = at.parts(), at.orders()
    n_steps = len(at.steps)
    swaps = {}

    def swap(h, k):
        if k:
            swaps[h, k - 1].wait_recv()
        up, down = at.spans(orders[h][:k])
        if k < n_steps:
            piece, peer = packs.at[parts[h], up, down, at.core], at.peer(orders[h][k])
        else:
            piece, peer = packs.at[parts[h], :, :, at.core], at.twin
        swaps[h, k] = go(remote(piece, piece, x_send.at[h, k], x_recv.at[h, k], peer))

    hs = range(len(parts))
    moves = {}

    def late_twin(h, k):
        up, down = at.spans(orders[h][:k])
        if k:
            kind, i = orders[h][k - 1]
            base = (getattr(at, kind) // 2**(i + 1)) * 2**(i + 1)
            other = pl.ds(base + (1 - at.bit((kind, i))) * 2**i, 2**i)
            up, down = (other, down) if kind == "up" else (up, other)
        piece = late_all.at[parts[h], up, down, at.core]
        moves[h, k, "twin"] = go(remote(piece, piece, lc_send.at[h, k], lc_recv.at[h, k], at.twin))

    def late_swap(k):
        for h in hs:
            if k:
                moves[h, k - 1, "swap"].wait_recv()
            if k < n_steps:
                up, down = at.spans(orders[h][:k])
                piece = late_all.at[parts[h], up, down, at.core]
                moves[h, k, "swap"] = go(remote(piece, piece, lx_send.at[h, k], lx_recv.at[h, k], at.peer(orders[h][k])))
            late_twin(h, k)

    for h in hs:
        swap(h, 0)
    late.step(n_t - 2)
    own_late.wait()
    late_swap(0)
    passed = 0
    for k in range(1, n_steps + 1):
        for h in hs:
            swap(h, k)
    if n_t > 2:
        tokens.step(0)
        passed = 1
    for h in hs:
        swaps[h, n_steps].wait_recv()

    slots = [(a, u, d, c) for a in range(n_t) for u in range(2**at.high) for d in range(2**at.low) for c in range(2)]
    for i in range(3):
        for p, s in enumerate(slots):
            wf[p * own:p * own + own, :] = packs[s[0], s[1], s[2], s[3], i * S:i * S + own, :].astype(f32)
        w[i] = wf[...].astype(bf)
    put(w, w_out)
    for p, s in enumerate(slots):
        rows = packs[s[0], s[1], s[2], s[3], misc:misc + 8, :].astype(f32)
        miscf[0, p:p + 1, :] = rows[0:1]
        miscf[1, p:p + 1, :] = rows[1:2]
        a, dp = p // n_dp, p % n_dp
        to = dp * n_t * part + a * part
        table[to:to + part, :] = packs[s[0], s[1], s[2], s[3], 3 * S:3 * S + part, :].astype(f32)
    if n_steps:
        late_swap(1)
    bias = [spread_row(miscf[0, :, 128 * i:128 * i + 128], own, D, 0) for i in range(3)]
    rel = table[...].astype(bf)
    tableb[...] = rel
    put(tableb, table_out)
    krel[...] = (dot_nt(rel, w[1]) + bias[1]).astype(bf)
    qrel[...] = (dot_nt(rel, w[0]) + bias[0]).astype(bf)
    put(krel, krel_out)
    put(qrel, qrel_out)
    kt[...] = dot_tn(ox[...], krel[...]).astype(bf)
    put(kt, kt_out)
    qr[...] = dot_tn(pick(back_ref, R * t), qrel[...]).astype(bf)
    put(qr, qr_out)
    if n_t > 3:
        tokens.step(1)
        passed = 2

    def project(tokens, i):
        return (dot_nt(tokens, w[i]) + bias[i]).astype(bf)

    qb[...] = project(tok_ref[...], 0)
    put(qb, q_out)
    width = n_all * inner // tiles
    for i in range(tiles):
        ibias_ref[i] = spread_row(miscf[0, :, 384:512], inner, width, i * (n_all // tiles))
    for i in range(2):
        gain_ref[i:i + 1, :] = spread_row(miscf[1, 0:n_dp, 128 * i:128 * i + 128], cols, D, 0)
    for i in range(4):
        shift_ref[i:i + 1, :] = spread_row(miscf[1, 0:n_dp, 256 + 128 * i:384 + 128 * i], cols, D, 0)

    for s in range(n_t):
        b = lax.rem(t - s + n_t, n_t)
        rows = pl.ds(pl.multiple_of(b * R, R), R)
        if s == 1:
            for k in range(2, n_steps + 1):
                late_swap(k)
            for i in range(passed, n_t - 1):
                tokens.step(i)
        src = tok_ref if s == 0 else toks.at[b]
        put(src, toks_out.at[b])
        kb[s] = project(src[...], 1)
        put(kb.at[s], k_out.at[rows])
        vb[s] = project(src[...], 2)
        put(vb.at[s], v_out.at[rows])
    for h in hs:
        for k in range(n_steps + 1):
            moves[h, k, "twin"].wait_recv()
    for copy in outs:
        copy.wait()
    for copy in copies:
        copy.wait_send()
    column.drain()
    late.drain()
    tokens.drain()

def begin(tokens, w_query, w_key, w_value, rel_table, qkv_bias, ff_bias, gains, shifts, ahead, back, w_ff_in, w_ff_out, w_out, n_t, n_dp, tiles):
    R, D = tokens.shape
    L = ahead.shape[1] // 2
    W = L + R
    own, inner, cols = w_query.shape[0], ff_bias.shape[1], gains.shape[1]
    part = rel_table.shape[0] // n_t
    n_all = n_t * n_dp
    width = n_all * inner // tiles
    PR = -(-(3 * eight(own) + eight(part) + 8) // 16) * 16
    LR = -(-(2 * w_ff_in.shape[0] + own) // 16) * 16
    bits = (n_dp // 2).bit_length() - 1
    low = bits // 2
    S = jax.ShapeDtypeStruct
    big = [(R, D), (L, D), (L, D), (NB, D), (NB, D), (W, D), (W, D), (n_t, R, D), (3, D, D), (W, NB), (W, NB), (NB, D),
           (n_t, 2**(bits - low), 2**low, 2, LR, D)]
    v = lambda s, t=bf: pltpu.VMEM(s, t)
    dma = lambda *s: pltpu.SemaphoreType.DMA(s)
    return pl.pallas_call(
        functools.partial(begin_kernel, n_t, n_dp, own, part, cols, inner, tiles, L),
        out_shape=[S(s, bf) for s in big] + [S((tiles, 1, width), f32), S((2, D), f32), S((4, D), f32)],
        in_specs=[VM] * 14, out_specs=[ANY] * len(big) + [VM] * 3,
        scratch_shapes=[v((n_t, R, D)), v((n_t, 2**(bits - low), 2**low, 2, PR, D)), v((PR, D)), v((PR, D), f32), v((D, D), f32),
                        v((3, D, D)), v((n_t, R, D)), v((n_t, R, D)), v((R, D)), v((NB, D)), v((NB, D)), v((W, D)), v((W, D)),
                        v((NB, D), f32), v((NB, D)), v((2, n_all, D), f32), v((NB, W)), v((W, NB)), v((W, NB)),
                        dma(2, n_t - 1, 2), dma(2, n_t - 1, 2), dma(2, n_t - 1, 1), dma(2, n_t - 1, 1), dma(2, bits + 1), dma(2, bits + 1),
                        dma(11 + 3 * n_t), dma(2, n_t - 1, 1), dma(2, n_t - 1, 1), dma(2, max(bits, 1)), dma(2, max(bits, 1)), dma(2, bits + 1), dma(2, bits + 1),
                        v((LR, D)), v((LR, D), f32)],
        compiler_params=pltpu.CompilerParams(collective_id=0, has_side_effects=True, vmem_limit_bytes=58 * 1024 * 1024),
        name="begin",
    )(tokens, w_query, w_key, w_value, rel_table, qkv_bias, ff_bias, gains, shifts, ahead, back, w_ff_in, w_ff_out, w_out)

def finish_kernel(n_t, n_dp, own, rel_rows, cols, inner, tiles,
                  dq_in, dk_in, dv_in, tok_in, toks_in, w_in, table_in, dqr_in, dkr_in, dres_in, sums_ref, bsum_ref,
                  tg_ref, gq_ref, gk_ref, gv_ref, rel_ref, qkvb_ref, ffb_ref, gains_ref, shifts_ref,
                  dq, dk, dv, tok, toks, w, table, dqr, dkr, dres, g, relf, m0, m1, miscs, pack, first, acc, got, total,
                  tok_got, tok_acc, tok_own, base, *rest):
    at = Place(n_t, n_dp)
    t = at.t
    n_steps = len(at.steps)
    bufs, (in_sem, tok_send, tok_recv, x_send, x_recv, z_send, z_recv) = rest[:2 * n_steps], rest[2 * n_steps:]
    R, D = tok.shape
    L = n_t * R
    n_all = n_t * n_dp
    S, S3 = eight(own), eight(rel_rows)
    misc = 3 * S
    PR = pack.shape[4]
    right = {"tensor": lax.rem(t + 1, n_t)}
    loads = []

    def load(src, dst):
        copy = pltpu.make_async_copy(src, dst, in_sem.at[len(loads)])
        copy.start()
        loads.append(copy)
        return copy

    def block(s):
        return lax.rem(t - 1 - s + 2 * n_t, n_t)

    l_w = load(w_in, w)
    l_kv = []
    for s in range(n_t):
        b = block(s)
        l_kv.append((load(dk_in.at[b], dk.at[b]), load(dv_in.at[b], dv.at[b])))
    l_toks = load(toks_in, toks)
    l_rest = [load(tok_in, tok), load(dq_in, dq), load(table_in, table), load(dqr_in, dqr), load(dkr_in, dkr), load(dres_in, dres)]
    meet(at.peers())
    copies = []

    def go(copy):
        copy.start()
        copies.append(copy)
        return copy

    half = R // 2
    token = {}

    def partial(s):
        for copy in l_kv[s]:
            copy.wait()
        b = block(s)
        return dot_nn(dk[b], w[1]) + dot_nn(dv[b], w[2])

    def send_token(s):
        for j in range(2):
            rows = pl.ds(j * half, half)
            if s:
                token[s - 1, j].wait_recv()
                tok_acc[s, rows] = (tok_own[rows].astype(f32) + tok_got[s - 1, rows].astype(f32)).astype(bf)
            token[s, j] = go(remote(tok_acc.at[s, rows], tok_got.at[s, rows], tok_send.at[s, j], tok_recv.at[s, j], right))

    l_w.wait()
    tok_acc[0] = partial(0).astype(bf)
    send_token(0)
    for s in range(1, n_t):
        for copy in l_kv[s]:
            copy.wait()
    l_kv = [()] * n_t
    l_toks.wait()
    for copy in l_rest:
        copy.wait()
    dqb, dkb = dqr[...].astype(bf), dkr[...].astype(bf)
    rel_table = table[...]
    g[0] = dot_tn(dq[...], tok[...]) + dot_tn(dqb, rel_table)
    g[1] = dot_tn(dk[...].reshape(L, D), toks[...].reshape(L, D)) + dot_tn(dkb, rel_table)
    g[2] = dot_tn(dv[...].reshape(L, D), toks[...].reshape(L, D))
    relf[...] = dot_nn(dqb, w[0]) + dot_nn(dkb, w[1])
    ones = lambda n: jnp.ones((8, n), bf)
    columns = [dot_nn(ones(R), dq[...])[0:1] + jnp.sum(dqr[...], axis=0, keepdims=True),
               dot_nn(ones(L), dk[...].reshape(L, D))[0:1] + jnp.sum(dkr[...], axis=0, keepdims=True),
               dot_nn(ones(L), dv[...].reshape(L, D))[0:1]]
    for i in range(3):
        m0[:, 128 * i:128 * i + 128] = fold_row(columns[i], own, n_all, 0)
    units = jnp.zeros((n_all, 128), f32)
    for i in range(tiles):
        units += fold_row(bsum_ref[i], inner, n_all, i * (n_all // tiles))
    m0[:, 384:512] = units
    for i in range(6):
        m1[:, 128 * i:128 * i + 128] = fold_row(sums_ref[i:i + 1, :], cols, n_dp, 0)
    miscs[...] = jnp.zeros_like(miscs)
    slots = [(a, u, d, c) for a in range(n_t) for u in range(2**at.high) for d in range(2**at.low) for c in range(2)]

    def padded(x, n):
        return jnp.concatenate([x, jnp.zeros((n - x.shape[0], D), f32)], axis=0) if n > x.shape[0] else x

    parts = at.parts()
    hs = range(len(parts))
    per = n_t // len(parts)
    orders = [list(reversed(o)) for o in at.orders()][:len(parts)]
    swaps = {}
    left = {h: {"up": at.high, "down": at.low} for h in hs}

    def region(h, cut=None):
        out = []
        for kind in ("up", "down"):
            n = left[h][kind]
            here = getattr(at, kind)
            if cut is not None and cut[0] == kind:
                start = (here // 2**n) * 2**n + (1 - at.bit(cut)) * 2**(n - 1)
                out.append((start, 2**(n - 1)))
            else:
                out.append(((here // 2**n) * 2**n, 2**n))
        return out

    def start(h, k):
        if k == 0:
            src, dst, peer = pack.at[parts[h], :, :, 1 - at.core], first.at[parts[h]], at.twin
        else:
            cut = orders[h][k - 1]
            up, down = [pl.ds(*x) for x in region(h, cut)]
            src, dst, peer = acc.at[parts[h], up, down], bufs[h * n_steps + k - 1], at.peer(cut)
        swaps[h, k] = go(remote(src, dst, x_send.at[h, k], x_recv.at[h, k], peer))

    def absorb(h, k):
        swaps[h, k].wait_recv()
        if k:
            left[h][orders[h][k - 1][0]] -= 1
        (u0, nu), (d0, nd) = region(h)
        buf = first if k == 0 else bufs[h * n_steps + k - 1]

        @pl.loop(0, per * nu * nd)
        def _(m):
            a, u, d = m // (nu * nd), m // nd % nu, m % nd
            if k == 0:
                x, y = pack[h * per + a, u, d, at.core], buf[h * per + a, u, d]
            else:
                x, y = acc[h * per + a, u0 + u, d0 + d], buf[a, u, d]
            acc[h * per + a, u0 + u, d0 + d] = (x.astype(f32) + y.astype(f32)).astype(bf)

    for p, s in enumerate(slots):
        dp = p % n_dp
        miscs[8 * p:8 * p + 1, 0:512] = m0[p:p + 1, :]
        miscs[8 * p + 1:8 * p + 2, :] = m1[dp:dp + 1, :]
        pieces = [padded(g[i, p * own:p * own + own, :], S) for i in range(3)]
        pieces += [miscs[8 * p:8 * p + 8, :], padded(relf[dp * rel_rows:dp * rel_rows + rel_rows, :], S3)]
        whole = padded(jnp.concatenate(pieces, axis=0), PR)
        pack[s[0], s[1], s[2], s[3]] = whole.astype(bf)
        if (p + 1) % (per * n_dp) == 0:
            start(p // (per * n_dp), 0)
    tok_own[...] = partial(1).astype(bf)
    sent = 1
    if n_t > 2:
        send_token(1)
        sent = 2
        tok_own[...] = partial(2).astype(bf)
    base[...] = partial(n_t - 1) + dres[...] + dot_nn(dq[...], w[0])
    for k in range(n_steps + 1):
        for h in hs:
            absorb(h, k)
            if k < n_steps:
                start(h, k + 1)
        if k == n_steps:
            ring = [go(remote(acc.at[o, at.up, at.down], got.at[i], z_send.at[i], z_recv.at[i], {"tensor": o}))
                    for i, o in enumerate(at.others)]
        if k and sent < n_t - 1:
            send_token(sent)
            sent += 1
            if sent < n_t - 1:
                tok_own[...] = partial(sent).astype(bf)
    for copy in ring:
        copy.wait_recv()
    total[...] = acc[t, at.up, at.down].astype(f32)
    for i in range(n_t - 1):
        total[...] += got[i].astype(f32)
    for i, ref in enumerate((gq_ref, gk_ref, gv_ref)):
        ref[...] = total[i * S:i * S + own, :]
    rel_ref[...] = total[misc + 8:misc + 8 + rel_rows, :]
    for i in range(3):
        qkvb_ref[i:i + 1, :] = total[misc:misc + 1, 128 * i:128 * i + own]
    ffb_ref[...] = total[misc:misc + 1, 384:384 + inner]
    for i in range(2):
        gains_ref[i:i + 1, :] = total[misc + 1:misc + 2, 128 * i:128 * i + cols]
    for i in range(4):
        shifts_ref[i:i + 1, :] = total[misc + 1:misc + 2, 256 + 128 * i:256 + 128 * i + cols]
    while sent < n_t - 1:
        send_token(sent)
        sent += 1
        if sent < n_t - 1:
            tok_own[...] = partial(sent).astype(bf)
    for j in range(2):
        rows = pl.ds(j * half, half)
        token[n_t - 2, j].wait_recv()
        tg_ref[rows, :] = base[rows, :] + tok_got[n_t - 2, rows].astype(f32)
    for copy in copies:
        copy.wait_send()

def finish(dq, dk, dv, tok, toks, w, table, dqr, dkr, dres, sums, bsum, own, rel_rows, cols, inner, n_t, n_dp):
    R, D = tok.shape
    L = n_t * R
    n_all = n_t * n_dp
    tiles = bsum.shape[0]
    S3 = eight(rel_rows)
    PR = -(-(3 * eight(own) + 8 + S3) // 16) * 16
    bits = (n_dp // 2).bit_length() - 1
    low = bits // 2
    high = bits - low
    per = n_t // 2
    v = lambda s, x=bf: pltpu.VMEM(s, x)
    dma = lambda *s: pltpu.SemaphoreType.DMA(s)
    bufs = []
    for order in ([("up", high), ("down", low)], [("down", low), ("up", high)]):
        left = {"up": high, "down": low}
        for kind, n in order:
            for _ in range(n):
                left[kind] -= 1
                bufs.append(v((per, 2**left["up"], 2**left["down"], PR, D)))
    S = jax.ShapeDtypeStruct
    outs = [(R, D), (own, D), (own, D), (own, D), (rel_rows, D), (3, own), (1, inner), (2, cols), (4, cols)]
    blocks = lambda x: x.reshape(n_t, R, D)
    return pl.pallas_call(
        functools.partial(finish_kernel, n_t, n_dp, own, rel_rows, cols, inner, tiles),
        out_shape=[S(s, f32) for s in outs],
        in_specs=[ANY] * 10 + [VM] * 2, out_specs=[VM] * len(outs),
        scratch_shapes=[v((R, D)), v((n_t, R, D)), v((n_t, R, D)), v((R, D)), v((n_t, R, D)), v((3, D, D)), v((NB, D)),
                        v((NB, D), f32), v((NB, D), f32), v((R, D), f32), v((3, D, D), f32), v((NB, D), f32),
                        v((n_all, 512), f32), v((n_dp, D), f32), v((8 * n_all, D), f32),
                        v((n_t, 2**high, 2**low, 2, PR, D)), v((n_t, 2**high, 2**low, PR, D)), v((n_t, 2**high, 2**low, PR, D)),
                        v((n_t - 1, PR, D)), v((PR, D), f32),
                        v((n_t - 1, R, D)), v((n_t - 1, R, D)), v((R, D)), v((R, D), f32)] + bufs
                       + [dma(2 * n_t + 8), dma(n_t - 1, 2), dma(n_t - 1, 2), dma(2, bits + 1), dma(2, bits + 1), dma(n_t - 1), dma(n_t - 1)],
        compiler_params=pltpu.CompilerParams(collective_id=1, has_side_effects=True, vmem_limit_bytes=60 * 1024 * 1024),
        name="finish",
    )(dq, blocks(dk), blocks(dv), tok, blocks(toks), w, table, dqr, dkr, dres, sums, bsum)

GROUPS, TILES = 32, 4
ALL=("tensor","dp")

def fold(name, grid, place, terms, shapes, out_maps):
    tail = terms[0][0].shape[-2:]
    block = lambda x, where: pl.BlockSpec((1,) * (len(x.shape) - 2) + tail, lambda *i: tuple(where(*i)) + (0, 0))
    n = len(terms)

    def kernel(place_ref, *refs):
        for k in range(n):
            x, y, out = refs[2 * k], refs[2 * k + 1], refs[2 * n + k]
            out[...] = (x[...].astype(f32) + y[...].astype(f32)).reshape(out.shape).astype(bf)

    outs = [jax.ShapeDtypeStruct(s + tail, bf) for s in shapes]
    return pl.pallas_call(
        kernel, out_shape=outs,
        grid_spec=pltpu.PrefetchScalarGridSpec(
            num_scalar_prefetch=1, grid=grid,
            in_specs=[block(z, where) for x, y, where in terms for z in (x, y)],
            out_specs=[block(o, where) for o, where in zip(outs, out_maps)]),
        compiler_params=pltpu.CompilerParams(vmem_limit_bytes=32 * 1024 * 1024, dimension_semantics=("arbitrary",) * len(grid)),
        cost_estimate=pl.CostEstimate(flops=0, bytes_accessed=sum(6 * math.prod(o.shape) for o in outs), transcendentals=0),
        name=name,
    )(place, *[z for x, y, _ in terms for z in (x, y)])

def finish_plain(dq, dk, dv, tok, toks, w, table, dqr, dkr, dres, sums, bsum, own, rel_rows, cols, inner, n_t, n_dp):
    times = lambda s, a, b: jnp.einsum(s, a.astype(bf), b.astype(bf), preferred_element_type=f32)
    scatter = lambda x: lax.psum_scatter(x, ALL, scatter_dimension=0, tiled=True)
    grads = [times("tf,td->fd", dq, tok) + times("tf,td->fd", dqr, table),
             times("tf,td->fd", dk, toks) + times("tf,td->fd", dkr, table), times("tf,td->fd", dv, toks)]
    rel = times("bf,fd->bd", dqr, w[0]) + times("bf,fd->bd", dkr, w[1])
    spread = (times("tf,fd->td", dk, w[1]) + times("tf,fd->td", dv, w[2])).astype(bf)
    back_sum = lax.psum_scatter(spread, "tensor", scatter_dimension=0, tiled=True).astype(f32)
    tokens_grad = dres + times("tf,fd->td", dq, w[0]) + back_sum
    column = lambda x: jnp.sum(x.astype(f32), axis=0)
    bias = jnp.stack([column(dq) + column(dqr), column(dk) + column(dkr), column(dv)])
    every = lambda x: lax.psum(x, ALL)
    dp = lax.axis_index("dp")
    place = lax.axis_index("tensor") * n_dp + dp
    cut = lambda x, i, n: lax.dynamic_slice_in_dim(x, i * n, n, 1)
    rel = lax.dynamic_slice_in_dim(every(rel), dp * rel_rows, rel_rows, 0)
    return [tokens_grad] + [scatter(x) for x in grads] + [rel, cut(every(bias), place, own), cut(every(bsum.reshape(1, -1)), place, inner),
            cut(every(sums[:2]), dp, cols), cut(every(sums[2:6]), dp, cols)]

def local(tokens, w_query, w_key, w_value, w_out, qkv_bias, w_ff_in, w_ff_out, ff_bias, rel_table,
          gains, shifts, rel_bucket, lengths, out_grad):
    D = tokens.shape[1]
    n_t, n_dp = lax.axis_size("tensor"), lax.axis_size("dp")
    n_all = n_t * n_dp
    t = lax.axis_index("tensor")
    R = tokens.shape[0]
    L = (rel_bucket.shape[0] + 1) // 2
    W = L + R
    own_rows, cols, inner = w_query.shape[0], gains.shape[1], ff_bias.shape[0]
    none = jnp.full((1,), -1, jnp.int32)
    ahead = jnp.concatenate([rel_bucket, none])[None]
    back = jnp.concatenate([rel_bucket[::-1], none])[None]
    late_rows = w_ff_in.shape[0]
    even = late_rows % 16 == 0 and own_rows % 8 == 0
    late_own = 2 * late_rows + own_rows
    late_all_rows = late_own + -late_own % 16
    (query, key, value, key_rel, query_rel, key_table, query_table, gathered, weights, pick_x, pick_y, table,
     late_all, inner_bias, gain, shift) = begin(tokens, w_query, w_key, w_value, rel_table, qkv_bias, ff_bias.reshape(1, -1), gains, shifts,
                                      ahead, back, w_ff_in, w_ff_out, w_out, n_t, n_dp, TILES)
    gathered = gathered.reshape(L, D)
    late_all = late_all.reshape(n_all, -1, D)
    cut = lambda x, at, n: x[:, at:at + n].reshape(n_all * n, D)
    groups = n_all if even else GROUPS
    group_rows, group_own = n_all * late_rows // groups, D // groups
    if not even:
        sections = [cut(late_all, 0, late_rows), cut(late_all, late_rows, late_rows), cut(late_all, 2 * late_rows, own_rows)]
        late_all = jnp.concatenate([x.reshape(groups, -1, D) for x in sections]
                                   + [jnp.zeros((groups, -group_own % 16, D), bf)], axis=1)
    mask = jnp.where(jnp.arange(L, dtype=jnp.int32) < lengths[0], 0.0, -1e9).astype(bf)
    mask = jnp.broadcast_to(mask[:, None], (L, 128))

    context, scale, shares = attention_forward(query, key, value, key_table, query_table, mask)
    layer_result_rows, d_resid_one, d_scaled, sums, bias_sums, keep, give = feed(
        context, tokens, out_grad, scale, late_all, inner_bias, gain, shift, group_rows, group_own)
    back_args = (query, key, value, d_scaled, context, shares, key_rel, query_rel, pick_x, pick_y)
    pairs = D // 128
    if even and n_dp == 8 and n_t % 2 == 0 and pairs >= 6:
        dp = lax.axis_index("dp")
        place = jnp.stack([dp // 4, dp // 2 % 2]).astype(jnp.int32)
        swap = lambda x, mask: lax.ppermute(x, "dp", [(i, i ^ mask) for i in range(n_dp)])
        shape = (n_t, 2, 2, late_all_rows, D)
        keep, give = keep.reshape(shape), give.reshape(shape)
        got = swap(give, 1)
        half = n_t // 2
        *grads, keep = attention_backward(*back_args, p0=0, count=pairs - 5, through=[keep])
        stay_one, away_one, stay_two, away_two = fold(
            "fold", (half, 2), place,
            [(keep, got, lambda i, j, s: (i, s[0], j)), (keep, got, lambda i, j, s: (i, 1 - s[0], j)),
             (keep, got, lambda i, j, s: (half + i, j, s[1])), (keep, got, lambda i, j, s: (half + i, j, 1 - s[1]))],
            [(half, 2)] * 4, [lambda i, j, s: (i, j)] * 4)
        got_one, got_two = swap(away_one, 4), swap(away_two, 2)
        *grads, stay_one, stay_two = attention_backward(
            *back_args, p0=pairs - 5, count=2, before=grads, after=[away_one, away_two], through=[stay_one, stay_two])
        stay_one, away_one, stay_two, away_two = fold(
            "fold", (half,), place,
            [(stay_one, got_one, lambda i, s: (i, s[1])), (stay_one, got_one, lambda i, s: (i, 1 - s[1])),
             (stay_two, got_two, lambda i, s: (i, s[0])), (stay_two, got_two, lambda i, s: (i, 1 - s[0]))],
            [(half,)] * 4, [lambda i, s: (i,)] * 4)
        got_one, got_two = swap(away_one, 2), swap(away_two, 4)
        *grads, stay_one, stay_two = attention_backward(
            *back_args, p0=pairs - 3, count=1, before=grads, after=[away_one, away_two], through=[stay_one, stay_two])
        column = jnp.concatenate(fold(
            "fold", (half,), place,
            [(stay_one, got_one, lambda i, s: (i,)), (stay_two, got_two, lambda i, s: (i,))],
            [(half,)] * 2, [lambda i, s: (i,)] * 2), axis=0)
        late_sum = lax.psum_scatter(column, "tensor", scatter_dimension=0, tiled=True)[0]
        grads = attention_backward(*back_args, p0=pairs - 2, count=2, before=grads, after=[column])
    else:
        grads = attention_backward(*back_args)
        core = lax.axis_index("dp") % 2
        late_grad = jnp.where(core == 0, jnp.stack([keep, give], axis=1), jnp.stack([give, keep], axis=1))
        late_grad = late_grad.reshape(groups, -1, D)
        parted = lambda x: x.reshape(n_all, -1, D)
        if not even:
            late_grad = jnp.concatenate([
                parted(late_grad[:, :group_rows]), parted(late_grad[:, group_rows:2 * group_rows]),
                parted(late_grad[:, 2 * group_rows:2 * group_rows + group_own]),
                jnp.zeros((n_all, late_all_rows - late_own, D), bf)], axis=1)
        late_sum = lax.psum_scatter(late_grad, ALL, scatter_dimension=0, tiled=True)[0]
    d_query, d_key, d_value, d_key_rel, d_query_rel = grads
    late_sum = late_sum.astype(f32)
    g_inner, g_outer, g_out = late_sum[:late_rows], late_sum[late_rows:2 * late_rows], late_sum[2 * late_rows:late_own]
    ends = (d_query, d_key, d_value, tokens, gathered, weights, table, d_query_rel, d_key_rel, d_resid_one, sums, bias_sums)
    rel_rows = rel_table.shape[0]
    finished = (finish if even else finish_plain)(*ends, own_rows, rel_rows, cols, inner, n_t, n_dp)
    tokens_grad, g_query, g_key, g_value, g_rel, g_qkv_bias, g_ff_bias, g_gains, g_shifts = finished
    return (layer_result_rows, tokens_grad, g_query, g_key, g_value, g_out,
            g_qkv_bias, g_inner, g_outer, g_ff_bias.reshape(inner), g_rel, g_gains, g_shifts)

def solution(mesh):
    rows, params = P(("dp", "tensor"), None), P(ALL, None)
    return jax.shard_map(
        local, mesh=mesh,
        in_specs=(rows, params, params, params, params, P(None, ALL), params, params, P(ALL), P("dp", None),
                  P(None, "dp"), P(None, "dp"), P(), P("dp"), rows),
        out_specs=(rows, rows, params, params, params, params, P(None, ALL), params, params, P(ALL), P("dp", None),
                   P(None, "dp"), P(None, "dp")),
        check_vma=False)
```
